32 devices in a mesh: dp: 16 (over z, y, x), head: 2 (over core).
Axes of the slice: x: 2, y: 2, z: 4, core: 2. Of those that a mesh axis runs over, the one named last changes fastest.
Arguments:
- tokens: bfloat16 [65536, 512], P(('dp', 'head')), may hold values from -6 to 6
- qkv_weight: bfloat16 [3, 512, 512], P(None, 'dp', 'head'), may hold values from -0.25 to 0.25
- out_weight: bfloat16 [512, 512], P('dp', 'head'), may hold values from -0.75 to 0.75
- up_weight: bfloat16 [512, 2048], P(('dp', 'head')), may hold values from -0.25 to 0.25
- down_weight: bfloat16 [2048, 512], P(('dp', 'head')), may hold values from -0.125 to 0.125
- norm_gains: bfloat16 [2, 512], P(None, ('dp', 'head')), may hold values from 0.099609375 to 1.8984375
- biases: bfloat16 [6, 512], P(None, ('dp', 'head')), may hold values from -3 to 3
- up_bias: bfloat16 [2048], P(('dp', 'head')), may hold values from -3 to 3
- segment: int32 [512, 128], P('dp'), may hold values from 0 to 15, as said below
- token_kinds: int32 [512, 128], P('dp'), may hold values from 0 to 2, as said below
- cotangent: bfloat16 [65536, 512], P(('dp', 'head')), may hold values from -6 to 6
Outputs:
- output: bfloat16 [65536, 512], P(('dp', 'head'))
- grad_tokens: float32 [65536, 512], P(('dp', 'head'))
- grad_qkv: float32 [3, 512, 512], P(None, 'dp', 'head')
- grad_out: float32 [512, 512], P('dp', 'head')
- grad_up: float32 [512, 2048], P(('dp', 'head'))
- grad_down: float32 [2048, 512], P(('dp', 'head'))
- grad_gains: float32 [2, 512], P(None, ('dp', 'head'))
- grad_biases: float32 [6, 512], P(None, ('dp', 'head'))
- grad_up_bias: float32 [2048], P(('dp', 'head'))
The draws below stay inside these ranges and needn't reach their ends.
Inputs may be any that keep to these rules, and one draw needn't show every extreme that they name: `segment`: in each row the ids start at 0 and rise by one at the first token of each episode fragment; a fragment may be a single token; a row holds at most 16 fragments. `token_kinds`: within a fragment the kinds follow the cycle frame, action, delta, delta, delta, delta, starting at any place in that cycle.
All inputs are finite; a program needn't handle non-finite values.
Results may differ from the reference program's by a relative error of at most 0.014.
Values may be sent and summed in bfloat16 or wider, within the bound.
A program may use at most 192 MiB of HBM per device.

```python
import jax
import jax.numpy as jnp
from jax import lax

D = 512
HEADS = 8
FF = 2048
HEAD_DIM = 64
SEQ = 128
FRAG = 24
TOKENS = 65536
ROWS = 512


def fragment_layout(key):
    position = lax.broadcasted_iota(jnp.int32, (ROWS, SEQ), 1)
    row_index = lax.broadcasted_iota(jnp.int32, (ROWS, SEQ), 0)
    starters = jax.random.randint(jax.random.fold_in(key, 101), (ROWS, SEQ), 0, FRAG)
    chosen_row = jax.random.randint(jax.random.fold_in(key, 103), (), 0, ROWS)
    forced = (row_index == chosen_row) & (position % 8 == 0)
    opening = (starters == 0) | (position == 0) | forced
    raw_ids = jnp.cumsum(opening.astype(jnp.int32), axis=1) - 1
    opening = opening & (raw_ids <= 15)
    segment = jnp.cumsum(opening.astype(jnp.int32), axis=1) - 1
    phases = jax.random.randint(jax.random.fold_in(key, 102), (ROWS, SEQ), 0, 6)
    begin_at = lax.cummax(jnp.where(opening, position, 0), axis=1)
    phase_at = jnp.take_along_axis(phases, begin_at, axis=1)
    cycle_pos = (phase_at + position - begin_at) % 6
    return (segment.astype(jnp.int32), jnp.minimum(cycle_pos, 2).astype(jnp.int32))


def draw_segment(key, part):
    layout = fragment_layout(key)
    return layout[0]


def draw_token_kinds(key, part):
    layout = fragment_layout(key)
    return layout[1]


def raised(values, key, source, target, parts, factor):
    def block_of(axis_at):
        return (jnp.arange(values.shape[axis_at]) // (values.shape[axis_at] // parts)).reshape((-1,) + (1,) * (values.ndim - 1 - axis_at))

    near = jax.random.permutation(key, parts)[block_of(target)]
    other_side = (block_of(target) + parts // 2) % parts
    return jnp.where((block_of(source) == near) | (block_of(source) == other_side), factor * values, values)


def shard_levels(own_key, shape, split, least, top_value):
    level, own = 1.0, jax.random.fold_in(own_key, 6)
    for dim, parts in split:
        draws = jnp.exp(jax.random.uniform(jax.random.fold_in(own, dim), (parts,), jnp.float32, least / len(split), top_value / len(split)))
        level = level * jnp.repeat(draws, shape[dim] // parts).reshape([-1 if axis == dim else 1 for axis in range(len(shape))])
    return level


def gaussian(stream_key, shape, scale, most, split=(), held_as=jnp.bfloat16):
    loudness = shard_levels(stream_key, shape, split, -0.22, 0.18) if split else 1.0
    values = jax.random.normal(stream_key, shape, jnp.float32) * scale * loudness
    return jnp.minimum(jnp.maximum(values, -most), most).astype(held_as)


def heavy_noise(rng, dims, spread, bound, cuts, heavy, dtype=jnp.bfloat16):
    values = spread * jax.random.normal(rng, dims, jnp.float32)
    if cuts:
        values = values * shard_levels(rng, dims, cuts, -0.22, 0.18)
    return jnp.clip(raised(values, jax.random.fold_in(rng, 3), *heavy), -bound, bound).astype(dtype)


def setup_inputs(seed: int = 0) -> dict:
    seeds = jax.random.split(jax.random.key(seed), 12)
    tokens = heavy_noise(seeds[0], (TOKENS, D), 1.0, 6.0, ((0, 32),), (0, 1, 32, 2.75))
    qkv_weight = gaussian(seeds[1], (3, D, D), D ** -0.5, 0.25, ((1, 16), (2, 2)))
    out_weight = gaussian(seeds[2], (D, D), (D // 8) ** -0.5, 0.75, ((0, 16), (1, 2)))
    up_weight = gaussian(seeds[3], (D, FF), D ** -0.5, 0.25, ((0, 32),))
    down_weight = gaussian(seeds[4], (FF, D), FF ** -0.5, 0.125, ((0, 32),))
    norm_gains = jnp.clip(1.0 + 0.18 * jax.random.normal(seeds[5], (2, D), jnp.float32), 0.099609375, 1.8984375).astype(jnp.bfloat16)
    biases = gaussian(seeds[6], (6, D), 0.5, 3.0, ((1, 32),))
    up_bias = gaussian(seeds[7], (FF,), 0.5, 3.0, ((0, 32),))
    segment = draw_segment(jax.random.fold_in(seeds[11], 71), 0)
    token_kinds = draw_token_kinds(jax.random.fold_in(seeds[11], 71), 0)
    cotangent = heavy_noise(seeds[10], (TOKENS, D), 1.0, 6.0, ((0, 32),), (0, 1, 32, 2.75))
    return dict(tokens=tokens, qkv_weight=qkv_weight, out_weight=out_weight, up_weight=up_weight, down_weight=down_weight, norm_gains=norm_gains, biases=biases, up_bias=up_bias, segment=segment, token_kinds=token_kinds, cotangent=cotangent)


eps_norm = 1e-05
highest = lax.Precision.HIGHEST

@jax.custom_vjp
def low(v):
    return lax.optimization_barrier(v.astype(jnp.bfloat16)).astype(jnp.float32)

@jax.custom_vjp
def low_back(v):
    return v

def low_keep(v):
    return (low(v), None)

def low_pass(kept, grad):
    return (grad,)

def back_keep(v):
    return (v, None)

def back_low(kept, grad):
    return (low(grad),)
low.defvjp(low_keep, low_pass)
low_back.defvjp(back_keep, back_low)

def layer_norm(values, gain, shift):
    center = values - lax.optimization_barrier(jnp.mean(values, axis=-1, keepdims=True))
    variance = lax.optimization_barrier(jnp.mean(center * center, axis=-1, keepdims=True))
    return center * lax.rsqrt(variance + eps_norm) * gain + shift

def visible(segment, token_kinds):
    is_delta = token_kinds == 2
    follows = (segment[:, 1:] == segment[:, :-1]) & is_delta[:, 1:] & is_delta[:, :-1]
    follows = jnp.concatenate([jnp.zeros_like(is_delta[:, :1]), follows], axis=1)
    run_id = jnp.cumsum(1 - follows.astype(jnp.int32), axis=1)
    position = lax.broadcasted_iota(jnp.int32, segment.shape, 1)
    same_seg = segment[:, :, None] == segment[:, None, :]
    causal = position[:, None, :] <= position[:, :, None]
    in_block = (run_id[:, :, None] == run_id[:, None, :]) & is_delta[:, :, None]
    return same_seg & (causal | in_block)

def attend(queries, keys_in, values_in, allowed):
    factor = HEAD_DIM ** (-0.5)
    scores = low_back(factor * jnp.einsum('rqhe,rkhe->rhqk', queries, keys_in, precision=highest))
    scores = jnp.where(allowed[:, None], scores, -jnp.inf)
    weights = low(jax.nn.softmax(scores, axis=-1))
    return jnp.einsum('rhqk,rkhe->rqhe', weights, values_in, precision=highest)

def forward(tokens, qkv_weight, out_weight, up_weight, down_weight, norm_gains, biases, up_bias, allowed):
    token_count = tokens.shape[0]
    normed = low(layer_norm(tokens, norm_gains[0], biases[0]))
    projected = jnp.einsum('td,sde->tse', normed, qkv_weight, precision=highest)
    queries = low(low_back(projected[:, 0] + biases[1]))
    keys_in = low(low_back(projected[:, 1]))
    values_in = low(low_back(projected[:, 2] + biases[2]))
    grid_shape = (token_count // SEQ, SEQ, HEADS, HEAD_DIM)
    mixture = attend(queries.reshape(grid_shape), keys_in.reshape(grid_shape), values_in.reshape(grid_shape), allowed)
    mixture = low(low_back(mixture.reshape(token_count, D)))
    branch = low_back(jnp.dot(mixture, out_weight.T, precision=highest) + biases[3])
    middle = tokens + branch
    normed_two = low(layer_norm(middle, norm_gains[1], biases[4]))
    hidden_pre = low_back(jnp.dot(normed_two, up_weight, precision=highest) + up_bias)
    hidden = low(jax.nn.gelu(hidden_pre, approximate=False))
    return middle + low_back(jnp.dot(hidden, down_weight, precision=highest) + biases[5])

def reference(tokens, qkv_weight, out_weight, up_weight, down_weight, norm_gains, biases, up_bias, segment, token_kinds, cotangent):
    weights = tuple((member.astype(jnp.float32) for member in (qkv_weight, out_weight, up_weight, down_weight, norm_gains, biases, up_bias)))
    group_rows = min(32, ROWS)
    groups = ROWS // group_rows
    group_tokens = group_rows * SEQ
    token_blocks = tokens.astype(jnp.float32).reshape(groups, group_tokens, D)
    cot_blocks = cotangent.astype(jnp.float32).reshape(groups, group_tokens, D)
    seg_blocks = segment.reshape(groups, group_rows, SEQ)
    kind_blocks = token_kinds.reshape(groups, group_rows, SEQ)

    def one_group(totals, inputs):
        tok_part, seg_part, kind_part, cot_part = inputs
        allowed = visible(seg_part, kind_part)

        def local_forward(tok_in, qkv_in, out_in, up_in, down_in, gain_in, bias_in, up_bias_in):
            return forward(tok_in, qkv_in, out_in, up_in, down_in, gain_in, bias_in, up_bias_in, allowed)
        result, pullback = jax.vjp(local_forward, tok_part, weights[0], weights[1], weights[2], weights[3], weights[4], weights[5], weights[6])
        gradients = pullback(cot_part)
        totals = tuple((earlier + update for earlier, update in zip(totals, gradients[1:])))
        return (totals, (result.astype(jnp.bfloat16), gradients[0]))
    initial = tuple((jnp.zeros_like(member) for member in weights))
    totals, outputs = lax.scan(one_group, initial, (token_blocks, seg_blocks, kind_blocks, cot_blocks))
    results, input_grads = outputs
    return (results.reshape(TOKENS, D), input_grads.reshape(TOKENS, D), totals[0], totals[1], totals[2], totals[3], totals[4], totals[5], totals[6])
```

```python
import math

import jax
import jax.numpy as jnp
from jax import lax
from jax.experimental import pallas as pl
from jax.experimental.pallas import tpu as pltpu
from jax.sharding import Mesh
from jax.sharding import PartitionSpec as P

bf16, f32 = jnp.bfloat16, jnp.float32
D = 512
SEQ = 128
LANES = 128
GRID_Z, GRID_P = 4, 4
EPS = 1e-5
MESH = pl.DeviceIdType.MESH
NN = (((1,), (0,)), ((), ()))
NT = (((1,), (1,)), ((), ()))
TN = (((0,), (0,)), ((), ()))
VMEM_LIMIT = (63 << 20) + (512 << 10)


def dot(a, b, dims=NN):
    return lax.dot_general(a, b, dims, preferred_element_type=f32)


def block(index, size):
    if isinstance(index, int):
        return pl.ds(index * size, size)
    return pl.ds(pl.multiple_of(index * size, size), size)


def parity(index):
    return index % 2 if isinstance(index, int) else lax.rem(index, 2)


class Place:
    def __init__(self):
        dp, self.h = lax.axis_index("dp"), lax.axis_index("head")
        self.z, self.p = dp // GRID_P, lax.rem(dp, GRID_P)
        x, y = lax.rem(self.p, 2), self.p // 2
        self.px = y * 2 + (1 - x)
        self.py = (1 - y) * 2 + x
        self.pd = (1 - y) * 2 + (1 - x)
        self.sib = 1 - self.h

    def at(self, z, p, h):
        return {"dp": z * GRID_P + p, "head": h}

    def line(self, k):
        return lax.rem(self.z + k, GRID_Z)

    def line_back(self, k):
        return lax.rem(self.z + (GRID_Z - k), GRID_Z)

    def plane(self):
        places = [(self.px, self.h), (self.py, self.h), (self.pd, self.h)]
        places += [(p, self.sib) for p in (self.p, self.px, self.py, self.pd)]
        return places


def barrier(me):
    sem = pltpu.get_barrier_semaphore()
    for p, h in me.plane():
        pl.semaphore_signal(sem, 1, device_id=me.at(me.z, p, h), device_id_type=MESH)
    for k in (1, 2, 3):
        pl.semaphore_signal(sem, 1, device_id=me.at(me.line(k), me.p, me.h), device_id_type=MESH)
    pl.semaphore_wait(sem, 10)


def remote(src, dst, send, recv, device):
    return pltpu.make_async_remote_copy(
        src_ref=src, dst_ref=dst, send_sem=send, recv_sem=recv, device_id=device, device_id_type=MESH
    )


class Gather:
    SENDS, RECVS = 11, 11

    def __init__(self, me, shard, view, send, recv, local):
        self.me, self.shard, self.view = me, shard, view
        self.send, self.recv, self.local = send, recv, local
        self.started = []

    def go(self, index, parts):
        def make():
            src, dst, device = parts()
            return remote(src, dst, self.send.at[index], self.recv.at[index], device)

        make().start()
        self.started.append(make)

    def landed(self, index, region):
        me = self.me
        remote(region, region, self.send.at[index], self.recv.at[index], me.at(me.z, me.p, me.sib)).wait_recv()

    def set_of(self, z, p):
        return self.view(z, p, self.me.h)

    def first(self):
        me = self.me
        self.mine = pltpu.make_async_copy(self.shard, self.set_of(me.z, me.p), self.local)
        self.mine.start()
        for k in (1, 2, 3):
            self.go(k - 1, lambda k=k: (self.shard, self.set_of(me.z, me.p), me.at(me.line(k), me.p, me.h)))

    def second(self):
        me = self.me
        self.mine.wait()
        for k in (1, 2, 3):
            self.landed(k - 1, self.view(me.line_back(k), me.p, me.h))
        line = lambda: self.set_of(pl.ds(0, 4), me.p)
        self.go(3, lambda: (line(), line(), me.at(me.z, me.px, me.h)))
        self.go(4, lambda: (line(), line(), me.at(me.z, me.py, me.h)))
        self.go(7, lambda: (line(), line(), me.at(me.z, me.p, me.sib)))

    def third(self):
        me = self.me
        from_x, from_y = lambda: self.set_of(pl.ds(0, 4), me.px), lambda: self.set_of(pl.ds(0, 4), me.py)
        half_x, half_y = lambda: self.set_of(pl.ds(0, 2), me.px), lambda: self.set_of(pl.ds(2, 2), me.py)
        self.landed(3, from_x())
        self.go(6, lambda: (half_x(), half_x(), me.at(me.z, me.py, me.h)))
        self.landed(4, from_y())
        self.go(5, lambda: (half_y(), half_y(), me.at(me.z, me.px, me.h)))
        self.go(8, lambda: (from_x(), from_x(), me.at(me.z, me.p, me.sib)))
        self.go(9, lambda: (from_y(), from_y(), me.at(me.z, me.p, me.sib)))

    def fourth(self):
        me = self.me
        self.landed(6, self.view(pl.ds(0, 2), me.pd, me.h))
        self.landed(5, self.view(pl.ds(2, 2), me.pd, me.h))
        diagonal = lambda: self.set_of(pl.ds(0, 4), me.pd)
        self.go(10, lambda: (diagonal(), diagonal(), me.at(me.z, me.p, me.sib)))

    def fifth(self):
        me = self.me
        for index, p in ((7, me.p), (8, me.px), (9, me.py), (10, me.pd)):
            self.landed(index, self.view(pl.ds(0, 4), p, me.sib))

    def close(self):
        for make in self.started:
            make().wait_send()


class SmallGather:
    SENDS, RECVS = 10, 10

    def __init__(self, me, tiles, send, recv):
        self.me, self.tiles, self.send, self.recv = me, tiles, send, recv
        self.started = []

    def go(self, index, parts):
        def make():
            region, device = parts()
            return remote(region, region, self.send.at[index], self.recv.at[index], device)

        make().start()
        self.started.append(make)

    def landed(self, index, region):
        me = self.me
        remote(region, region, self.send.at[index], self.recv.at[index], me.at(me.z, me.p, me.sib)).wait_recv()

    def first(self, gains, biases, up_bias):
        me = self.me
        place = lambda rows, width, start: dot(
            rows,
            jnp.where(
                lax.broadcasted_iota(jnp.int32, (width, LANES), 1)
                == lax.broadcasted_iota(jnp.int32, (width, LANES), 0) + start,
                1.0,
                0.0,
            ).astype(bf16),
        )
        start = (me.p * 2 + me.h) * 16
        rows = jnp.concatenate(
            [
                place(gains[...], 16, start),
                place(biases[...], 16, start),
                place(up_bias[...], 64, me.h * 64),
                jnp.zeros((7, LANES), f32),
            ],
            axis=0,
        )
        self.tiles[me.z, me.p, me.h] = rows.astype(bf16)

    def second(self):
        me = self.me
        for index, (p, h) in enumerate(me.plane()):
            self.go(index, lambda p=p, h=h: (self.tiles.at[me.z, me.p, me.h], me.at(me.z, p, h)))

    def third(self):
        me = self.me
        for index, (p, h) in enumerate(me.plane()):
            self.landed(index, self.tiles.at[me.z, p, h])
        for k in (1, 2, 3):
            self.go(6 + k, lambda k=k: (self.tiles.at[me.z], me.at(me.line(k), me.p, me.h)))

    def fourth(self, gain_bias, up_bias):
        me = self.me
        for k in (1, 2, 3):
            self.landed(6 + k, self.tiles.at[me.line_back(k)])
        for z in range(GRID_Z):
            total = jnp.zeros((8, LANES), f32)
            for p in range(GRID_P):
                pair = self.tiles[z, p, 0].astype(f32) + self.tiles[z, p, 1].astype(f32)
                total = total + pair[:8]
                up_bias[:, (z * GRID_P + p) * LANES : (z * GRID_P + p + 1) * LANES] = pair[8:9]
            gain_bias[:, z * LANES : (z + 1) * LANES] = total

    def close(self):
        for make in self.started:
            make().wait_send()


class Scatter:
    SENDS, RECVS = 8, 8

    def __init__(self, me, part, core, cross, sets, line, send, recv):
        self.me, self.part, self.core, self.cross, self.sets, self.line = me, part, core, cross, sets, line
        self.send, self.recv = send, recv
        self.started = []

    def go(self, index, parts):
        def make():
            src, dst, device = parts()
            return remote(src, dst, self.send.at[index], self.recv.at[index], device)

        make().start()
        self.started.append(make)

    def landed(self, index, region):
        me = self.me
        remote(region, region, self.send.at[index], self.recv.at[index], me.at(me.z, me.p, me.sib)).wait_recv()

    def first(self):
        me = self.me
        self.go(0, lambda: (self.part.at[me.sib], self.core, me.at(me.z, me.p, me.sib)))

    def second(self):
        me, part = self.me, self.part
        self.landed(0, self.core)

        def add(i, carry):
            z, p = i // GRID_P, lax.rem(i, GRID_P)
            part[me.h, z, p] = (part[me.h, z, p].astype(f32) + self.core[z, p].astype(f32)).astype(bf16)
            return carry

        lax.fori_loop(0, GRID_Z * GRID_P, add, 0)
        self.go(1, lambda: (part.at[me.h, pl.ds(0, 2), me.pd], self.cross.at[0], me.at(me.z, me.py, me.h)))
        self.go(2, lambda: (part.at[me.h, pl.ds(2, 2), me.pd], self.cross.at[1], me.at(me.z, me.px, me.h)))

    def third(self):
        me, part = self.me, self.part
        self.landed(1, self.cross.at[0])
        self.landed(2, self.cross.at[1])

        for i in range(2):
            part[me.h, i, me.px] = (part[me.h, i, me.px].astype(f32) + self.cross[0, i].astype(f32)).astype(bf16)
            part[me.h, 2 + i, me.py] = (
                part[me.h, 2 + i, me.py].astype(f32) + self.cross[1, i].astype(f32)
            ).astype(bf16)
        self.go(3, lambda: (part.at[me.h, :, me.px], self.sets.at[0], me.at(me.z, me.px, me.h)))
        self.go(4, lambda: (part.at[me.h, :, me.py], self.sets.at[1], me.at(me.z, me.py, me.h)))

    def fourth(self):
        me, part = self.me, self.part
        self.landed(3, self.sets.at[0])
        self.landed(4, self.sets.at[1])
        for i in range(GRID_Z):
            part[me.h, i, me.p] = (
                part[me.h, i, me.p].astype(f32) + self.sets[0, i].astype(f32) + self.sets[1, i].astype(f32)
            ).astype(bf16)
        for k in (1, 2, 3):
            self.go(
                4 + k,
                lambda k=k: (
                    part.at[me.h, me.line(k), me.p], self.line.at[k - 1], me.at(me.line(k), me.p, me.h)
                ),
            )

    def fifth(self):
        me = self.me
        total = self.part[me.h, me.z, me.p].astype(f32)
        for k in (1, 2, 3):
            self.landed(4 + k, self.line.at[k - 1])
            total = total + self.line[k - 1].astype(f32)
        return total

    def close(self):
        for make in self.started:
            make().wait_send()


class SmallScatter:
    SENDS, RECVS = 10, 10

    def __init__(self, me, part, line, sets, send, recv):
        self.me, self.part, self.line, self.sets = me, part, line, sets
        self.send, self.recv = send, recv
        self.started = []

    def go(self, index, parts):
        def make():
            src, dst, device = parts()
            return remote(src, dst, self.send.at[index], self.recv.at[index], device)

        make().start()
        self.started.append(make)

    def landed(self, index, region):
        me = self.me
        remote(region, region, self.send.at[index], self.recv.at[index], me.at(me.z, me.p, me.sib)).wait_recv()

    def first(self):
        me = self.me
        for k in (1, 2, 3):
            self.go(
                k - 1,
                lambda k=k: (self.part.at[me.line(k)], self.line.at[k - 1], me.at(me.line(k), me.p, me.h)),
            )

    def second(self):
        me = self.me
        total = self.part[me.z]
        for k in (1, 2, 3):
            self.landed(k - 1, self.line.at[k - 1])
            total = total + self.line[k - 1]
        self.sets[7] = total
        for index, (p, h) in enumerate(me.plane()):
            self.go(
                3 + index, lambda i=index, p=p, h=h: (self.sets.at[7], self.sets.at[i], me.at(me.z, p, h))
            )

    def third(self, gains, biases, up_bias):
        me = self.me
        total = self.sets[7]
        for index in range(7):
            self.landed(3 + index, self.sets.at[index])
            total = total + self.sets[index]
        rows = pltpu.roll(total[:8], LANES - 16 * (me.p * 2 + me.h), 1)
        gains[...] = rows[0:2, 0:16]
        biases[...] = rows[2:8, 0:16]
        row = lax.broadcasted_iota(jnp.int32, (8, LANES), 0)
        hidden = jnp.sum(jnp.where(row == me.p, total[8:], 0.0), axis=0, keepdims=True)
        hidden = jnp.where(me.h == 0, hidden[:, 0:64], hidden[:, 64:128])
        up_bias[...] = hidden

    def close(self):
        for make in self.started:
            make().wait_send()


ANY = pl.BlockSpec(memory_space=pl.ANY)
VM = pl.BlockSpec(memory_space=pltpu.VMEM)


def normalized(x):
    center = x - jnp.mean(x, axis=-1, keepdims=True)
    rstd = lax.rsqrt(jnp.mean(center * center, axis=-1, keepdims=True) + EPS)
    return center * rstd, rstd


def norm_back(e, xhat, rstd, gain):
    u = e * gain
    return rstd * (
        u - jnp.mean(u, axis=-1, keepdims=True) - xhat * jnp.mean(u * xhat, axis=-1, keepdims=True)
    )


def column_sums(x):
    return jnp.sum(x.reshape(x.shape[0] // 8, 8, x.shape[1]), axis=0)


def gelu_and_slope(u):
    phi = 0.5 + 0.5 * lax.erf(u * math.sqrt(0.5))
    return u * phi, phi + u * (jnp.exp(u * u * -0.5) * (1 / math.sqrt(2 * math.pi)))


def two_heads(x):
    first = lax.broadcasted_iota(jnp.int32, x.shape, 1) < 64
    zero = jnp.zeros_like(x)
    return jnp.concatenate([jnp.where(first, x, zero), jnp.where(first, zero, x)], axis=0)


def tiles(ref, rows):
    return jnp.concatenate([ref[p, rows] for p in range(4)], axis=1)


def hidden_masks(segment, kinds, mask):
    s, k = segment, kinds
    position = lax.broadcasted_iota(jnp.int32, s.shape, 1)
    follows = (s == pltpu.roll(s, 1, 1)) & (k == 2) & (pltpu.roll(k, 1, 1) == 2) & (position > 0)
    upper = lax.broadcasted_iota(jnp.int32, (SEQ, SEQ), 0) <= lax.broadcasted_iota(jnp.int32, (SEQ, SEQ), 1)
    run = dot(jnp.where(follows, 0.0, 1.0).astype(bf16), jnp.where(upper, 1.0, 0.0).astype(bf16))
    seg = s.astype(f32)
    for r in range(s.shape[0]):
        seg_j = jnp.broadcast_to(seg[r : r + 1], (SEQ, SEQ))
        run_j = jnp.broadcast_to(run[r : r + 1], (SEQ, SEQ))
        mask[r] = jnp.where((seg_j.T == seg_j) & (run_j <= run_j.T), 0.0, -jnp.inf).astype(bf16)


def layer_kernel(
    tokens_hbm, cot_hbm, qkv_s, out_s, up_s, down_s, gains, biases, up_bias, segment, kinds,
    output_hbm, grad_hbm, g_qkv, g_out, g_up, g_down, g_gains, g_biases, g_up_bias,
    tok, cot, w_qkv, w_out, w_up, w_down, gb, upb, mask,
    normed, packed, att, mix, hid, gpre, gbr, gmix, acc, acc_up, acc_q,
    out_stage, grad_stage,
    p_down, p_up, p_out, p_qkv, p_small,
    core0, core1, core2, core3, cross0, cross1, cross2, cross3,
    sets0, sets1, sets2, sets3, line0, line1, line2, line3,
    small_tiles, small_line, small_sets,
    g_send, g_recv, g_local, s_send, s_recv, io_sem, out_sem,
):
    T = tok.shape[0]
    ROWS = T // SEQ
    me = Place()
    load_tok = pltpu.make_async_copy(tokens_hbm, tok, io_sem.at[0])
    load_cot = pltpu.make_async_copy(cot_hbm, cot, io_sem.at[1])
    load_tok.start()
    load_cot.start()

    def qkv_view(s):
        return lambda z, p, h: w_qkv.at[s, z, p, :, pl.ds(pl.multiple_of(h * 256, 256), 256)]

    views = [(qkv_s.at[s], qkv_view(s)) for s in range(3)]
    views += [
        (out_s, lambda z, p, h: w_out.at[z, p, :, pl.ds(pl.multiple_of(h * 256, 256), 256)]),
        (up_s, lambda z, p, h: w_up.at[z, p, h]),
        (down_s, lambda z, p, h: w_down.at[z, p, h]),
    ]
    big = [
        Gather(me, shard, view, g_send.at[i], g_recv.at[i], g_local.at[i])
        for i, (shard, view) in enumerate(views)
    ]
    attn_w, mlp_w = big[:3], big[3:]
    small = SmallGather(me, small_tiles, g_send.at[6], g_recv.at[6])
    small.first(gains, biases, up_bias)
    barrier(me)
    small.second()
    for g in attn_w:
        g.first()
    own_rows = pl.ds(pl.multiple_of(me.h * ROWS, ROWS), ROWS)
    hidden_masks(segment[own_rows, :], kinds[own_rows, :], mask)
    small.third()
    for g in attn_w:
        g.second()
    small.fourth(gb, upb)
    load_tok.wait()

    def norm_one(i, carry):
        r = block(i, 256)
        xhat, _ = normalized(tok[r, :].astype(f32))
        normed[r, :] = (xhat * gb[0:1, :] + gb[2:3, :]).astype(bf16)
        return carry

    lax.fori_loop(0, T // 256, norm_one, 0)
    for g in attn_w:
        g.third()
    for g in mlp_w:
        g.first()
    for g in attn_w:
        g.fourth()
    for g in attn_w:
        g.fifth()

    def project(i, carry):
        r = block(i, 512)
        x = normed[r, :]
        q = (dot(x, w_qkv[0].reshape(D, D)) + gb[3:4, :]).astype(bf16) * jnp.asarray(0.125, bf16)
        k = dot(x, w_qkv[1].reshape(D, D)).astype(bf16)
        v = (dot(x, w_qkv[2].reshape(D, D)) + gb[4:5, :]).astype(bf16)
        for p in range(4):
            for s, value in enumerate((q, k, v)):
                packed[s, p, r, :] = value[:, LANES * p : LANES * p + LANES]
        return carry

    lax.fori_loop(0, T // 512, project, 0)
    for g in mlp_w:
        g.second()

    def attend(i, carry):
        for r in (2 * i, 2 * i + 1):
            rows = block(r, SEQ)
            hide = mask[r].astype(f32)
            for p in range(4):
                keys, values = two_heads(packed[1, p, rows, :]), two_heads(packed[2, p, rows, :])
                scores = dot(packed[0, p, rows, :], keys, NT)
                weights = []
                for h in range(2):
                    t = scores[:, SEQ * h : SEQ * h + SEQ] + hide
                    e = jnp.exp(t - jnp.max(t, axis=-1, keepdims=True))
                    a = (e * (1.0 / jnp.sum(e, axis=-1, keepdims=True))).astype(bf16)
                    att[r, 2 * p + h] = a
                    weights.append(a)
                mix[p, rows, :] = dot(jnp.concatenate(weights, axis=1), values).astype(bf16)

        @pl.when(i == 3)
        def _():
            for g in mlp_w:
                g.third()

        @pl.when(i == 6)
        def _():
            for g in mlp_w:
                g.fourth()

        return carry

    lax.fori_loop(0, ROWS // 2, attend, 0)
    load_cot.wait()
    for g in mlp_w:
        g.fifth()

    acc[...] = jnp.zeros_like(acc)
    acc_up[...] = jnp.zeros_like(acc_up)
    BM = out_stage.shape[1]

    def out_copy(i):
        return pltpu.make_async_copy(
            out_stage.at[parity(i)], output_hbm.at[block(i, BM), :], out_sem.at[parity(i)]
        )

    def feed_forward(i, carry):
        r = block(i, BM)

        @pl.when(i >= 2)
        def _():
            out_copy(i - 2).wait()

        middle = tok[r, :].astype(f32) + dot(tiles(mix, r), w_out[...].reshape(D, D), NT) + gb[5:6, :]
        xhat, rstd = normalized(middle)
        two = (xhat * gb[1:2, :] + gb[6:7, :]).astype(bf16)
        tok[r, :] = two
        c = cot[r, :]
        total = middle + gb[7:8, :]
        e = jnp.zeros((BM, D), f32)
        for j in range(4):
            cols = slice(512 * j, 512 * j + 512)
            w_up_j = w_up[:, :, :, :, cols].reshape(D, 512)
            w_down_j = w_down[j].reshape(512, D)
            u = dot(two, w_up_j) + upb[:, cols]
            grad_hidden = dot(c, w_down_j, NT)
            hidden, slope = gelu_and_slope(u)
            hidden = hidden.astype(bf16)
            hid[r, cols] = hidden
            total = total + dot(hidden, w_down_j)
            grad_pre = grad_hidden * slope
            acc_up[:, cols] += column_sums(grad_pre)
            grad_pre = grad_pre.astype(bf16)
            gpre[r, cols] = grad_pre
            e = e + dot(grad_pre, w_up_j, NT)
        out_stage[parity(i)] = total.astype(bf16)
        out_copy(i).start()
        cot_f32 = c.astype(f32)
        branch = (cot_f32 + norm_back(e, xhat, rstd, gb[1:2, :])).astype(bf16)
        gbr[r, :] = branch
        grad_mix = dot(branch, w_out[...].reshape(D, D)).astype(bf16)
        for p in range(4):
            gmix[p, r, :] = grad_mix[:, LANES * p : LANES * p + LANES]
        acc[1] += column_sums(e * xhat)
        acc[6] += column_sums(e)
        acc[5] += column_sums(branch.astype(f32))
        acc[7] += column_sums(cot_f32)
        return carry

    count = T // BM
    lax.fori_loop(0, count, feed_forward, 0)

    units = [
        Scatter(me, *refs, s_send.at[i], s_recv.at[i])
        for i, refs in enumerate(
            (
                (p_down, core0, cross0, sets0, line0),
                (p_up, core1, cross1, sets1, line1),
                (p_out, core2, cross2, sets2, line2),
                (p_qkv, core3, cross3, sets3, line3),
            )
        )
    ]
    down_u, up_u, out_u, qkv_u = units

    def grad_down_chunk(z, carry):
        o = dot(hid[:, block(z, 512)], cot[...], TN).astype(bf16)
        for p in range(GRID_P):
            for h in range(2):
                for j in range(4):
                    p_down[h, z, p, 64 * j : 64 * j + 64] = o[
                        64 * (2 * p + h) : 64 * (2 * p + h) + 64, LANES * j : LANES * j + LANES
                    ]
        return carry

    lax.fori_loop(0, 4, grad_down_chunk, 0)
    down_u.first()

    def grad_up_chunk(c, carry):
        o = dot(tok[...], gpre[:, block(c, 512)], TN).astype(bf16)
        for z in range(GRID_Z):
            for p in range(GRID_P):
                for h in range(2):
                    d = (z * 4 + p) * 2 + h
                    for j in range(4):
                        p_up[h, z, p, pl.ds(pl.multiple_of(64 * c + 16 * j, 16), 16)] = o[
                            16 * d : 16 * d + 16, LANES * j : LANES * j + LANES
                        ]
        return carry

    lax.fori_loop(0, 4, grad_up_chunk, 0)
    up_u.first()
    load_tok = pltpu.make_async_copy(tokens_hbm, tok, io_sem.at[0])
    load_tok.start()
    down_u.second()

    o = dot(gbr[...], jnp.concatenate([mix[p] for p in range(4)], axis=1), TN).astype(bf16)
    for z in range(GRID_Z):
        for p in range(GRID_P):
            d = z * 4 + p
            for h in range(2):
                for j in range(2):
                    p_out[h, z, p, 32 * j : 32 * j + 32] = o[
                        32 * d : 32 * d + 32, 256 * h + LANES * j : 256 * h + LANES * j + LANES
                    ]
    out_u.first()

    def attend_back(half):
        def body(r, carry):
            rows = block(r, SEQ)
            for pp in range(2):
                p = 2 * half + pp
                queries, keys = two_heads(packed[0, p, rows, :]), two_heads(packed[1, p, rows, :])
                values = two_heads(packed[2, p, rows, :])
                grad = gmix[p, rows, :]
                grad_two = two_heads(grad)
                grad_weight = dot(grad, values, NT)
                product = grad.astype(f32) * mix[p, rows, :].astype(f32)
                first = lax.broadcasted_iota(jnp.int32, (SEQ, LANES), 1) < 64
                scores, weights = [], []
                for h in range(2):
                    inner = jnp.sum(jnp.where(first == (h == 0), product, 0.0), axis=-1, keepdims=True)
                    a = att[r, 2 * p + h]
                    weights.append(a)
                    scores.append(
                        (a.astype(f32) * (grad_weight[:, SEQ * h : SEQ * h + SEQ] - inner)).astype(bf16)
                    )
                g_q = dot(jnp.concatenate(scores, axis=1), keys) * 0.125
                g_k = dot(jnp.concatenate(scores, axis=0), queries, TN)
                g_v = dot(jnp.concatenate(weights, axis=0), grad_two, TN)
                packed[0, p, rows, :] = g_q.astype(bf16)
                packed[1, p, rows, :] = g_k.astype(bf16)
                packed[2, p, rows, :] = g_v.astype(bf16)
                acc_q[0, p] += column_sums(g_q)
                acc_q[1, p] += column_sums(g_v)
            return carry

        return body

    acc_q[...] = jnp.zeros_like(acc_q)

    def grad_qkv_half(half):
        def body(s, carry):
            wide = jnp.concatenate([packed[s, 2 * half], packed[s, 2 * half + 1]], axis=1)
            o = dot(normed[...], wide, TN).astype(bf16)
            for z in range(GRID_Z):
                for p in range(GRID_P):
                    d = z * 4 + p
                    for j in range(2):
                        p_qkv[half, z, p, pl.ds(pl.multiple_of(64 * s + 32 * j, 32), 32)] = o[
                            32 * d : 32 * d + 32, LANES * j : LANES * j + LANES
                        ]
            return carry

        return body

    lax.fori_loop(0, ROWS, attend_back(me.sib), 0)
    down_u.third()
    up_u.second()
    lax.fori_loop(0, 3, grad_qkv_half(me.sib), 0)
    qkv_u.first()
    down_u.fourth()
    up_u.third()
    out_u.second()
    lax.fori_loop(0, ROWS, attend_back(me.h), 0)
    up_u.fourth()
    out_u.third()
    lax.fori_loop(0, 3, grad_qkv_half(me.h), 0)
    qkv_u.second()
    out_u.fourth()
    load_tok.wait()

    def grad_copy(i):
        return pltpu.make_async_copy(
            grad_stage.at[parity(i)], grad_hbm.at[block(i, BM), :], out_sem.at[2 + parity(i)]
        )

    def norm_one_back(i, carry):
        r = block(i, BM)

        @pl.when(i >= 2)
        def _():
            grad_copy(i - 2).wait()

        e = dot(tiles(packed.at[0], r), w_qkv[0].reshape(D, D), NT)
        e = e + dot(tiles(packed.at[1], r), w_qkv[1].reshape(D, D), NT)
        e = e + dot(tiles(packed.at[2], r), w_qkv[2].reshape(D, D), NT)
        xhat, rstd = normalized(tok[r, :].astype(f32))
        grad_stage[parity(i)] = gbr[r, :].astype(f32) + norm_back(e, xhat, rstd, gb[0:1, :])
        grad_copy(i).start()
        acc[0] += column_sums(e * xhat)
        acc[2] += column_sums(e)

        @pl.when(i == 2)
        def _():
            qkv_u.third()

        @pl.when(i == 6)
        def _():
            qkv_u.fourth()

        return carry

    lax.fori_loop(0, count, norm_one_back, 0)
    for p in range(4):
        acc[3, :, LANES * p : LANES * p + LANES] = acc_q[0, p]
        acc[4, :, LANES * p : LANES * p + LANES] = acc_q[1, p]
    for z in range(GRID_Z):
        rows = [jnp.sum(acc[n, :, LANES * z : LANES * z + LANES], axis=0, keepdims=True) for n in range(8)]
        rows += [
            jnp.sum(acc_up[:, 512 * z + LANES * p : 512 * z + LANES * p + LANES], axis=0, keepdims=True)
            for p in range(GRID_P)
        ]
        rows += [jnp.zeros((4, LANES), f32)]
        p_small[z] = jnp.concatenate(rows, axis=0)
    small_sum = SmallScatter(me, p_small, small_line, small_sets, s_send.at[4], s_recv.at[4])
    small_sum.first()
    total = down_u.fifth()
    for j in range(4):
        g_down[:, LANES * j : LANES * j + LANES] = total[64 * j : 64 * j + 64]
    total = up_u.fifth()
    for j in range(16):
        g_up[:, LANES * j : LANES * j + LANES] = total[16 * j : 16 * j + 16]
    small_sum.second()
    total = out_u.fifth()
    for j in range(2):
        g_out[:, LANES * j : LANES * j + LANES] = total[32 * j : 32 * j + 32]
    total = qkv_u.fifth()
    for s in range(3):
        for j in range(2):
            g_qkv[s, :, LANES * j : LANES * j + LANES] = total[64 * s + 32 * j : 64 * s + 32 * j + 32]
    small_sum.third(g_gains, g_biases, g_up_bias)
    for i in (count - 2, count - 1):
        out_copy(i).wait()
        grad_copy(i).wait()
    for item in big + units + [small, small_sum]:
        item.close()


def layer(tokens, cotangent, qkv, out, up, down, gains, biases, up_bias, segment, kinds):
    shape = jax.ShapeDtypeStruct
    T = tokens.shape[0]
    rows = T // SEQ
    outs = (
        shape((T, D), bf16),
        shape((T, D), f32),
        shape((3, 32, 256), f32),
        shape((32, 256), f32),
        shape((16, 2048), f32),
        shape((64, 512), f32),
        shape((2, 16), f32),
        shape((6, 16), f32),
        shape((1, 64), f32),
    )
    sizes = [256, 256, 64, 192]
    BM = 256
    V, S = pltpu.VMEM, pltpu.SemaphoreType.DMA
    scratch = [
        V((T, D), bf16), V((T, D), bf16),
        V((3, 4, 4, 32, 512), bf16), V((4, 4, 32, 512), bf16),
        V((4, 4, 2, 16, 2048), bf16), V((4, 4, 2, 64, 512), bf16),
        V((8, 512), f32), V((1, 2048), f32), V((rows, SEQ, SEQ), bf16),
        V((T, D), bf16), V((3, 4, T, LANES), bf16), V((rows, 8, SEQ, SEQ), bf16),
        V((4, T, LANES), bf16), V((T, 2048), bf16), V((T, 2048), bf16),
        V((T, D), bf16), V((4, T, LANES), bf16), V((8, 8, 512), f32), V((8, 2048), f32),
        V((2, 4, 8, LANES), f32),
        V((2, BM, D), bf16), V((2, BM, D), f32),
    ]
    scratch += [V((2, 4, 4, r, LANES), bf16) for r in sizes] + [V((4, 16, LANES), f32)]
    scratch += [V((4, 4, r, LANES), bf16) for r in sizes]
    scratch += [V((2, 2, r, LANES), bf16) for r in sizes]
    scratch += [V((2, 4, r, LANES), bf16) for r in sizes]
    scratch += [V((3, r, LANES), bf16) for r in sizes]
    scratch += [V((4, 4, 2, 16, LANES), bf16), V((3, 16, LANES), f32), V((8, 16, LANES), f32)]
    scratch += [S((7, 11)), S((7, 11)), S((6,)), S((5, 10)), S((5, 10)), S((2,)), S((4,))]
    return pl.pallas_call(
        layer_kernel,
        out_shape=outs,
        in_specs=[ANY] * 6 + [VM] * 5,
        out_specs=[ANY] * 2 + [VM] * 7,
        scratch_shapes=scratch,
        compiler_params=pltpu.CompilerParams(
            collective_id=0, has_side_effects=True, vmem_limit_bytes=VMEM_LIMIT
        ),
        name="layer",
    )(tokens, cotangent, qkv, out, up, down, gains, biases, up_bias, segment, kinds)


def widened(x, axes, dim):
    return lax.all_gather(x, axes, axis=dim, tiled=True)


def on_device(rep):
    def run(
        tokens, qkv, out, up, down, gains, biases, up_bias, segment, kinds, cotangent
    ):
        up_bias = up_bias.reshape(1, -1)
        head = lax.axis_index("head")
        if rep > 1:
            both = ("rep", "head")
            qkv, out = widened(qkv, "rep", 1), widened(out, "rep", 0)
            up = lax.dynamic_slice_in_dim(widened(up, both, 0), head * 16, 16, 0)
            down = lax.dynamic_slice_in_dim(widened(down, both, 0), head * 64, 64, 0)
            gains = lax.dynamic_slice_in_dim(widened(gains, both, 1), head * 16, 16, 1)
            biases = lax.dynamic_slice_in_dim(widened(biases, both, 1), head * 16, 16, 1)
            up_bias = lax.dynamic_slice_in_dim(widened(up_bias, both, 1), head * 64, 64, 1)
        output, grad, *grads = layer(
            tokens, cotangent, qkv, out, up, down, gains, biases, up_bias, segment, kinds
        )
        if rep > 1:
            place = lax.axis_index("rep") * 2 + head

            def own(x, dim):
                x = lax.all_gather(lax.psum(x, "rep"), "head", axis=dim, tiled=True)
                size = x.shape[dim] // (2 * rep)
                return lax.dynamic_slice_in_dim(x, place * size, size, dim)

            for i, dim in ((0, 1), (1, 0)):
                grads[i] = lax.psum_scatter(grads[i], "rep", scatter_dimension=dim, tiled=True)
            for i, dim in ((2, 0), (3, 0), (4, 1), (5, 1), (6, 1)):
                grads[i] = own(grads[i], dim)
        grads[6] = grads[6].reshape(-1)
        return (output, grad, *grads)

    return run


def solution(mesh):
    rep = mesh.shape["dp"] // (GRID_Z * GRID_P)
    wide = Mesh(mesh.devices.reshape(GRID_Z * GRID_P, rep, 2), ("dp", "rep", "head"))
    dp, every = ("dp", "rep"), ("dp", "rep", "head")
    in_specs = (
        P(every, None),
        P(None, dp, "head"),
        P(dp, "head"),
        P(every, None),
        P(every, None),
        P(None, every),
        P(None, every),
        P(every),
        P(dp, None),
        P(dp, None),
        P(every, None),
    )
    out_specs = (
        P(every, None),
        P(every, None),
        P(None, dp, "head"),
        P(dp, "head"),
        P(every, None),
        P(every, None),
        P(None, every),
        P(None, every),
        P(every),
    )
    return jax.shard_map(
        on_device(rep), mesh=wide, in_specs=in_specs, out_specs=out_specs, check_vma=False
    )
```

```python
import math

import jax
import jax.numpy as jnp
from jax import lax
from jax.experimental import pallas as pl
from jax.experimental.pallas import tpu as pltpu
from jax.sharding import Mesh
from jax.sharding import PartitionSpec as P

bf16, f32 = jnp.bfloat16, jnp.float32
D = 512
SEQ = 128
LANES = 128
GRID_Z, GRID_P = 4, 4
EPS = 1e-5
MESH = pl.DeviceIdType.MESH
NN = (((1,), (0,)), ((), ()))
NT = (((1,), (1,)), ((), ()))
TN = (((0,), (0,)), ((), ()))
VMEM_LIMIT = (63 << 20) + (512 << 10)


def dot(a, b, dims=NN):
    return lax.dot_general(a, b, dims, preferred_element_type=f32)


def block(index, size):
    if isinstance(index, int):
        return pl.ds(index * size, size)
    return pl.ds(pl.multiple_of(index * size, size), size)


def parity(index):
    return index % 2 if isinstance(index, int) else lax.rem(index, 2)


class Place:
    def __init__(self):
        dp, self.h = lax.axis_index("dp"), lax.axis_index("head")
        self.z, self.p = dp // GRID_P, lax.rem(dp, GRID_P)
        x, y = lax.rem(self.p, 2), self.p // 2
        self.px = y * 2 + (1 - x)
        self.py = (1 - y) * 2 + x
        self.pd = (1 - y) * 2 + (1 - x)
        self.sib = 1 - self.h

    def at(self, z, p, h):
        return {"dp": z * GRID_P + p, "head": h}

    def line(self, k):
        return lax.rem(self.z + k, GRID_Z)

    def line_back(self, k):
        if k == 0:
            return self.z
        return lax.rem(self.z + (GRID_Z - k), GRID_Z)

    def plane(self):
        places = [(self.px, self.h), (self.py, self.h), (self.pd, self.h)]
        places += [(p, self.sib) for p in (self.p, self.px, self.py, self.pd)]
        return places


def barrier(me):
    sem = pltpu.get_barrier_semaphore()
    for p, h in me.plane():
        pl.semaphore_signal(sem, 1, device_id=me.at(me.z, p, h), device_id_type=MESH)
    for k in (1, 2, 3):
        pl.semaphore_signal(sem, 1, device_id=me.at(me.line(k), me.p, me.h), device_id_type=MESH)
    pl.semaphore_wait(sem, 10)


def remote(src, dst, send, recv, device):
    return pltpu.make_async_remote_copy(
        src_ref=src, dst_ref=dst, send_sem=send, recv_sem=recv, device_id=device, device_id_type=MESH
    )


class Gather:
    SENDS, RECVS = 11, 11

    def __init__(self, me, shard, view, send, recv, local):
        self.me, self.shard, self.view = me, shard, view
        self.send, self.recv, self.local = send, recv, local
        self.started = []

    def go(self, index, parts):
        def make():
            src, dst, device = parts()
            return remote(src, dst, self.send.at[index], self.recv.at[index], device)

        make().start()
        self.started.append(make)

    def landed(self, index, region):
        me = self.me
        remote(region, region, self.send.at[index], self.recv.at[index], me.at(me.z, me.p, me.sib)).wait_recv()

    def set_of(self, z, p):
        return self.view(z, p, self.me.h)

    def first(self):
        me = self.me
        self.mine = pltpu.make_async_copy(self.shard, self.set_of(me.z, me.p), self.local)
        self.mine.start()
        for k in (1, 2, 3):
            self.go(k - 1, lambda k=k: (self.shard, self.set_of(me.z, me.p), me.at(me.line(k), me.p, me.h)))

    def second(self):
        me = self.me
        self.mine.wait()
        for k in (1, 2, 3):
            self.landed(k - 1, self.view(me.line_back(k), me.p, me.h))
        line = lambda: self.set_of(pl.ds(0, 4), me.p)
        self.go(3, lambda: (line(), line(), me.at(me.z, me.px, me.h)))
        self.go(4, lambda: (line(), line(), me.at(me.z, me.py, me.h)))
        self.go(7, lambda: (line(), line(), me.at(me.z, me.p, me.sib)))

    def third(self):
        me = self.me
        from_x, from_y = lambda: self.set_of(pl.ds(0, 4), me.px), lambda: self.set_of(pl.ds(0, 4), me.py)
        half_x, half_y = lambda: self.set_of(pl.ds(0, 2), me.px), lambda: self.set_of(pl.ds(2, 2), me.py)
        self.landed(3, from_x())
        self.go(6, lambda: (half_x(), half_x(), me.at(me.z, me.py, me.h)))
        self.landed(4, from_y())
        self.go(5, lambda: (half_y(), half_y(), me.at(me.z, me.px, me.h)))
        self.go(8, lambda: (from_x(), from_x(), me.at(me.z, me.p, me.sib)))
        self.go(9, lambda: (from_y(), from_y(), me.at(me.z, me.p, me.sib)))

    def fourth(self):
        me = self.me
        self.landed(6, self.view(pl.ds(0, 2), me.pd, me.h))
        self.landed(5, self.view(pl.ds(2, 2), me.pd, me.h))
        diagonal = lambda: self.set_of(pl.ds(0, 4), me.pd)
        self.go(10, lambda: (diagonal(), diagonal(), me.at(me.z, me.p, me.sib)))

    def fifth(self):
        me = self.me
        for index, p in ((7, me.p), (8, me.px), (9, me.py), (10, me.pd)):
            self.landed(index, self.view(pl.ds(0, 4), p, me.sib))

    def close(self):
        for make in self.started:
            make().wait_send()


class PieceGather(Gather):
    def first(self):
        me = self.me
        own = lambda: self.set_of(me.z, me.p)
        self.mine = pltpu.make_async_copy(self.shard, own(), self.local)
        self.mine.start()
        for k in (1, 2, 3):
            self.go(k - 1, lambda k=k: (self.shard, own(), me.at(me.line(k), me.p, me.h)))
        self.go(3, lambda: (self.shard, own(), me.at(me.z, me.px, me.h)))
        self.go(7, lambda: (self.shard, own(), me.at(me.z, me.py, me.h)))

    def relay(self, k):
        me = self.me
        piece = lambda: self.set_of(me.line_back(k), me.p)
        self.landed(k - 1, piece())
        self.go(3 + k, lambda: (piece(), piece(), me.at(me.z, me.px, me.h)))
        self.go(7 + k, lambda: (piece(), piece(), me.at(me.z, me.py, me.h)))

    def forward(self, k):
        me = self.me
        x, y = lambda: self.set_of(me.line_back(k), me.px), lambda: self.set_of(me.line_back(k), me.py)
        if k < 2:
            self.landed(3 + k, x())
            self.go(11 + k, lambda: (x(), x(), me.at(me.z, me.py, me.h)))
        else:
            self.landed(7 + k, y())
            self.go(11 + k, lambda: (y(), y(), me.at(me.z, me.px, me.h)))

    def across(self, index, p):
        me = self.me
        group = lambda: self.set_of(pl.ds(0, 4), p)
        self.go(index, lambda: (group(), group(), me.at(me.z, me.p, me.sib)))

    def own_across(self):
        self.mine.wait()
        self.across(15, self.me.p)

    def neighbours_across(self):
        me = self.me
        for k in (2, 3):
            self.landed(3 + k, self.set_of(me.line_back(k), me.px))
        self.across(16, me.px)
        for k in (0, 1):
            self.landed(7 + k, self.set_of(me.line_back(k), me.py))
        self.across(17, me.py)

    def diagonal_across(self):
        me = self.me
        for k in range(4):
            self.landed(11 + k, self.set_of(me.line_back(k), me.pd))
        self.across(18, me.pd)

    def fifth(self):
        me = self.me
        for index, p in ((15, me.p), (16, me.px), (17, me.py), (18, me.pd)):
            self.landed(index, self.view(pl.ds(0, 4), p, me.sib))


class SmallGather:
    SENDS, RECVS = 10, 10

    def __init__(self, me, tiles, send, recv):
        self.me, self.tiles, self.send, self.recv = me, tiles, send, recv
        self.started = []

    def go(self, index, parts):
        def make():
            region, device = parts()
            return remote(region, region, self.send.at[index], self.recv.at[index], device)

        make().start()
        self.started.append(make)

    def landed(self, index, region):
        me = self.me
        remote(region, region, self.send.at[index], self.recv.at[index], me.at(me.z, me.p, me.sib)).wait_recv()

    def first(self, gains, biases, up_bias):
        me = self.me
        place = lambda rows, width, start: dot(
            rows,
            jnp.where(
                lax.broadcasted_iota(jnp.int32, (width, LANES), 1)
                == lax.broadcasted_iota(jnp.int32, (width, LANES), 0) + start,
                1.0,
                0.0,
            ).astype(bf16),
        )
        start = (me.p * 2 + me.h) * 16
        rows = jnp.concatenate(
            [
                place(gains[...], 16, start),
                place(biases[...], 16, start),
                place(up_bias[...], 64, me.h * 64),
                jnp.zeros((7, LANES), f32),
            ],
            axis=0,
        )
        self.tiles[me.p, me.h, me.z] = rows.astype(bf16)

    def second(self):
        me = self.me
        for k in (1, 2, 3):
            self.go(k - 1, lambda k=k: (self.tiles.at[me.p, me.h, me.z], me.at(me.line(k), me.p, me.h)))

    def third(self):
        me = self.me
        for k in (1, 2, 3):
            self.landed(k - 1, self.tiles.at[me.p, me.h, me.line_back(k)])
        for index, (p, h) in enumerate(me.plane()):
            self.go(3 + index, lambda p=p, h=h: (self.tiles.at[me.p, me.h], me.at(me.z, p, h)))

    def fourth(self, gain_bias, up_bias):
        me = self.me
        for index, (p, h) in enumerate(me.plane()):
            self.landed(3 + index, self.tiles.at[p, h])
        for z in range(GRID_Z):
            total = jnp.zeros((8, LANES), f32)
            for p in range(GRID_P):
                pair = self.tiles[p, 0, z].astype(f32) + self.tiles[p, 1, z].astype(f32)
                total = total + pair[:8]
                up_bias[:, (z * GRID_P + p) * LANES : (z * GRID_P + p + 1) * LANES] = pair[8:9]
            gain_bias[:, z * LANES : (z + 1) * LANES] = total

    def close(self):
        for make in self.started:
            make().wait_send()


class Scatter:
    SENDS, RECVS = 8, 8

    def __init__(self, me, part, core, cross, sets, line, send, recv):
        self.me, self.part, self.core, self.cross, self.sets, self.line = me, part, core, cross, sets, line
        self.send, self.recv = send, recv
        self.started = []

    def go(self, index, parts):
        def make():
            src, dst, device = parts()
            return remote(src, dst, self.send.at[index], self.recv.at[index], device)

        make().start()
        self.started.append(make)

    def landed(self, index, region):
        me = self.me
        remote(region, region, self.send.at[index], self.recv.at[index], me.at(me.z, me.p, me.sib)).wait_recv()

    def first(self):
        me = self.me
        self.go(0, lambda: (self.part.at[me.sib], self.core, me.at(me.z, me.p, me.sib)))

    def second(self):
        me, part = self.me, self.part
        self.landed(0, self.core)

        def add(i, carry):
            z, p = i // GRID_P, lax.rem(i, GRID_P)
            part[me.h, z, p] = (part[me.h, z, p].astype(f32) + self.core[z, p].astype(f32)).astype(bf16)
            return carry

        lax.fori_loop(0, GRID_Z * GRID_P, add, 0)
        self.go(1, lambda: (part.at[me.h, pl.ds(0, 2), me.pd], self.cross.at[0], me.at(me.z, me.py, me.h)))
        self.go(2, lambda: (part.at[me.h, pl.ds(2, 2), me.pd], self.cross.at[1], me.at(me.z, me.px, me.h)))

    def third(self):
        me, part = self.me, self.part
        self.landed(1, self.cross.at[0])
        self.landed(2, self.cross.at[1])

        for i in range(2):
            part[me.h, i, me.px] = (part[me.h, i, me.px].astype(f32) + self.cross[0, i].astype(f32)).astype(bf16)
            part[me.h, 2 + i, me.py] = (
                part[me.h, 2 + i, me.py].astype(f32) + self.cross[1, i].astype(f32)
            ).astype(bf16)
        self.go(3, lambda: (part.at[me.h, :, me.px], self.sets.at[0], me.at(me.z, me.px, me.h)))
        self.go(4, lambda: (part.at[me.h, :, me.py], self.sets.at[1], me.at(me.z, me.py, me.h)))

    def fourth(self):
        me, part = self.me, self.part
        self.landed(3, self.sets.at[0])
        self.landed(4, self.sets.at[1])
        for i in range(GRID_Z):
            part[me.h, i, me.p] = (
                part[me.h, i, me.p].astype(f32) + self.sets[0, i].astype(f32) + self.sets[1, i].astype(f32)
            ).astype(bf16)
        for k in (1, 2, 3):
            self.go(
                4 + k,
                lambda k=k: (
                    part.at[me.h, me.line(k), me.p], self.line.at[k - 1], me.at(me.line(k), me.p, me.h)
                ),
            )

    def fifth(self):
        me = self.me
        total = self.part[me.h, me.z, me.p].astype(f32)
        for k in (1, 2, 3):
            self.landed(4 + k, self.line.at[k - 1])
            total = total + self.line[k - 1].astype(f32)
        return total

    def close(self):
        for make in self.started:
            make().wait_send()


class SmallScatter:
    SENDS, RECVS = 10, 10

    def __init__(self, me, part, line, sets, send, recv):
        self.me, self.part, self.line, self.sets = me, part, line, sets
        self.send, self.recv = send, recv
        self.started = []

    def go(self, index, parts):
        def make():
            src, dst, device = parts()
            return remote(src, dst, self.send.at[index], self.recv.at[index], device)

        make().start()
        self.started.append(make)

    def landed(self, index, region):
        me = self.me
        remote(region, region, self.send.at[index], self.recv.at[index], me.at(me.z, me.p, me.sib)).wait_recv()

    def first(self):
        me = self.me
        for k in (1, 2, 3):
            self.go(
                k - 1,
                lambda k=k: (self.part.at[me.line(k)], self.line.at[k - 1], me.at(me.line(k), me.p, me.h)),
            )

    def second(self):
        me = self.me
        total = self.part[me.z]
        for k in (1, 2, 3):
            self.landed(k - 1, self.line.at[k - 1])
            total = total + self.line[k - 1]
        self.sets[7] = total
        for index, (p, h) in enumerate(me.plane()):
            self.go(
                3 + index, lambda i=index, p=p, h=h: (self.sets.at[7], self.sets.at[i], me.at(me.z, p, h))
            )

    def third(self, gains, biases, up_bias):
        me = self.me
        total = self.sets[7]
        for index in range(7):
            self.landed(3 + index, self.sets.at[index])
            total = total + self.sets[index]
        rows = pltpu.roll(total[:8], LANES - 16 * (me.p * 2 + me.h), 1)
        gains[...] = rows[0:2, 0:16]
        biases[...] = rows[2:8, 0:16]
        row = lax.broadcasted_iota(jnp.int32, (8, LANES), 0)
        hidden = jnp.sum(jnp.where(row == me.p, total[8:], 0.0), axis=0, keepdims=True)
        hidden = jnp.where(me.h == 0, hidden[:, 0:64], hidden[:, 64:128])
        up_bias[...] = hidden

    def close(self):
        for make in self.started:
            make().wait_send()


ANY = pl.BlockSpec(memory_space=pl.ANY)
VM = pl.BlockSpec(memory_space=pltpu.VMEM)


def normalized(x):
    center = x - jnp.mean(x, axis=-1, keepdims=True)
    rstd = lax.rsqrt(jnp.mean(center * center, axis=-1, keepdims=True) + EPS)
    return center * rstd, rstd


def norm_back(e, xhat, rstd, gain):
    u = e * gain
    return rstd * (
        u - jnp.mean(u, axis=-1, keepdims=True) - xhat * jnp.mean(u * xhat, axis=-1, keepdims=True)
    )


def column_sums(x):
    return jnp.sum(x.reshape(x.shape[0] // 8, 8, x.shape[1]), axis=0)


def gelu_and_slope(u):
    phi = 0.5 + 0.5 * lax.erf(u * math.sqrt(0.5))
    return u * phi, phi + u * (jnp.exp(u * u * -0.5) * (1 / math.sqrt(2 * math.pi)))


def two_heads(x):
    first = lax.broadcasted_iota(jnp.int32, x.shape, 1) < 64
    zero = jnp.zeros_like(x)
    return jnp.concatenate([jnp.where(first, x, zero), jnp.where(first, zero, x)], axis=0)


def tiles(ref, rows):
    return jnp.concatenate([ref[p, rows] for p in range(4)], axis=1)


def hidden_masks(segment, kinds, mask):
    s, k = segment, kinds
    position = lax.broadcasted_iota(jnp.int32, s.shape, 1)
    follows = (s == pltpu.roll(s, 1, 1)) & (k == 2) & (pltpu.roll(k, 1, 1) == 2) & (position > 0)
    upper = lax.broadcasted_iota(jnp.int32, (SEQ, SEQ), 0) <= lax.broadcasted_iota(jnp.int32, (SEQ, SEQ), 1)
    run = dot(jnp.where(follows, 0.0, 1.0).astype(bf16), jnp.where(upper, 1.0, 0.0).astype(bf16))
    seg = s.astype(f32)
    for r in range(s.shape[0]):
        seg_j = jnp.broadcast_to(seg[r : r + 1], (SEQ, SEQ))
        run_j = jnp.broadcast_to(run[r : r + 1], (SEQ, SEQ))
        mask[r] = jnp.where((seg_j.T == seg_j) & (run_j.T <= run_j), 0.0, -jnp.inf).astype(bf16)


def layer_kernel(
    tokens_hbm, cot_hbm, qkv_s, out_s, up_s, down_s, gains, biases, up_bias, segment, kinds,
    output_hbm, grad_hbm, g_qkv, g_out, g_up, g_down, g_gains, g_biases, g_up_bias,
    tok, cot, w_qkv, w_out, w_up, w_down, gb, upb, mask,
    normed, packed, att, mix, hid, gpre, gbr, gmix, acc, acc_up, acc_q,
    out_stage, grad_stage,
    p_down0, p_down1, p_up0, p_up1, p_out, p_qkv, p_small,
    core0, core1, core2, core3, core4, core5, cross0, cross1, cross2, cross3, cross4, cross5,
    sets0, sets1, sets2, sets3, sets4, sets5, line0, line1, line2, line3, line4, line5,
    small_tiles, small_line, small_sets,
    g_send, g_recv, g_local, s_send, s_recv, io_sem, out_sem,
):
    T = tok.shape[0]
    ROWS = T // SEQ
    BM = out_stage.shape[1]
    count = T // BM
    me = Place()
    load_tok = pltpu.make_async_copy(tokens_hbm, tok, io_sem.at[0])
    load_cot = pltpu.make_async_copy(cot_hbm, cot, io_sem.at[1])
    load_tok.start()
    load_cot.start()

    def columns(h):
        return pl.ds(pl.multiple_of(h * 256, 256), 256)

    def up_view(half):
        return lambda z, p, h: w_up.at[z, p, h, :, pl.ds(1024 * half, 1024)]

    def down_view(half):
        return lambda z, p, h: w_down.at[z, p, h, pl.ds(32 * half, 32)]

    views = [
        (qkv_s, lambda z, p, h: w_qkv.at[:, z, p, :, columns(h)]),
        (out_s, lambda z, p, h: w_out.at[z, p, :, columns(h)]),
        (up_s.at[:, pl.ds(0, 1024)], up_view(0)),
        (up_s.at[:, pl.ds(1024, 1024)], up_view(1)),
        (down_s.at[pl.ds(0, 32)], down_view(0)),
        (down_s.at[pl.ds(32, 32)], down_view(1)),
    ]
    gathers = [
        (PieceGather if i == 0 else Gather)(me, shard, view, g_send.at[i], g_recv.at[i], g_local.at[i])
        for i, (shard, view) in enumerate(views)
    ]
    qkv_g, out_g, up_a, up_b, down_a, down_b = gathers
    small = SmallGather(me, small_tiles, g_send.at[6], g_recv.at[6])
    small.first(gains, biases, up_bias)
    barrier(me)
    small.second()
    qkv_g.first()
    own_rows = pl.ds(pl.multiple_of(me.h * ROWS, ROWS), ROWS)
    hidden_masks(segment[own_rows, :], kinds[own_rows, :], mask)
    small.third()
    qkv_g.relay(1)
    qkv_g.forward(0)
    qkv_g.relay(2)
    qkv_g.forward(1)
    qkv_g.relay(3)
    qkv_g.own_across()
    out_g.first()
    up_a.first()
    small.fourth(gb, upb)
    qkv_g.forward(2)
    qkv_g.forward(3)
    qkv_g.neighbours_across()
    up_b.first()
    out_g.second()
    load_tok.wait()

    def norm_one(i, carry):
        r = block(i, 256)
        xhat, _ = normalized(tok[r, :].astype(f32))
        normed[r, :] = (xhat * gb[0:1, :] + gb[2:3, :]).astype(bf16)
        return carry

    lax.fori_loop(0, T // 256, norm_one, 0)
    qkv_g.diagonal_across()
    up_a.second()
    down_a.first()
    down_b.first()
    qkv_g.fifth()

    def at_step(i, steps):
        for n, actions in steps.items():

            @pl.when(i == n)
            def _():
                for action in actions:
                    action()

    def project(i, carry):
        r = block(i, 512)
        x = normed[r, :]
        q = (dot(x, w_qkv[0].reshape(D, D)) + gb[3:4, :]).astype(bf16) * jnp.asarray(0.125, bf16)
        k = dot(x, w_qkv[1].reshape(D, D)).astype(bf16)
        v = (dot(x, w_qkv[2].reshape(D, D)) + gb[4:5, :]).astype(bf16)
        for p in range(4):
            for s, value in enumerate((q, k, v)):
                packed[s, p, r, :] = value[:, LANES * p : LANES * p + LANES]
        at_step(i, {1: [up_b.second], 2: [out_g.third]})
        return carry

    lax.fori_loop(0, T // 512, project, 0)

    def attend(i, carry):
        items = [(4 * i + u, p) for u in range(4) for p in range(4)]
        scores = [dot(two_heads(packed[1, p, block(r, SEQ), :]), packed[0, p, block(r, SEQ), :], NT) for r, p in items]
        weights = []
        for (r, p), pair in zip(items, scores):
            heads = []
            for h in range(2):
                t = pair[SEQ * h : SEQ * h + SEQ] + mask[r].astype(f32)
                e = jnp.exp(t - jnp.max(t, axis=0, keepdims=True))
                a = (e * (1.0 / jnp.sum(e, axis=0, keepdims=True))).astype(bf16)
                att[r, 2 * p + h] = a
                heads.append(a)
            weights.append(jnp.concatenate(heads, axis=0))
        for (r, p), pair in zip(items, weights):
            mix[p, block(r, SEQ), :] = dot(pair, two_heads(packed[2, p, block(r, SEQ), :]), TN).astype(bf16)
        at_step(i, {0: [up_a.third], 1: [out_g.fourth, down_a.second], 2: [up_b.third], 3: [down_b.second, up_a.fourth]})
        return carry

    lax.fori_loop(0, ROWS // 4, attend, 0)
    out_g.fifth()

    def middle_of(r):
        return tok[r, :].astype(f32) + dot(tiles(mix, r), w_out[...].reshape(D, D), NT) + gb[5:6, :]

    def norm_two(i, carry):
        r = block(i, 512)
        middle = middle_of(r)
        xhat, _ = normalized(middle)
        tok[r, :] = (xhat * gb[1:2, :] + gb[6:7, :]).astype(bf16)
        middle = middle.astype(bf16)
        for p in range(4):
            gmix[p, r, :] = middle[:, LANES * p : LANES * p + LANES]
        return carry

    lax.fori_loop(0, T // 512, norm_two, 0)
    up_b.fourth()
    up_a.fifth()
    up_b.fifth()

    def hidden_block(i, carry):
        r = block(i, BM)
        two = tok[r, :]
        for j in range(4):
            cols = slice(512 * j, 512 * j + 512)
            u = dot(two, w_up[:, :, :, :, cols].reshape(D, 512)) + upb[:, cols]
            hidden, slope = gelu_and_slope(u)
            hid[r, cols] = hidden.astype(bf16)
            gpre[r, cols] = slope.astype(bf16)
        at_step(i, {1: [down_a.third], 3: [down_b.third], 5: [down_a.fourth], 7: [down_b.fourth]})
        return carry

    lax.fori_loop(0, count, hidden_block, 0)
    load_cot.wait()
    down_a.fifth()
    down_b.fifth()
    acc[...] = jnp.zeros_like(acc)
    acc_up[...] = jnp.zeros_like(acc_up)
    acc_q[...] = jnp.zeros_like(acc_q)

    def hidden_back(i, carry):
        r = block(i, BM)
        c = cot[r, :]
        e = jnp.zeros((BM, D), f32)
        for j in range(4):
            cols = slice(512 * j, 512 * j + 512)
            grad_pre = dot(c, w_down[j].reshape(512, D), NT) * gpre[r, cols].astype(f32)
            acc_up[:, cols] += column_sums(grad_pre)
            grad_pre = grad_pre.astype(bf16)
            gpre[r, cols] = grad_pre
            e = e + dot(grad_pre, w_up[:, :, :, :, cols].reshape(D, 512), NT)
        xhat, rstd = normalized(tiles(gmix, r).astype(f32))
        cot_f32 = c.astype(f32)
        branch = (cot_f32 + norm_back(e, xhat, rstd, gb[1:2, :])).astype(bf16)
        gbr[r, :] = branch
        grad_mix = dot(branch, w_out[...].reshape(D, D)).astype(bf16)
        for p in range(4):
            gmix[p, r, :] = grad_mix[:, LANES * p : LANES * p + LANES]
        acc[1] += column_sums(e * xhat)
        acc[6] += column_sums(e)
        acc[5] += column_sums(branch.astype(f32))
        acc[7] += column_sums(cot_f32)
        return carry

    lax.fori_loop(0, count, hidden_back, 0)

    units = [
        Scatter(me, *refs, s_send.at[i], s_recv.at[i])
        for i, refs in enumerate(
            (
                (p_down0, core0, cross0, sets0, line0),
                (p_down1, core1, cross1, sets1, line1),
                (p_up0, core2, cross2, sets2, line2),
                (p_up1, core3, cross3, sets3, line3),
                (p_out, core4, cross4, sets4, line4),
                (p_qkv, core5, cross5, sets5, line5),
            )
        )
    ]
    d0, d1, u0, u1, out_u, qkv_u = units

    def grad_down_chunk(half, part):
        def body(z, carry):
            o = dot(cot[:, 256 * half : 256 * half + 256], hid[:, block(z, 512)], TN).astype(bf16).T
            for p in range(GRID_P):
                for h in range(2):
                    for j in range(2):
                        part[h, z, p, 64 * j : 64 * j + 64] = o[
                            64 * (2 * p + h) : 64 * (2 * p + h) + 64, LANES * j : LANES * j + LANES
                        ]
            return carry

        return body

    def grad_up_chunk(half, part):
        def body(c, carry):
            o = dot(tok[...], gpre[:, block(2 * half + c, 512)], TN).astype(bf16)
            for z in range(GRID_Z):
                for p in range(GRID_P):
                    for h in range(2):
                        d = (z * 4 + p) * 2 + h
                        for j in range(4):
                            part[h, z, p, pl.ds(pl.multiple_of(64 * c + 16 * j, 16), 16)] = o[
                                16 * d : 16 * d + 16, LANES * j : LANES * j + LANES
                            ]
            return carry

        return body

    lax.fori_loop(0, 4, grad_down_chunk(0, p_down0), 0)
    d0.first()
    lax.fori_loop(0, 4, grad_down_chunk(1, p_down1), 0)
    d1.first()
    d0.second()
    lax.fori_loop(0, 2, grad_up_chunk(0, p_up0), 0)
    u0.first()
    d1.second()
    lax.fori_loop(0, 2, grad_up_chunk(1, p_up1), 0)
    u1.first()
    load_tok = pltpu.make_async_copy(tokens_hbm, tok, io_sem.at[0])
    load_tok.start()
    u0.second()
    d0.third()

    o = dot(gbr[...], jnp.concatenate([mix[p] for p in range(4)], axis=1), TN).astype(bf16)
    for z in range(GRID_Z):
        for p in range(GRID_P):
            d = z * 4 + p
            for h in range(2):
                for j in range(2):
                    p_out[h, z, p, 32 * j : 32 * j + 32] = o[
                        32 * d : 32 * d + 32, 256 * h + LANES * j : 256 * h + LANES * j + LANES
                    ]
    out_u.first()
    u1.second()
    d1.third()

    def attend_back(half, steps):
        def body(i, carry):
            row = lax.broadcasted_iota(jnp.int32, (2 * SEQ, LANES), 0) // SEQ
            lane = lax.broadcasted_iota(jnp.int32, (2 * SEQ, LANES), 1) // 64
            minus = jnp.where(row == lane, -1.0, 0.0).astype(bf16)
            items = [(4 * i + u, 2 * half + pp) for u in range(4) for pp in range(2)]
            grads, slopes = [], []
            for r, p in items:
                rows = block(r, SEQ)
                grad = gmix[p, rows, :]
                product = (grad.astype(f32) * mix[p, rows, :].astype(f32)).astype(bf16)
                values = jnp.concatenate([two_heads(packed[2, p, rows, :]), minus], axis=1)
                grads.append(dot(values, jnp.concatenate([grad, product], axis=1), NT))
            for (r, p), pair in zip(items, grads):
                slopes.append(
                    [
                        (att[r, 2 * p + h].astype(f32) * pair[SEQ * h : SEQ * h + SEQ]).astype(bf16)
                        for h in range(2)
                    ]
                )
            for (r, p), pair in zip(items, slopes):
                rows = block(r, SEQ)
                queries, keys = two_heads(packed[0, p, rows, :]), two_heads(packed[1, p, rows, :])
                g_q = dot(jnp.concatenate(pair, axis=0), keys, TN) * 0.125
                g_k = dot(jnp.concatenate(pair, axis=1), queries)
                weights = jnp.concatenate([att[r, 2 * p], att[r, 2 * p + 1]], axis=1)
                g_v = dot(weights, two_heads(gmix[p, rows, :]))
                packed[0, p, rows, :] = g_q.astype(bf16)
                packed[1, p, rows, :] = g_k.astype(bf16)
                packed[2, p, rows, :] = g_v.astype(bf16)
                acc_q[0, p] += column_sums(g_q)
                acc_q[1, p] += column_sums(g_v)
            at_step(i, steps)
            return carry

        return body

    def grad_qkv_half(half):
        def body(s, carry):
            wide = jnp.concatenate([packed[s, 2 * half], packed[s, 2 * half + 1]], axis=1)
            o = dot(normed[...], wide, TN).astype(bf16)
            for z in range(GRID_Z):
                for p in range(GRID_P):
                    d = z * 4 + p
                    for j in range(2):
                        p_qkv[half, z, p, pl.ds(pl.multiple_of(64 * s + 32 * j, 32), 32)] = o[
                            32 * d : 32 * d + 32, LANES * j : LANES * j + LANES
                        ]
            return carry

        return body

    lax.fori_loop(0, ROWS // 4, attend_back(me.sib, {0: [u0.third], 1: [d0.fourth], 3: [out_u.second]}), 0)
    lax.fori_loop(0, 3, grad_qkv_half(me.sib), 0)
    qkv_u.first()
    u1.third()
    d1.fourth()
    lax.fori_loop(0, ROWS // 4, attend_back(me.h, {1: [out_u.third], 2: [u0.fourth]}), 0)
    lax.fori_loop(0, 3, grad_qkv_half(me.h), 0)
    qkv_u.second()
    u1.fourth()
    out_u.fourth()
    load_tok.wait()

    def grad_copy(i):
        return pltpu.make_async_copy(
            grad_stage.at[parity(i)], grad_hbm.at[block(i, BM), :], out_sem.at[2 + parity(i)]
        )

    def norm_one_back(i, carry):
        r = block(i, BM)

        @pl.when(i >= 2)
        def _():
            grad_copy(i - 2).wait()

        e = dot(tiles(packed.at[0], r), w_qkv[0].reshape(D, D), NT)
        e = e + dot(tiles(packed.at[1], r), w_qkv[1].reshape(D, D), NT)
        e = e + dot(tiles(packed.at[2], r), w_qkv[2].reshape(D, D), NT)
        xhat, rstd = normalized(tok[r, :].astype(f32))
        grad_stage[parity(i)] = gbr[r, :].astype(f32) + norm_back(e, xhat, rstd, gb[0:1, :])
        grad_copy(i).start()
        acc[0] += column_sums(e * xhat)
        acc[2] += column_sums(e)
        at_step(i, {5: [qkv_u.third]})
        return carry

    lax.fori_loop(0, count, norm_one_back, 0)
    for p in range(4):
        acc[3, :, LANES * p : LANES * p + LANES] = acc_q[0, p]
        acc[4, :, LANES * p : LANES * p + LANES] = acc_q[1, p]
    for z in range(GRID_Z):
        rows = [jnp.sum(acc[n, :, LANES * z : LANES * z + LANES], axis=0, keepdims=True) for n in range(8)]
        rows += [
            jnp.sum(acc_up[:, 512 * z + LANES * p : 512 * z + LANES * p + LANES], axis=0, keepdims=True)
            for p in range(GRID_P)
        ]
        rows += [jnp.zeros((4, LANES), f32)]
        p_small[z] = jnp.concatenate(rows, axis=0)
    small_sum = SmallScatter(me, p_small, small_line, small_sets, s_send.at[6], s_recv.at[6])
    small_sum.first()

    def out_copy(i):
        return pltpu.make_async_copy(
            out_stage.at[parity(i)], output_hbm.at[block(i, BM), :], out_sem.at[parity(i)]
        )

    def output_block(i, carry):
        r = block(i, BM)

        @pl.when(i >= 2)
        def _():
            out_copy(i - 2).wait()

        total = middle_of(r) + dot(hid[r, :], w_down[...].reshape(2048, D)) + gb[7:8, :]
        out_stage[parity(i)] = total.astype(bf16)
        out_copy(i).start()
        at_step(i, {3: [small_sum.second, qkv_u.fourth]})
        return carry

    lax.fori_loop(0, count, output_block, 0)
    for unit, j0 in ((d0, 0), (d1, 2)):
        total = unit.fifth()
        for j in range(2):
            g_down[:, LANES * (j0 + j) : LANES * (j0 + j) + LANES] = total[64 * j : 64 * j + 64]
    for unit, j0 in ((u0, 0), (u1, 8)):
        total = unit.fifth()
        for j in range(8):
            g_up[:, LANES * (j0 + j) : LANES * (j0 + j) + LANES] = total[16 * j : 16 * j + 16]
    total = out_u.fifth()
    for j in range(2):
        g_out[:, LANES * j : LANES * j + LANES] = total[32 * j : 32 * j + 32]
    small_sum.third(g_gains, g_biases, g_up_bias)
    total = qkv_u.fifth()
    for s in range(3):
        for j in range(2):
            g_qkv[s, :, LANES * j : LANES * j + LANES] = total[64 * s + 32 * j : 64 * s + 32 * j + 32]
    for i in (count - 2, count - 1):
        out_copy(i).wait()
        grad_copy(i).wait()
    for item in gathers + units + [small, small_sum]:
        item.close()


def finish_kernel(*refs):
    for source, target in zip(refs[:9], refs[9:]):
        target[...] = source[...]


def finish(*arrays):
    steps = 4

    def spec(array, n):
        if n < 2:
            return pl.BlockSpec((array.shape[0] // steps, array.shape[1]), lambda i: (i, 0))
        return pl.BlockSpec(array.shape, lambda i: (0,) * array.ndim)

    specs = [spec(a, n) for n, a in enumerate(arrays)]
    return pl.pallas_call(
        finish_kernel,
        out_shape=tuple(jax.ShapeDtypeStruct(a.shape, a.dtype) for a in arrays),
        grid=(steps,),
        in_specs=specs,
        out_specs=specs,
        compiler_params=pltpu.CompilerParams(vmem_limit_bytes=VMEM_LIMIT),
        name="finish",
    )(*arrays)


def layer(tokens, cotangent, qkv, out, up, down, gains, biases, up_bias, segment, kinds):
    shape = jax.ShapeDtypeStruct
    T = tokens.shape[0]
    rows = T // SEQ
    outs = (
        shape((T, D), bf16),
        shape((T, D), f32),
        shape((3, 32, 256), f32),
        shape((32, 256), f32),
        shape((16, 2048), f32),
        shape((64, 512), f32),
        shape((2, 16), f32),
        shape((6, 16), f32),
        shape((1, 64), f32),
    )
    sizes = [128, 128, 128, 128, 64, 192]
    BM = 256
    V, S = pltpu.VMEM, pltpu.SemaphoreType.DMA
    scratch = [
        V((T, D), bf16), V((T, D), bf16),
        V((3, 4, 4, 32, 512), bf16), V((4, 4, 32, 512), bf16),
        V((4, 4, 2, 16, 2048), bf16), V((4, 4, 2, 64, 512), bf16),
        V((8, 512), f32), V((1, 2048), f32), V((rows, SEQ, SEQ), bf16),
        V((T, D), bf16), V((3, 4, T, LANES), bf16), V((rows, 8, SEQ, SEQ), bf16),
        V((4, T, LANES), bf16), V((T, 2048), bf16), V((T, 2048), bf16),
        V((T, D), bf16), V((4, T, LANES), bf16), V((8, 8, 512), f32), V((8, 2048), f32),
        V((2, 4, 8, LANES), f32),
        V((2, BM, D), bf16), V((2, BM, D), f32),
    ]
    scratch += [V((2, 4, 4, r, LANES), bf16) for r in sizes] + [V((4, 16, LANES), f32)]
    scratch += [V((4, 4, r, LANES), bf16) for r in sizes]
    scratch += [V((2, 2, r, LANES), bf16) for r in sizes]
    scratch += [V((2, 4, r, LANES), bf16) for r in sizes]
    scratch += [V((3, r, LANES), bf16) for r in sizes]
    scratch += [V((4, 2, 4, 16, LANES), bf16), V((3, 16, LANES), f32), V((8, 16, LANES), f32)]
    scratch += [S((7, 19)), S((7, 19)), S((6,)), S((7, 10)), S((7, 10)), S((2,)), S((4,))]
    return pl.pallas_call(
        layer_kernel,
        out_shape=outs,
        in_specs=[ANY] * 6 + [VM] * 5,
        out_specs=[ANY] * 2 + [VM] * 7,
        scratch_shapes=scratch,
        compiler_params=pltpu.CompilerParams(
            collective_id=0, has_side_effects=True, vmem_limit_bytes=VMEM_LIMIT
        ),
        name="layer",
    )(tokens, cotangent, qkv, out, up, down, gains, biases, up_bias, segment, kinds)


def widened(x, axes, dim):
    return lax.all_gather(x, axes, axis=dim, tiled=True)


def on_device(rep):
    def run(
        tokens, qkv, out, up, down, gains, biases, up_bias, segment, kinds, cotangent
    ):
        up_bias = up_bias.reshape(1, -1)
        head = lax.axis_index("head")
        if rep > 1:
            both = ("rep", "head")
            qkv, out = widened(qkv, "rep", 1), widened(out, "rep", 0)
            up = lax.dynamic_slice_in_dim(widened(up, both, 0), head * 16, 16, 0)
            down = lax.dynamic_slice_in_dim(widened(down, both, 0), head * 64, 64, 0)
            gains = lax.dynamic_slice_in_dim(widened(gains, both, 1), head * 16, 16, 1)
            biases = lax.dynamic_slice_in_dim(widened(biases, both, 1), head * 16, 16, 1)
            up_bias = lax.dynamic_slice_in_dim(widened(up_bias, both, 1), head * 64, 64, 1)
        output, grad, *grads = finish(
            *layer(tokens, cotangent, qkv, out, up, down, gains, biases, up_bias, segment, kinds)
        )
        if rep > 1:
            place = lax.axis_index("rep") * 2 + head

            def own(x, dim):
                x = lax.all_gather(lax.psum(x, "rep"), "head", axis=dim, tiled=True)
                size = x.shape[dim] // (2 * rep)
                return lax.dynamic_slice_in_dim(x, place * size, size, dim)

            for i, dim in ((0, 1), (1, 0)):
                grads[i] = lax.psum_scatter(grads[i], "rep", scatter_dimension=dim, tiled=True)
            for i, dim in ((2, 0), (3, 0), (4, 1), (5, 1), (6, 1)):
                grads[i] = own(grads[i], dim)
        grads[6] = grads[6].reshape(-1)
        return (output, grad, *grads)

    return run


def solution(mesh):
    rep = mesh.shape["dp"] // (GRID_Z * GRID_P)
    wide = Mesh(mesh.devices.reshape(GRID_Z * GRID_P, rep, 2), ("dp", "rep", "head"))
    dp, every = ("dp", "rep"), ("dp", "rep", "head")
    in_specs = (
        P(every, None),
        P(None, dp, "head"),
        P(dp, "head"),
        P(every, None),
        P(every, None),
        P(None, every),
        P(None, every),
        P(every),
        P(dp, None),
        P(dp, None),
        P(every, None),
    )
    out_specs = (
        P(every, None),
        P(every, None),
        P(None, dp, "head"),
        P(dp, "head"),
        P(every, None),
        P(every, None),
        P(None, every),
        P(None, every),
        P(every),
    )
    return jax.shard_map(
        on_device(rep), mesh=wide, in_specs=in_specs, out_specs=out_specs, check_vma=False
    )
```

```python
import math

import jax
import jax.numpy as jnp
from jax import lax
from jax.experimental import pallas as pl
from jax.experimental.pallas import tpu as pltpu
from jax.sharding import Mesh
from jax.sharding import PartitionSpec as P

bf16, f32 = jnp.bfloat16, jnp.float32
D = 512
SEQ = 128
LANES = 128
GRID_Z, GRID_P = 4, 4
EPS = 1e-5
MESH = pl.DeviceIdType.MESH
NN = (((1,), (0,)), ((), ()))
NT = (((1,), (1,)), ((), ()))
TN = (((0,), (0,)), ((), ()))
DOWN_ROWS, UP_ROWS, OUT_ROWS, QKV_ROWS, SMALL_ROWS, ALL_ROWS = 0, 256, 512, 576, 768, 784
VMEM_LIMIT = (63 << 20) + (512 << 10)


def dot(a, b, dims=NN):
    return lax.dot_general(a, b, dims, preferred_element_type=f32)


def block(index, size):
    if isinstance(index, int):
        return pl.ds(index * size, size)
    return pl.ds(pl.multiple_of(index * size, size), size)


def parity(index):
    return index % 2 if isinstance(index, int) else lax.rem(index, 2)


class Place:
    def __init__(self):
        dp, self.h = lax.axis_index("dp"), lax.axis_index("head")
        self.z, self.p = dp // GRID_P, lax.rem(dp, GRID_P)
        x, y = lax.rem(self.p, 2), self.p // 2
        self.px = y * 2 + (1 - x)
        self.py = (1 - y) * 2 + x
        self.pd = (1 - y) * 2 + (1 - x)
        self.sib = 1 - self.h

    def at(self, z, p, h):
        return {"dp": z * GRID_P + p, "head": h}

    def line(self, k):
        return lax.rem(self.z + k, GRID_Z)

    def line_back(self, k):
        if k == 0:
            return self.z
        return lax.rem(self.z + (GRID_Z - k), GRID_Z)

    def plane(self):
        places = [(self.px, self.h), (self.py, self.h), (self.pd, self.h)]
        places += [(p, self.sib) for p in (self.p, self.px, self.py, self.pd)]
        return places


def barrier(me):
    sem = pltpu.get_barrier_semaphore()
    for p, h in me.plane():
        pl.semaphore_signal(sem, 1, device_id=me.at(me.z, p, h), device_id_type=MESH)
    for k in (1, 2, 3):
        pl.semaphore_signal(sem, 1, device_id=me.at(me.line(k), me.p, me.h), device_id_type=MESH)
    pl.semaphore_wait(sem, 10)


def remote(src, dst, send, recv, device):
    return pltpu.make_async_remote_copy(
        src_ref=src, dst_ref=dst, send_sem=send, recv_sem=recv, device_id=device, device_id_type=MESH
    )


class Gather:
    SENDS, RECVS = 11, 11

    def __init__(self, me, shard, view, send, recv, local):
        self.me, self.shard, self.view = me, shard, view
        self.send, self.recv, self.local = send, recv, local
        self.started = []

    def go(self, index, parts):
        def make():
            src, dst, device = parts()
            return remote(src, dst, self.send.at[index], self.recv.at[index], device)

        make().start()
        self.started.append(make)

    def landed(self, index, region):
        me = self.me
        remote(region, region, self.send.at[index], self.recv.at[index], me.at(me.z, me.p, me.sib)).wait_recv()

    def set_of(self, z, p):
        return self.view(z, p, self.me.h)

    def first(self):
        me = self.me
        self.mine = pltpu.make_async_copy(self.shard, self.set_of(me.z, me.p), self.local)
        self.mine.start()
        for k in (1, 2, 3):
            self.go(k - 1, lambda k=k: (self.shard, self.set_of(me.z, me.p), me.at(me.line(k), me.p, me.h)))

    def second(self):
        me = self.me
        self.mine.wait()
        for k in (1, 2, 3):
            self.landed(k - 1, self.view(me.line_back(k), me.p, me.h))
        line = lambda: self.set_of(pl.ds(0, 4), me.p)
        self.go(3, lambda: (line(), line(), me.at(me.z, me.px, me.h)))
        self.go(4, lambda: (line(), line(), me.at(me.z, me.py, me.h)))
        self.go(7, lambda: (line(), line(), me.at(me.z, me.p, me.sib)))

    def third(self):
        me = self.me
        from_x, from_y = lambda: self.set_of(pl.ds(0, 4), me.px), lambda: self.set_of(pl.ds(0, 4), me.py)
        half_x, half_y = lambda: self.set_of(pl.ds(0, 2), me.px), lambda: self.set_of(pl.ds(2, 2), me.py)
        self.landed(3, from_x())
        self.go(6, lambda: (half_x(), half_x(), me.at(me.z, me.py, me.h)))
        self.landed(4, from_y())
        self.go(5, lambda: (half_y(), half_y(), me.at(me.z, me.px, me.h)))
        self.go(8, lambda: (from_x(), from_x(), me.at(me.z, me.p, me.sib)))
        self.go(9, lambda: (from_y(), from_y(), me.at(me.z, me.p, me.sib)))

    def fourth(self):
        me = self.me
        self.landed(6, self.view(pl.ds(0, 2), me.pd, me.h))
        self.landed(5, self.view(pl.ds(2, 2), me.pd, me.h))
        diagonal = lambda: self.set_of(pl.ds(0, 4), me.pd)
        self.go(10, lambda: (diagonal(), diagonal(), me.at(me.z, me.p, me.sib)))

    def fifth(self):
        me = self.me
        for index, p in ((7, me.p), (8, me.px), (9, me.py), (10, me.pd)):
            self.landed(index, self.view(pl.ds(0, 4), p, me.sib))

    def close(self):
        for make in self.started:
            make().wait_send()


class DirectGather(Gather):
    def others(self):
        return self.me.px, self.me.py, self.me.pd

    def first(self):
        me = self.me
        own = lambda: self.set_of(me.z, me.p)
        self.mine = pltpu.make_async_copy(self.shard, own(), self.local)
        self.mine.start()
        for k in (1, 2, 3):
            self.go(k - 1, lambda k=k: (self.shard, own(), me.at(me.line(k), me.p, me.h)))
        for n, p in enumerate(self.others()):
            self.go(3 + 4 * n, lambda p=p: (self.shard, own(), me.at(me.z, p, me.h)))

    def relay(self, k):
        me = self.me
        piece = lambda: self.set_of(me.line_back(k), me.p)
        self.landed(k - 1, piece())
        for n, p in enumerate(self.others()):
            self.go(3 + 4 * n + k, lambda p=p: (piece(), piece(), me.at(me.z, p, me.h)))

    def across(self, index, p):
        me = self.me
        group = lambda: self.set_of(pl.ds(0, 4), p)
        self.go(index, lambda: (group(), group(), me.at(me.z, me.p, me.sib)))

    def own_across(self):
        self.mine.wait()
        self.across(15, self.me.p)

    def other_across(self, n):
        me = self.me
        p = self.others()[n]
        for k in range(4):
            self.landed(3 + 4 * n + k, self.set_of(me.line_back(k), p))
        self.across(16 + n, p)

    def fifth(self):
        me = self.me
        for index, p in ((15, me.p), (16, me.px), (17, me.py), (18, me.pd)):
            self.landed(index, self.view(pl.ds(0, 4), p, me.sib))


class PlaneGather(Gather):
    def group(self, z):
        return self.view(z, pl.ds(0, 4), self.me.h)

    def first(self):
        me = self.me
        own = lambda: self.set_of(me.z, me.p)
        self.mine = pltpu.make_async_copy(self.shard, own(), self.local)
        self.mine.start()
        for n, p in enumerate((me.px, me.py, me.pd)):
            self.go(n, lambda p=p: (self.shard, own(), me.at(me.z, p, me.h)))

    def second(self):
        me = self.me
        self.mine.wait()
        for n, p in enumerate((me.px, me.py, me.pd)):
            self.landed(n, self.set_of(me.z, p))
        for k in (1, 2, 3):
            self.go(2 + k, lambda k=k: (self.group(me.z), self.group(me.z), me.at(me.line(k), me.p, me.h)))
        self.go(6, lambda: (self.group(me.z), self.group(me.z), me.at(me.z, me.p, me.sib)))

    def third(self):
        me = self.me
        for k in (1, 2, 3):
            z = me.line_back(k)
            self.landed(2 + k, self.group(z))
            self.go(6 + k, lambda z=z: (self.group(z), self.group(z), me.at(me.z, me.p, me.sib)))

    def fourth(self):
        pass

    def fifth(self):
        me = self.me
        for k in range(4):
            self.landed(6 + k, self.view(me.line_back(k), pl.ds(0, 4), me.sib))


class SmallGather:
    def __init__(self, me, tiles, lines, send, recv):
        self.me, self.tiles, self.lines, self.send, self.recv = me, tiles, lines, send, recv
        self.started = []

    def go(self, index, parts):
        def make():
            region, device = parts()
            return remote(region, region, self.send.at[index], self.recv.at[index], device)

        make().start()
        self.started.append(make)

    def landed(self, index, region):
        me = self.me
        remote(region, region, self.send.at[index], self.recv.at[index], me.at(me.z, me.p, me.sib)).wait_recv()

    def first(self, gains, biases, up_bias):
        me = self.me
        place = lambda rows, width, start: dot(
            rows,
            jnp.where(
                lax.broadcasted_iota(jnp.int32, (width, LANES), 1)
                == lax.broadcasted_iota(jnp.int32, (width, LANES), 0) + start,
                1.0,
                0.0,
            ).astype(bf16),
        )
        start = (me.p * 2 + me.h) * 16
        row = lax.broadcasted_iota(jnp.int32, (8, LANES), 0)
        hidden = jnp.broadcast_to(place(up_bias[...], 64, me.h * 64), (8, LANES))
        rows = jnp.concatenate(
            [
                place(gains[...], 16, start),
                place(biases[...], 16, start),
                jnp.where(row == me.p, hidden, 0.0),
            ],
            axis=0,
        )
        self.tiles[me.p, me.h] = rows.astype(bf16)

    def second(self):
        me = self.me
        for index, (p, h) in enumerate(me.plane()):
            self.go(index, lambda p=p, h=h: (self.tiles.at[me.p, me.h], me.at(me.z, p, h)))

    def third(self):
        me = self.me
        for index, (p, h) in enumerate(me.plane()):
            self.landed(index, self.tiles.at[p, h])
        total = jnp.zeros((16, LANES), f32)
        for p in range(GRID_P):
            for h in range(2):
                total = total + self.tiles[p, h].astype(f32)
        self.lines[me.z] = total.astype(bf16)
        for k in (1, 2, 3):
            self.go(6 + k, lambda k=k: (self.lines.at[me.z], me.at(me.line(k), me.p, me.h)))

    def fourth(self, gain_bias, up_bias):
        me = self.me
        for k in (1, 2, 3):
            self.landed(6 + k, self.lines.at[me.line_back(k)])
        for z in range(GRID_Z):
            line = self.lines[z].astype(f32)
            gain_bias[:, z * LANES : (z + 1) * LANES] = line[:8]
            for p in range(GRID_P):
                up_bias[:, (z * GRID_P + p) * LANES : (z * GRID_P + p + 1) * LANES] = line[8 + p : 9 + p]

    def close(self):
        for make in self.started:
            make().wait_send()


class Scatter:
    SENDS, RECVS = 8, 8

    def __init__(self, me, part, core, cross, sets, line, send, recv):
        self.me, self.part, self.core, self.cross, self.sets, self.line = me, part, core, cross, sets, line
        self.send, self.recv = send, recv
        self.started = []

    def go(self, index, parts):
        def make():
            src, dst, device = parts()
            return remote(src, dst, self.send.at[index], self.recv.at[index], device)

        make().start()
        self.started.append(make)

    def landed(self, index, region):
        me = self.me
        remote(region, region, self.send.at[index], self.recv.at[index], me.at(me.z, me.p, me.sib)).wait_recv()

    def first(self):
        me = self.me
        self.go(0, lambda: (self.part.at[me.sib], self.core, me.at(me.z, me.p, me.sib)))

    def second(self):
        me, part = self.me, self.part
        self.landed(0, self.core)
        part[me.h] = part[me.h] + self.core[...]
        self.go(1, lambda: (part.at[me.h, pl.ds(0, 2), me.pd], self.cross.at[0], me.at(me.z, me.py, me.h)))
        self.go(2, lambda: (part.at[me.h, pl.ds(2, 2), me.pd], self.cross.at[1], me.at(me.z, me.px, me.h)))

    def third(self):
        me, part = self.me, self.part
        self.landed(1, self.cross.at[0])
        self.landed(2, self.cross.at[1])

        for i in range(2):
            part[me.h, i, me.px] = part[me.h, i, me.px] + self.cross[0, i]
            part[me.h, 2 + i, me.py] = part[me.h, 2 + i, me.py] + self.cross[1, i]
        self.go(3, lambda: (part.at[me.h, :, me.px], self.sets.at[0], me.at(me.z, me.px, me.h)))
        self.go(4, lambda: (part.at[me.h, :, me.py], self.sets.at[1], me.at(me.z, me.py, me.h)))

    def fourth(self):
        me, part = self.me, self.part
        self.landed(3, self.sets.at[0])
        self.landed(4, self.sets.at[1])
        for i in range(GRID_Z):
            part[me.h, i, me.p] = (
                part[me.h, i, me.p].astype(f32) + self.sets[0, i].astype(f32) + self.sets[1, i].astype(f32)
            ).astype(bf16)
        for k in (1, 2, 3):
            self.go(
                4 + k,
                lambda k=k: (
                    part.at[me.h, me.line(k), me.p], self.line.at[k - 1], me.at(me.line(k), me.p, me.h)
                ),
            )

    def fifth(self):
        me = self.me
        total = self.part[me.h, me.z, me.p].astype(f32)
        for k in (1, 2, 3):
            self.landed(4 + k, self.line.at[k - 1])
            total = total + self.line[k - 1].astype(f32)
        return total

    def close(self):
        for make in self.started:
            make().wait_send()


class SmallScatter:
    SENDS, RECVS = 10, 10

    def __init__(self, me, part, line, sets, send, recv):
        self.me, self.part, self.line, self.sets = me, part, line, sets
        self.send, self.recv = send, recv
        self.started = []

    def go(self, index, parts):
        def make():
            src, dst, device = parts()
            return remote(src, dst, self.send.at[index], self.recv.at[index], device)

        make().start()
        self.started.append(make)

    def landed(self, index, region):
        me = self.me
        remote(region, region, self.send.at[index], self.recv.at[index], me.at(me.z, me.p, me.sib)).wait_recv()

    def first(self):
        me = self.me
        for k in (1, 2, 3):
            self.go(
                k - 1,
                lambda k=k: (self.part.at[me.line(k)], self.line.at[k - 1], me.at(me.line(k), me.p, me.h)),
            )

    def second(self):
        me = self.me
        total = self.part[me.z]
        for k in (1, 2, 3):
            self.landed(k - 1, self.line.at[k - 1])
            total = total + self.line[k - 1]
        self.sets[7] = total
        for index, (p, h) in enumerate(me.plane()):
            self.go(
                3 + index, lambda i=index, p=p, h=h: (self.sets.at[7], self.sets.at[i], me.at(me.z, p, h))
            )

    def third(self, sums):
        me = self.me
        total = self.sets[7]
        for index in range(7):
            self.landed(3 + index, self.sets.at[index])
            total = total + self.sets[index]
        sums[SMALL_ROWS : SMALL_ROWS + 8] = pltpu.roll(total[:8], LANES - 16 * (me.p * 2 + me.h), 1)
        row = lax.broadcasted_iota(jnp.int32, (8, LANES), 0)
        hidden = jnp.sum(jnp.where(row == me.p, total[8:], 0.0), axis=0, keepdims=True)
        hidden = jnp.broadcast_to(hidden, (8, LANES))
        sums[SMALL_ROWS + 8 : SMALL_ROWS + 16] = jnp.where(me.h == 0, hidden, pltpu.roll(hidden, 64, 1))

    def close(self):
        for make in self.started:
            make().wait_send()


ANY = pl.BlockSpec(memory_space=pl.ANY)
VM = pl.BlockSpec(memory_space=pltpu.VMEM)


def normalized(x):
    center = x - jnp.mean(x, axis=-1, keepdims=True)
    rstd = lax.rsqrt(jnp.mean(center * center, axis=-1, keepdims=True) + EPS)
    return center * rstd, rstd


def norm_back(e, xhat, rstd, gain):
    u = e * gain
    return rstd * (
        u - jnp.mean(u, axis=-1, keepdims=True) - xhat * jnp.mean(u * xhat, axis=-1, keepdims=True)
    )


def column_sums(x):
    return jnp.sum(x.reshape(x.shape[0] // 8, 8, x.shape[1]), axis=0)


def gelu_and_slope(u):
    phi = 0.5 + 0.5 * lax.erf(u * math.sqrt(0.5))
    return u * phi, phi + u * (jnp.exp(u * u * -0.5) * (1 / math.sqrt(2 * math.pi)))


def two_heads(x):
    first = lax.broadcasted_iota(jnp.int32, x.shape, 1) < 64
    zero = jnp.zeros_like(x)
    return jnp.concatenate([jnp.where(first, x, zero), jnp.where(first, zero, x)], axis=0)


def tiles(ref, rows):
    return jnp.concatenate([ref[p, rows] for p in range(4)], axis=1)


def hidden_masks(segment, kinds, mask):
    s, k = segment, kinds
    position = lax.broadcasted_iota(jnp.int32, s.shape, 1)
    follows = (s == pltpu.roll(s, 1, 1)) & (k == 2) & (pltpu.roll(k, 1, 1) == 2) & (position > 0)
    upper = lax.broadcasted_iota(jnp.int32, (SEQ, SEQ), 0) <= lax.broadcasted_iota(jnp.int32, (SEQ, SEQ), 1)
    run = dot(jnp.where(follows, 0.0, 1.0).astype(bf16), jnp.where(upper, 1.0, 0.0).astype(bf16))
    seg = s.astype(f32)
    for r in range(s.shape[0]):
        seg_j = jnp.broadcast_to(seg[r : r + 1], (SEQ, SEQ))
        run_j = jnp.broadcast_to(run[r : r + 1], (SEQ, SEQ))
        mask[r] = jnp.where((seg_j.T == seg_j) & (run_j.T <= run_j), 0.0, -jnp.inf).astype(bf16)


def layer_kernel(
    tokens_hbm, cot_hbm, qkv_s, out_s, up_s, down_s, gains, biases, up_bias, segment, kinds,
    output_hbm, grad_hbm, sums,
    tok, cot, w_qkv, w_out, w_up, w_down, gb, upb, mask,
    normed, packed, att, mix, hid, gpre, gbr, gmix, acc, acc_up, acc_q,
    grad_stage,
    p_down0, p_down1, p_up0, p_up1, p_out, p_qkv, p_small,
    core0, core1, core2, core3, core4, core5, cross0, cross1, cross2, cross3, cross4, cross5,
    sets0, sets1, sets2, sets3, sets4, sets5, line0, line1, line2, line3, line4, line5,
    small_tiles, small_lines, small_line, small_sets,
    g_send, g_recv, g_local, s_send, s_recv, io_sem, out_sem,
):
    T = tok.shape[0]
    ROWS = T // SEQ
    BM = 256
    count = T // BM
    BACK = grad_stage.shape[1]
    back_count = T // BACK
    me = Place()
    load_tok = pltpu.make_async_copy(tokens_hbm, tok, io_sem.at[0])
    load_cot = pltpu.make_async_copy(cot_hbm, cot, io_sem.at[1])
    load_tok.start()
    load_cot.start()

    def columns(h, width=256):
        return pl.ds(pl.multiple_of(h * width, width), width)

    def qkv_view(c):
        return lambda z, p, h: w_qkv.at[c, :, z, p, :, columns(h, LANES)]

    def up_view(half):
        return lambda z, p, h: w_up.at[z, p, h, :, pl.ds(1024 * half, 1024)]

    def down_view(half):
        return lambda z, p, h: w_down.at[z, p, h, pl.ds(32 * half, 32)]

    views = [
        (qkv_s.at[:, :, pl.ds(0, LANES)], qkv_view(0)),
        (qkv_s.at[:, :, pl.ds(LANES, LANES)], qkv_view(1)),
        (out_s, lambda z, p, h: w_out.at[z, p, :, columns(h)]),
        (up_s.at[:, pl.ds(0, 1024)], up_view(0)),
        (up_s.at[:, pl.ds(1024, 1024)], up_view(1)),
        (down_s.at[pl.ds(0, 32)], down_view(0)),
        (down_s.at[pl.ds(32, 32)], down_view(1)),
    ]
    gathers = [
        (DirectGather if i < 2 else PlaneGather if i == 6 else Gather)(me, shard, view, g_send.at[i], g_recv.at[i], g_local.at[i])
        for i, (shard, view) in enumerate(views)
    ]
    qkv_a, qkv_b, out_g, up_a, up_b, down_a, down_b = gathers
    small = SmallGather(me, small_tiles, small_lines, g_send.at[7], g_recv.at[7])
    small.first(gains, biases, up_bias)
    barrier(me)
    small.second()
    qkv_a.first()
    own_rows = pl.ds(pl.multiple_of(me.h * ROWS, ROWS), ROWS)
    hidden_masks(segment[own_rows, :], kinds[own_rows, :], mask)
    qkv_a.relay(1)
    small.third()
    qkv_a.relay(2)
    qkv_a.relay(3)
    qkv_b.first()
    down_b.first()
    out_g.first()
    up_a.first()
    qkv_a.own_across()
    small.fourth(gb, upb)
    load_tok.wait()

    def norm_one(i, carry):
        r = block(i, 256)
        xhat, _ = normalized(tok[r, :].astype(f32))
        normed[r, :] = (xhat * gb[0:1, :] + gb[2:3, :]).astype(bf16)
        return carry

    lax.fori_loop(0, T // 256, norm_one, 0)
    for n in range(2):
        qkv_a.other_across(n)
    for k in (1, 2, 3):
        qkv_b.relay(k)
    qkv_a.other_across(2)
    qkv_b.own_across()
    up_b.first()
    down_a.first()
    qkv_a.fifth()

    def at_step(i, steps):
        for n, actions in steps.items():

            @pl.when(i == n)
            def _():
                for action in actions:
                    action()

    blocks = T // 512

    def project(i):
        c, r = i // blocks, block(lax.rem(i, blocks), 512)
        x = normed[r, :]
        values = []
        for s in range(3):
            value = dot(x, w_qkv[c, s].reshape(D, 256))
            if s != 1:
                row = 3 + s // 2
                value = value + jnp.concatenate(
                    [gb[row : row + 1, columns(c, LANES)], gb[row : row + 1, columns(2 + c, LANES)]], axis=1
                )
            value = value.astype(bf16)
            values.append(value * jnp.asarray(0.125, bf16) if s == 0 else value)
        return values

    def keep(i, projected):
        c, r = i // blocks, block(lax.rem(i, blocks), 512)
        for n in range(2):
            for s, value in enumerate(projected):
                packed[s, 2 * n + c, r, :] = value[:, LANES * n : LANES * n + LANES]

    start = me.z * 0
    keep(start, project(start))

    def attend(i, carry):
        c, b = i // blocks, lax.rem(i, blocks)
        items = [(4 * b + u, 2 * n + c) for u in range(4) for n in range(2)]
        scores = [
            dot(two_heads(packed[1, p, block(r, SEQ), :]), packed[0, p, block(r, SEQ), :], NT) for r, p in items
        ]
        values = [two_heads(packed[2, p, block(r, SEQ), :]) for r, p in items]
        following = jnp.minimum(i + 1, 2 * blocks - 1)
        projected = project(following)
        weights = []
        for (r, p), pair in zip(items, scores):
            heads = []
            for h in range(2):
                t = pair[SEQ * h : SEQ * h + SEQ] + mask[r].astype(f32)
                e = jnp.exp(t - jnp.max(t, axis=0, keepdims=True))
                a = (e * (1.0 / jnp.sum(e, axis=0, keepdims=True))).astype(bf16)
                att[r, 2 * p + h] = a
                heads.append(a)
            weights.append(jnp.concatenate(heads, axis=0))
        for (r, p), pair, value in zip(items, weights, values):
            mix[p, block(r, SEQ), :] = dot(pair, value, TN).astype(bf16)
        keep(following, projected)
        at_step(
            i,
            {
                0: [lambda: qkv_b.other_across(0), lambda: qkv_b.other_across(1), out_g.second, up_a.second],
                1: [lambda: qkv_b.other_across(2)],
                2: [qkv_b.fifth, up_b.second, down_b.second],
                3: [out_g.third],
                5: [up_a.third],
                6: [out_g.fourth],
                7: [up_b.third, down_a.second],
            },
        )
        return carry

    lax.fori_loop(0, 2 * blocks, attend, 0)
    out_g.fifth()

    def middle_of(r):
        return tok[r, :].astype(f32) + dot(tiles(mix, r), w_out[...].reshape(D, D), NT) + gb[5:6, :]

    def norm_two(i, carry):
        r = block(i, 512)
        middle = middle_of(r)
        xhat, _ = normalized(middle)
        tok[r, :] = (xhat * gb[1:2, :] + gb[6:7, :]).astype(bf16)
        middle = middle.astype(bf16)
        for p in range(4):
            gmix[p, r, :] = middle[:, LANES * p : LANES * p + LANES]
        at_step(i, {1: [up_a.fourth]})
        return carry

    lax.fori_loop(0, T // 512, norm_two, 0)
    up_b.fourth()
    up_a.fifth()

    half_count = count // 2

    def up_columns(j):
        return w_up[:, :, :, :, 512 * j : 512 * j + 512].reshape(D, 512)

    def hidden_block(columns_in, steps):
        def body(i, carry):
            r = block(i, BM)
            two = tok[r, :]
            for j in columns_in:
                cols = slice(512 * j, 512 * j + 512)
                hidden, slope = gelu_and_slope(dot(two, up_columns(j)) + upb[:, cols])
                hid[r, cols] = hidden.astype(bf16)
                gpre[r, cols] = slope.astype(bf16)
            at_step(i, steps)
            return carry

        return body

    lax.fori_loop(0, half_count, hidden_block((0, 1), {3: [down_a.third]}), 0)
    up_b.fifth()
    lax.fori_loop(0, half_count, hidden_block((2, 3), {3: [down_a.fourth]}), 0)
    down_b.third()
    load_cot.wait()
    down_a.fifth()
    down_b.fifth()
    acc[...] = jnp.zeros_like(acc)
    acc_up[...] = jnp.zeros_like(acc_up)
    acc_q[...] = jnp.zeros_like(acc_q)

    def branch_back(r, e, c):
        xhat, rstd = normalized(tiles(gmix, r).astype(f32))
        cot_f32 = c.astype(f32)
        branch = (cot_f32 + norm_back(e, xhat, rstd, gb[1:2, :])).astype(bf16)
        gbr[r, :] = branch
        grad_mix = dot(branch, w_out[...].reshape(D, D)).astype(bf16)
        for p in range(4):
            gmix[p, r, :] = grad_mix[:, LANES * p : LANES * p + LANES]
        acc[1] += column_sums(e * xhat)
        acc[6] += column_sums(e)
        acc[5] += column_sums(branch.astype(f32))
        acc[7] += column_sums(cot_f32)

    def hidden_back(i, carry):
        ra, rb = block(i, BM), block(i + half_count, BM)
        ca, cb, two = cot[ra, :], cot[rb, :], tok[rb, :]
        ea = eb = 0.0
        for j in range(4):
            cols = slice(512 * j, 512 * j + 512)
            w_up_j, w_down_j = up_columns(j), w_down[j].reshape(512, D)
            hidden, slope = gelu_and_slope(dot(two, w_up_j) + upb[:, cols])
            hid[rb, cols] = hidden.astype(bf16)
            pre_a = dot(ca, w_down_j, NT) * gpre[ra, cols].astype(f32)
            pre_b = dot(cb, w_down_j, NT) * slope
            acc_up[:, cols] += column_sums(pre_a) + column_sums(pre_b)
            pre_a, pre_b = pre_a.astype(bf16), pre_b.astype(bf16)
            gpre[ra, cols] = pre_a
            gpre[rb, cols] = pre_b
            ea = ea + dot(pre_a, w_up_j, NT)
            eb = eb + dot(pre_b, w_up_j, NT)
        branch_back(ra, ea, ca)
        branch_back(rb, eb, cb)
        return carry

    lax.fori_loop(0, half_count, hidden_back, 0)

    units = [
        Scatter(me, *refs, s_send.at[i], s_recv.at[i])
        for i, refs in enumerate(
            (
                (p_down0, core0, cross0, sets0, line0),
                (p_down1, core1, cross1, sets1, line1),
                (p_up0, core2, cross2, sets2, line2),
                (p_up1, core3, cross3, sets3, line3),
                (p_out, core4, cross4, sets4, line4),
                (p_qkv, core5, cross5, sets5, line5),
            )
        )
    ]
    d0, d1, u0, u1, out_u, qkv_u = units

    def grad_down_chunk(z, carry):
        o = dot(cot[...], hid[:, block(z, 512)], TN).astype(bf16).T
        for half, part in enumerate((p_down0, p_down1)):
            for p in range(GRID_P):
                for h in range(2):
                    for j in range(2):
                        part[h, z, p, 64 * j : 64 * j + 64] = o[
                            64 * (2 * p + h) : 64 * (2 * p + h) + 64,
                            256 * half + LANES * j : 256 * half + LANES * j + LANES,
                        ]
        return carry

    def grad_up_chunk(half, part):
        def body(c, carry):
            o = dot(tok[...], gpre[:, block(2 * half + c, 512)], TN).astype(bf16)
            for z in range(GRID_Z):
                for p in range(GRID_P):
                    for h in range(2):
                        d = (z * 4 + p) * 2 + h
                        for j in range(4):
                            part[h, z, p, pl.ds(pl.multiple_of(64 * c + 16 * j, 16), 16)] = o[
                                16 * d : 16 * d + 16, LANES * j : LANES * j + LANES
                            ]
            return carry

        return body

    o = dot(gbr[...], jnp.concatenate([mix[p] for p in range(4)], axis=1), TN).astype(bf16)
    for z in range(GRID_Z):
        for p in range(GRID_P):
            d = z * 4 + p
            for h in range(2):
                for j in range(2):
                    p_out[h, z, p, 32 * j : 32 * j + 32] = o[
                        32 * d : 32 * d + 32, 256 * h + LANES * j : 256 * h + LANES * j + LANES
                    ]
    out_u.first()
    lax.fori_loop(0, 4, grad_down_chunk, 0)
    out_u.second()
    d0.first()
    d1.first()
    lax.fori_loop(0, 2, grad_up_chunk(0, p_up0), 0)
    d0.second()
    u0.first()
    d1.second()
    lax.fori_loop(0, 2, grad_up_chunk(1, p_up1), 0)
    u1.first()
    out_u.third()
    load_tok = pltpu.make_async_copy(tokens_hbm, tok, io_sem.at[0])
    load_tok.start()
    u0.second()
    d0.third()

    u1.second()
    d1.third()

    def attend_back(half, steps):
        def body(i, carry):
            row = lax.broadcasted_iota(jnp.int32, (2 * SEQ, LANES), 0) // SEQ
            lane = lax.broadcasted_iota(jnp.int32, (2 * SEQ, LANES), 1) // 64
            minus = jnp.where(row == lane, -1.0, 0.0).astype(bf16)
            items = [(4 * i + u, 2 * half + pp) for u in range(4) for pp in range(2)]
            grads, slopes = [], []
            for r, p in items:
                rows = block(r, SEQ)
                grad = gmix[p, rows, :]
                product = (grad.astype(f32) * mix[p, rows, :].astype(f32)).astype(bf16)
                values = jnp.concatenate([two_heads(packed[2, p, rows, :]), minus], axis=1)
                grads.append(dot(values, jnp.concatenate([grad, product], axis=1), NT))
            for (r, p), pair in zip(items, grads):
                slopes.append(
                    [
                        (att[r, 2 * p + h].astype(f32) * pair[SEQ * h : SEQ * h + SEQ]).astype(bf16)
                        for h in range(2)
                    ]
                )
            results, sums = [], [0.0] * 4
            for n, ((r, p), pair) in enumerate(zip(items, slopes)):
                rows = block(r, SEQ)
                queries, keys = two_heads(packed[0, p, rows, :]), two_heads(packed[1, p, rows, :])
                g_q = dot(jnp.concatenate(pair, axis=0), keys, TN) * 0.125
                g_k = dot(jnp.concatenate(pair, axis=1), queries)
                weights = jnp.concatenate([att[r, 2 * p], att[r, 2 * p + 1]], axis=1)
                g_v = dot(weights, two_heads(gmix[p, rows, :]))
                sums[n % 2] = sums[n % 2] + column_sums(g_q)
                sums[2 + n % 2] = sums[2 + n % 2] + column_sums(g_v)
                results.append((g_q.astype(bf16), g_k.astype(bf16), g_v.astype(bf16)))
            for (r, p), result in zip(items, results):
                for n in range(3):
                    packed[n, p, block(r, SEQ), :] = result[n]
            for pp in range(2):
                acc_q[0, 2 * half + pp] += sums[pp]
                acc_q[1, 2 * half + pp] += sums[2 + pp]
            at_step(i, steps)
            return carry

        return body

    def grad_qkv_half(half):
        def body(s, carry):
            wide = jnp.concatenate([packed[s, 2 * half], packed[s, 2 * half + 1]], axis=1)
            o = dot(normed[...], wide, TN).astype(bf16)
            for z in range(GRID_Z):
                for p in range(GRID_P):
                    d = z * 4 + p
                    for j in range(2):
                        p_qkv[half, z, p, pl.ds(pl.multiple_of(64 * s + 32 * j, 32), 32)] = o[
                            32 * d : 32 * d + 32, LANES * j : LANES * j + LANES
                        ]
            return carry

        return body

    lax.fori_loop(0, ROWS // 4, attend_back(me.sib, {1: [out_u.fourth], 2: [u0.third]}), 0)
    lax.fori_loop(0, 3, grad_qkv_half(me.sib), 0)
    qkv_u.first()
    d0.fourth()
    u1.third()
    lax.fori_loop(0, ROWS // 4, attend_back(me.h, {3: [d1.fourth]}), 0)
    lax.fori_loop(0, 3, grad_qkv_half(me.h), 0)
    qkv_u.second()
    u0.fourth()
    load_tok.wait()

    def grad_copy(i):
        return pltpu.make_async_copy(
            grad_stage.at[parity(i)], grad_hbm.at[block(i, BACK), :], out_sem.at[parity(i)]
        )

    def norm_one_back(i, carry):
        r = block(i, BACK)

        @pl.when(i >= 2)
        def _():
            grad_copy(i - 2).wait()

        e = 0.0
        for c in range(2):
            for s in range(3):
                pair = jnp.concatenate([packed[s, c, r, :], packed[s, 2 + c, r, :]], axis=1)
                e = e + dot(pair, w_qkv[c, s].reshape(D, 256), NT)
        xhat, rstd = normalized(tok[r, :].astype(f32))
        grad_stage[parity(i)] = gbr[r, :].astype(f32) + norm_back(e, xhat, rstd, gb[0:1, :])
        grad_copy(i).start()
        acc[0] += column_sums(e * xhat)
        acc[2] += column_sums(e)
        at_step(i, {3: [u1.fourth], 6: [qkv_u.third]})
        return carry

    lax.fori_loop(0, back_count, norm_one_back, 0)
    for p in range(4):
        acc[3, :, LANES * p : LANES * p + LANES] = acc_q[0, p]
        acc[4, :, LANES * p : LANES * p + LANES] = acc_q[1, p]
    for z in range(GRID_Z):
        rows = [jnp.sum(acc[n, :, LANES * z : LANES * z + LANES], axis=0, keepdims=True) for n in range(8)]
        rows += [
            jnp.sum(acc_up[:, 512 * z + LANES * p : 512 * z + LANES * p + LANES], axis=0, keepdims=True)
            for p in range(GRID_P)
        ]
        rows += [jnp.zeros((4, LANES), f32)]
        p_small[z] = jnp.concatenate(rows, axis=0)
    small_sum = SmallScatter(me, p_small, small_line, small_sets, s_send.at[6], s_recv.at[6])
    small_sum.first()

    def out_copies(i):
        r = block(i, 512)
        return [
            pltpu.make_async_copy(
                gmix.at[p, r], output_hbm.at[r, pl.ds(LANES * p, LANES)], out_sem.at[2]
            )
            for p in range(4)
        ]

    def output_block(i, carry):
        r = block(i, 512)
        total = middle_of(r) + dot(hid[r, :], w_down[...].reshape(2048, D)) + gb[7:8, :]
        total = total.astype(bf16)
        for p in range(4):
            gmix[p, r, :] = total[:, LANES * p : LANES * p + LANES]
        for copy in out_copies(i):
            copy.start()
        at_step(i, {2: [small_sum.second], 3: [qkv_u.fourth]})
        return carry

    lax.fori_loop(0, T // 512, output_block, 0)
    for unit, rows in ((out_u, OUT_ROWS), (d0, DOWN_ROWS), (d1, DOWN_ROWS + 128), (u0, UP_ROWS), (u1, UP_ROWS + 128)):
        total = unit.fifth()
        sums[rows : rows + total.shape[0]] = total
    small_sum.third(sums)
    sums[QKV_ROWS : QKV_ROWS + 192] = qkv_u.fifth()
    for i in range(T // 512):
        for copy in out_copies(i):
            copy.wait()
    for i in (back_count - 2, back_count - 1):
        grad_copy(i).wait()
    for item in gathers + units + [small, small_sum]:
        item.close()


def finish_kernel(output, grad, sums_hbm, *refs):
    targets, stages, sums, sems = refs[:9], refs[9:18], refs[18], refs[19]
    loads, stores = [], []
    load_sums = pltpu.make_async_copy(sums_hbm, sums, sems.at[0, 0, 4])
    load_sums.start()
    for n in range(4):
        for a, source in ((1, grad), (0, output)):
            size = source.shape[0] // 4
            rows = pl.ds(n * size, size)
            loads.append(pltpu.make_async_copy(source.at[rows], stages[a].at[rows], sems.at[0, a, n]))
            stores.append(pltpu.make_async_copy(stages[a].at[rows], targets[a].at[rows], sems.at[1, a, n]))
    for load in loads:
        load.start()
    g_qkv, g_out, g_up, g_down, g_gains, g_biases, g_up_bias = stages[2:]
    load_sums.wait()

    def tile(start, rows, j):
        return sums[start + rows * j : start + rows * (j + 1)]

    for j in range(4):
        g_down[:, LANES * j : LANES * j + LANES] = tile(DOWN_ROWS, 64, j)
    for j in range(16):
        g_up[:, LANES * j : LANES * j + LANES] = tile(UP_ROWS, 16, j)
    for j in range(2):
        g_out[:, LANES * j : LANES * j + LANES] = tile(OUT_ROWS, 32, j)
        for s in range(3):
            g_qkv[s, :, LANES * j : LANES * j + LANES] = tile(QKV_ROWS + 64 * s, 32, j)
    g_gains[...] = sums[SMALL_ROWS : SMALL_ROWS + 2, 0:16]
    g_biases[...] = sums[SMALL_ROWS + 2 : SMALL_ROWS + 8, 0:16]
    g_up_bias[...] = sums[SMALL_ROWS + 8 : SMALL_ROWS + 9, 0:64]
    for n in range(2, 9):
        stores.append(pltpu.make_async_copy(stages[n], targets[n], sems.at[2, n // 5, n % 5]))
        stores[-1].start()
    for load, store in zip(loads, stores):
        load.wait()
        store.start()
    for store in stores:
        store.wait()


def finish(output, grad, sums):
    shape = jax.ShapeDtypeStruct
    outs = (
        shape(output.shape, bf16),
        shape(grad.shape, f32),
        shape((3, 32, 256), f32),
        shape((32, 256), f32),
        shape((16, 2048), f32),
        shape((64, 512), f32),
        shape((2, 16), f32),
        shape((6, 16), f32),
        shape((1, 64), f32),
    )
    return pl.pallas_call(
        finish_kernel,
        out_shape=outs,
        in_specs=[ANY] * 3,
        out_specs=[ANY] * 9,
        scratch_shapes=[pltpu.VMEM(o.shape, o.dtype) for o in outs]
        + [pltpu.VMEM(sums.shape, f32), pltpu.SemaphoreType.DMA((3, 2, 5))],
        compiler_params=pltpu.CompilerParams(vmem_limit_bytes=VMEM_LIMIT),
        name="finish",
    )(output, grad, sums)


def layer(tokens, cotangent, qkv, out, up, down, gains, biases, up_bias, segment, kinds):
    shape = jax.ShapeDtypeStruct
    T = tokens.shape[0]
    rows = T // SEQ
    outs = (shape((T, D), bf16), shape((T, D), f32), shape((ALL_ROWS, LANES), f32))
    sizes = [128, 128, 128, 128, 64, 192]
    V, S = pltpu.VMEM, pltpu.SemaphoreType.DMA
    scratch = [
        V((T, D), bf16), V((T, D), bf16),
        V((2, 3, 4, 4, 32, 256), bf16), V((4, 4, 32, 512), bf16),
        V((4, 4, 2, 16, 2048), bf16), V((4, 4, 2, 64, 512), bf16),
        V((8, 512), f32), V((1, 2048), f32), V((rows, SEQ, SEQ), bf16),
        V((T, D), bf16), V((3, 4, T, LANES), bf16), V((rows, 8, SEQ, SEQ), bf16),
        V((4, T, LANES), bf16), V((T, 2048), bf16), V((T, 2048), bf16),
        V((T, D), bf16), V((4, T, LANES), bf16), V((8, 8, 512), f32), V((8, 2048), f32),
        V((2, 4, 8, LANES), f32),
        V((2, 256, D), f32),
    ]
    scratch += [V((2, 4, 4, r, LANES), bf16) for r in sizes] + [V((4, 16, LANES), f32)]
    scratch += [V((4, 4, r, LANES), bf16) for r in sizes]
    scratch += [V((2, 2, r, LANES), bf16) for r in sizes]
    scratch += [V((2, 4, r, LANES), bf16) for r in sizes]
    scratch += [V((3, r, LANES), bf16) for r in sizes]
    scratch += [V((4, 2, 16, LANES), bf16), V((4, 16, LANES), bf16), V((3, 16, LANES), f32), V((8, 16, LANES), f32)]
    scratch += [S((8, 19)), S((8, 19)), S((7,)), S((7, 10)), S((7, 10)), S((2,)), S((3,))]
    return pl.pallas_call(
        layer_kernel,
        out_shape=outs,
        in_specs=[ANY] * 6 + [VM] * 5,
        out_specs=[ANY] * 2 + [VM],
        scratch_shapes=scratch,
        compiler_params=pltpu.CompilerParams(
            collective_id=0, has_side_effects=True, vmem_limit_bytes=VMEM_LIMIT
        ),
        name="layer",
    )(tokens, cotangent, qkv, out, up, down, gains, biases, up_bias, segment, kinds)


def widened(x, axes, dim):
    return lax.all_gather(x, axes, axis=dim, tiled=True)


def on_device(rep):
    def run(
        tokens, qkv, out, up, down, gains, biases, up_bias, segment, kinds, cotangent
    ):
        up_bias = up_bias.reshape(1, -1)
        head = lax.axis_index("head")
        if rep > 1:
            both = ("rep", "head")
            qkv, out = widened(qkv, "rep", 1), widened(out, "rep", 0)
            up = lax.dynamic_slice_in_dim(widened(up, both, 0), head * 16, 16, 0)
            down = lax.dynamic_slice_in_dim(widened(down, both, 0), head * 64, 64, 0)
            gains = lax.dynamic_slice_in_dim(widened(gains, both, 1), head * 16, 16, 1)
            biases = lax.dynamic_slice_in_dim(widened(biases, both, 1), head * 16, 16, 1)
            up_bias = lax.dynamic_slice_in_dim(widened(up_bias, both, 1), head * 64, 64, 1)
        output, grad, *grads = finish(
            *layer(tokens, cotangent, qkv, out, up, down, gains, biases, up_bias, segment, kinds)
        )
        if rep > 1:
            place = lax.axis_index("rep") * 2 + head

            def own(x, dim):
                x = lax.all_gather(lax.psum(x, "rep"), "head", axis=dim, tiled=True)
                size = x.shape[dim] // (2 * rep)
                return lax.dynamic_slice_in_dim(x, place * size, size, dim)

            for i, dim in ((0, 1), (1, 0)):
                grads[i] = lax.psum_scatter(grads[i], "rep", scatter_dimension=dim, tiled=True)
            for i, dim in ((2, 0), (3, 0), (4, 1), (5, 1), (6, 1)):
                grads[i] = own(grads[i], dim)
        grads[6] = grads[6].reshape(-1)
        return (output, grad, *grads)

    return run


def solution(mesh):
    rep = mesh.shape["dp"] // (GRID_Z * GRID_P)
    wide = Mesh(mesh.devices.reshape(GRID_Z * GRID_P, rep, 2), ("dp", "rep", "head"))
    dp, every = ("dp", "rep"), ("dp", "rep", "head")
    in_specs = (
        P(every, None),
        P(None, dp, "head"),
        P(dp, "head"),
        P(every, None),
        P(every, None),
        P(None, every),
        P(None, every),
        P(every),
        P(dp, None),
        P(dp, None),
        P(every, None),
    )
    out_specs = (
        P(every, None),
        P(every, None),
        P(None, dp, "head"),
        P(dp, "head"),
        P(every, None),
        P(every, None),
        P(None, every),
        P(None, every),
        P(every),
    )
    return jax.shard_map(
        on_device(rep), mesh=wide, in_specs=in_specs, out_specs=out_specs, check_vma=False
    )
```

```python
import math

import jax
import jax.numpy as jnp
from jax import lax
from jax.experimental import pallas as pl
from jax.experimental.pallas import tpu as pltpu
from jax.sharding import Mesh
from jax.sharding import PartitionSpec as P

bf16, f32 = jnp.bfloat16, jnp.float32
D = 512
SEQ = 128
LANES = 128
GRID_Z, GRID_P = 4, 4
EPS = 1e-5
MESH = pl.DeviceIdType.MESH
NN = (((1,), (0,)), ((), ()))
NT = (((1,), (1,)), ((), ()))
TN = (((0,), (0,)), ((), ()))
DOWN_ROWS, UP_ROWS, OUT_ROWS, QKV_ROWS, SMALL_ROWS, ALL_ROWS = 0, 256, 512, 576, 768, 784
VMEM_LIMIT = (63 << 20) + (512 << 10)


def dot(a, b, dims=NN):
    return lax.dot_general(a, b, dims, preferred_element_type=f32)


def block(index, size):
    if isinstance(index, int):
        return pl.ds(index * size, size)
    return pl.ds(pl.multiple_of(index * size, size), size)


def parity(index):
    return index % 2 if isinstance(index, int) else lax.rem(index, 2)


class Place:
    def __init__(self):
        dp, self.h = lax.axis_index("dp"), lax.axis_index("head")
        self.z, self.p = dp // GRID_P, lax.rem(dp, GRID_P)
        x, y = lax.rem(self.p, 2), self.p // 2
        self.px = y * 2 + (1 - x)
        self.py = (1 - y) * 2 + x
        self.pd = (1 - y) * 2 + (1 - x)
        self.sib = 1 - self.h

    def at(self, z, p, h):
        return {"dp": z * GRID_P + p, "head": h}

    def line(self, k):
        return lax.rem(self.z + k, GRID_Z)

    def line_back(self, k):
        if k == 0:
            return self.z
        return lax.rem(self.z + (GRID_Z - k), GRID_Z)

    def plane(self):
        places = [(self.px, self.h), (self.py, self.h), (self.pd, self.h)]
        places += [(p, self.sib) for p in (self.p, self.px, self.py, self.pd)]
        return places


def barrier(me):
    sem = pltpu.get_barrier_semaphore()
    for p, h in me.plane():
        pl.semaphore_signal(sem, 1, device_id=me.at(me.z, p, h), device_id_type=MESH)
    for k in (1, 2, 3):
        pl.semaphore_signal(sem, 1, device_id=me.at(me.line(k), me.p, me.h), device_id_type=MESH)
    pl.semaphore_wait(sem, 10)


def remote(src, dst, send, recv, device):
    return pltpu.make_async_remote_copy(
        src_ref=src, dst_ref=dst, send_sem=send, recv_sem=recv, device_id=device, device_id_type=MESH
    )


class Gather:
    SENDS, RECVS = 11, 11

    def __init__(self, me, shard, view, send, recv, local):
        self.me, self.shard, self.view = me, shard, view
        self.send, self.recv, self.local = send, recv, local
        self.started = []

    def go(self, index, parts):
        def make():
            src, dst, device = parts()
            return remote(src, dst, self.send.at[index], self.recv.at[index], device)

        make().start()
        self.started.append(make)

    def landed(self, index, region):
        me = self.me
        remote(region, region, self.send.at[index], self.recv.at[index], me.at(me.z, me.p, me.sib)).wait_recv()

    def set_of(self, z, p):
        return self.view(z, p, self.me.h)

    def first(self):
        me = self.me
        self.mine = pltpu.make_async_copy(self.shard, self.set_of(me.z, me.p), self.local)
        self.mine.start()
        for k in (1, 2, 3):
            self.go(k - 1, lambda k=k: (self.shard, self.set_of(me.z, me.p), me.at(me.line(k), me.p, me.h)))

    def second(self):
        me = self.me
        self.mine.wait()
        for k in (1, 2, 3):
            self.landed(k - 1, self.view(me.line_back(k), me.p, me.h))
        line = lambda: self.set_of(pl.ds(0, 4), me.p)
        self.go(3, lambda: (line(), line(), me.at(me.z, me.px, me.h)))
        self.go(4, lambda: (line(), line(), me.at(me.z, me.py, me.h)))
        self.go(7, lambda: (line(), line(), me.at(me.z, me.p, me.sib)))

    def third(self):
        me = self.me
        from_x, from_y = lambda: self.set_of(pl.ds(0, 4), me.px), lambda: self.set_of(pl.ds(0, 4), me.py)
        half_x, half_y = lambda: self.set_of(pl.ds(0, 2), me.px), lambda: self.set_of(pl.ds(2, 2), me.py)
        self.landed(3, from_x())
        self.go(6, lambda: (half_x(), half_x(), me.at(me.z, me.py, me.h)))
        self.landed(4, from_y())
        self.go(5, lambda: (half_y(), half_y(), me.at(me.z, me.px, me.h)))
        self.go(8, lambda: (from_x(), from_x(), me.at(me.z, me.p, me.sib)))
        self.go(9, lambda: (from_y(), from_y(), me.at(me.z, me.p, me.sib)))

    def fourth(self):
        me = self.me
        self.landed(6, self.view(pl.ds(0, 2), me.pd, me.h))
        self.landed(5, self.view(pl.ds(2, 2), me.pd, me.h))
        diagonal = lambda: self.set_of(pl.ds(0, 4), me.pd)
        self.go(10, lambda: (diagonal(), diagonal(), me.at(me.z, me.p, me.sib)))

    def fifth(self):
        me = self.me
        for index, p in ((7, me.p), (8, me.px), (9, me.py), (10, me.pd)):
            self.landed(index, self.view(pl.ds(0, 4), p, me.sib))

    def close(self):
        for make in self.started:
            make().wait_send()


class DirectGather(Gather):
    def others(self):
        return self.me.px, self.me.py, self.me.pd

    def first(self):
        me = self.me
        own = lambda: self.set_of(me.z, me.p)
        self.mine = pltpu.make_async_copy(self.shard, own(), self.local)
        self.mine.start()
        for k in (1, 2, 3):
            self.go(k - 1, lambda k=k: (self.shard, own(), me.at(me.line(k), me.p, me.h)))
        for n, p in enumerate(self.others()):
            self.go(3 + 4 * n, lambda p=p: (self.shard, own(), me.at(me.z, p, me.h)))

    def relay(self, k):
        me = self.me
        piece = lambda: self.set_of(me.line_back(k), me.p)
        self.landed(k - 1, piece())
        for n, p in enumerate(self.others()):
            self.go(3 + 4 * n + k, lambda p=p: (piece(), piece(), me.at(me.z, p, me.h)))

    def across(self, index, p):
        me = self.me
        group = lambda: self.set_of(pl.ds(0, 4), p)
        self.go(index, lambda: (group(), group(), me.at(me.z, me.p, me.sib)))

    def own_across(self):
        self.mine.wait()
        self.across(15, self.me.p)

    def other_across(self, n):
        me = self.me
        p = self.others()[n]
        for k in range(4):
            self.landed(3 + 4 * n + k, self.set_of(me.line_back(k), p))
        self.across(16 + n, p)

    def fifth(self):
        me = self.me
        for index, p in ((15, me.p), (16, me.px), (17, me.py), (18, me.pd)):
            self.landed(index, self.view(pl.ds(0, 4), p, me.sib))


class PlaneGather(Gather):
    def group(self, z):
        return self.view(z, pl.ds(0, 4), self.me.h)

    def first(self):
        me = self.me
        own = lambda: self.set_of(me.z, me.p)
        self.mine = pltpu.make_async_copy(self.shard, own(), self.local)
        self.mine.start()
        for n, p in enumerate((me.px, me.py, me.pd)):
            self.go(n, lambda p=p: (self.shard, own(), me.at(me.z, p, me.h)))

    def second(self):
        me = self.me
        self.mine.wait()
        for n, p in enumerate((me.px, me.py, me.pd)):
            self.landed(n, self.set_of(me.z, p))
        for k in (1, 2, 3):
            self.go(2 + k, lambda k=k: (self.group(me.z), self.group(me.z), me.at(me.line(k), me.p, me.h)))
        self.go(6, lambda: (self.group(me.z), self.group(me.z), me.at(me.z, me.p, me.sib)))

    def third(self):
        me = self.me
        for k in (1, 2, 3):
            z = me.line_back(k)
            self.landed(2 + k, self.group(z))
            self.go(6 + k, lambda z=z: (self.group(z), self.group(z), me.at(me.z, me.p, me.sib)))

    def fourth(self):
        pass

    def fifth(self):
        me = self.me
        for k in range(4):
            self.landed(6 + k, self.view(me.line_back(k), pl.ds(0, 4), me.sib))


class SmallGather:
    def __init__(self, me, tiles, lines, send, recv):
        self.me, self.tiles, self.lines, self.send, self.recv = me, tiles, lines, send, recv
        self.started = []

    def go(self, index, parts):
        def make():
            region, device = parts()
            return remote(region, region, self.send.at[index], self.recv.at[index], device)

        make().start()
        self.started.append(make)

    def landed(self, index, region):
        me = self.me
        remote(region, region, self.send.at[index], self.recv.at[index], me.at(me.z, me.p, me.sib)).wait_recv()

    def first(self, gains, biases, up_bias):
        me = self.me
        place = lambda rows, width, start: dot(
            rows,
            jnp.where(
                lax.broadcasted_iota(jnp.int32, (width, LANES), 1)
                == lax.broadcasted_iota(jnp.int32, (width, LANES), 0) + start,
                1.0,
                0.0,
            ).astype(bf16),
        )
        start = (me.p * 2 + me.h) * 16
        row = lax.broadcasted_iota(jnp.int32, (8, LANES), 0)
        hidden = jnp.broadcast_to(place(up_bias[...], 64, me.h * 64), (8, LANES))
        rows = jnp.concatenate(
            [
                place(gains[...], 16, start),
                place(biases[...], 16, start),
                jnp.where(row == me.p, hidden, 0.0),
            ],
            axis=0,
        )
        self.tiles[me.p, me.h] = rows.astype(bf16)

    def second(self):
        me = self.me
        for index, (p, h) in enumerate(me.plane()):
            self.go(index, lambda p=p, h=h: (self.tiles.at[me.p, me.h], me.at(me.z, p, h)))

    def third(self):
        me = self.me
        for index, (p, h) in enumerate(me.plane()):
            self.landed(index, self.tiles.at[p, h])
        total = jnp.zeros((16, LANES), f32)
        for p in range(GRID_P):
            for h in range(2):
                total = total + self.tiles[p, h].astype(f32)
        self.lines[me.z] = total.astype(bf16)
        for k in (1, 2, 3):
            self.go(6 + k, lambda k=k: (self.lines.at[me.z], me.at(me.line(k), me.p, me.h)))

    def fourth(self, gain_bias, up_bias):
        me = self.me
        for k in (1, 2, 3):
            self.landed(6 + k, self.lines.at[me.line_back(k)])
        for z in range(GRID_Z):
            line = self.lines[z].astype(f32)
            gain_bias[:, z * LANES : (z + 1) * LANES] = line[:8]
            for p in range(GRID_P):
                up_bias[:, (z * GRID_P + p) * LANES : (z * GRID_P + p + 1) * LANES] = line[8 + p : 9 + p]

    def close(self):
        for make in self.started:
            make().wait_send()


class Scatter:
    SENDS, RECVS = 8, 8

    def __init__(self, me, part, core, cross, sets, line, send, recv):
        self.me, self.part, self.core, self.cross, self.sets, self.line = me, part, core, cross, sets, line
        self.send, self.recv = send, recv
        self.started = []

    def go(self, index, parts):
        def make():
            src, dst, device = parts()
            return remote(src, dst, self.send.at[index], self.recv.at[index], device)

        make().start()
        self.started.append(make)

    def landed(self, index, region):
        me = self.me
        remote(region, region, self.send.at[index], self.recv.at[index], me.at(me.z, me.p, me.sib)).wait_recv()

    def first(self):
        me = self.me
        self.go(0, lambda: (self.part.at[me.sib], self.core, me.at(me.z, me.p, me.sib)))

    def second(self):
        me, part = self.me, self.part
        self.landed(0, self.core)
        part[me.h] = part[me.h] + self.core[...]
        self.go(1, lambda: (part.at[me.h, pl.ds(0, 2), me.pd], self.cross.at[0], me.at(me.z, me.py, me.h)))
        self.go(2, lambda: (part.at[me.h, pl.ds(2, 2), me.pd], self.cross.at[1], me.at(me.z, me.px, me.h)))

    def third(self):
        me, part = self.me, self.part
        self.landed(1, self.cross.at[0])
        self.landed(2, self.cross.at[1])

        for i in range(2):
            part[me.h, i, me.px] = part[me.h, i, me.px] + self.cross[0, i]
            part[me.h, 2 + i, me.py] = part[me.h, 2 + i, me.py] + self.cross[1, i]
        self.go(3, lambda: (part.at[me.h, :, me.px], self.sets.at[0], me.at(me.z, me.px, me.h)))
        self.go(4, lambda: (part.at[me.h, :, me.py], self.sets.at[1], me.at(me.z, me.py, me.h)))

    def fourth(self):
        me, part = self.me, self.part
        self.landed(3, self.sets.at[0])
        self.landed(4, self.sets.at[1])
        for i in range(GRID_Z):
            part[me.h, i, me.p] = (
                part[me.h, i, me.p].astype(f32) + self.sets[0, i].astype(f32) + self.sets[1, i].astype(f32)
            ).astype(bf16)
        for k in (1, 2, 3):
            self.go(
                4 + k,
                lambda k=k: (
                    part.at[me.h, me.line(k), me.p], self.line.at[k - 1], me.at(me.line(k), me.p, me.h)
                ),
            )

    def fifth(self):
        me = self.me
        total = self.part[me.h, me.z, me.p].astype(f32)
        for k in (1, 2, 3):
            self.landed(4 + k, self.line.at[k - 1])
            total = total + self.line[k - 1].astype(f32)
        return total

    def close(self):
        for make in self.started:
            make().wait_send()


class SmallScatter:
    SENDS, RECVS = 10, 10

    def __init__(self, me, part, line, sets, send, recv):
        self.me, self.part, self.line, self.sets = me, part, line, sets
        self.send, self.recv = send, recv
        self.started = []

    def go(self, index, parts):
        def make():
            src, dst, device = parts()
            return remote(src, dst, self.send.at[index], self.recv.at[index], device)

        make().start()
        self.started.append(make)

    def landed(self, index, region):
        me = self.me
        remote(region, region, self.send.at[index], self.recv.at[index], me.at(me.z, me.p, me.sib)).wait_recv()

    def first(self):
        me = self.me
        for k in (1, 2, 3):
            self.go(
                k - 1,
                lambda k=k: (self.part.at[me.line(k)], self.line.at[k - 1], me.at(me.line(k), me.p, me.h)),
            )

    def second(self):
        me = self.me
        total = self.part[me.z]
        for k in (1, 2, 3):
            self.landed(k - 1, self.line.at[k - 1])
            total = total + self.line[k - 1]
        self.sets[7] = total
        for index, (p, h) in enumerate(me.plane()):
            self.go(
                3 + index, lambda i=index, p=p, h=h: (self.sets.at[7], self.sets.at[i], me.at(me.z, p, h))
            )

    def third(self, sums):
        me = self.me
        total = self.sets[7]
        for index in range(7):
            self.landed(3 + index, self.sets.at[index])
            total = total + self.sets[index]
        sums[SMALL_ROWS : SMALL_ROWS + 8] = pltpu.roll(total[:8], LANES - 16 * (me.p * 2 + me.h), 1)
        row = lax.broadcasted_iota(jnp.int32, (8, LANES), 0)
        hidden = jnp.sum(jnp.where(row == me.p, total[8:], 0.0), axis=0, keepdims=True)
        hidden = jnp.broadcast_to(hidden, (8, LANES))
        sums[SMALL_ROWS + 8 : SMALL_ROWS + 16] = jnp.where(me.h == 0, hidden, pltpu.roll(hidden, 64, 1))

    def close(self):
        for make in self.started:
            make().wait_send()


ANY = pl.BlockSpec(memory_space=pl.ANY)
VM = pl.BlockSpec(memory_space=pltpu.VMEM)


def normalized(x):
    center = x - jnp.mean(x, axis=-1, keepdims=True)
    rstd = lax.rsqrt(jnp.mean(center * center, axis=-1, keepdims=True) + EPS)
    return center * rstd, rstd


def norm_back(e, xhat, rstd, gain):
    u = e * gain
    return rstd * (
        u - jnp.mean(u, axis=-1, keepdims=True) - xhat * jnp.mean(u * xhat, axis=-1, keepdims=True)
    )


def column_sums(x):
    return jnp.sum(x.reshape(x.shape[0] // 8, 8, x.shape[1]), axis=0)


def gelu_and_slope(u):
    phi = 0.5 + 0.5 * lax.erf(u * math.sqrt(0.5))
    return u * phi, phi + u * (jnp.exp(u * u * -0.5) * (1 / math.sqrt(2 * math.pi)))


def two_heads(x):
    first = lax.broadcasted_iota(jnp.int32, x.shape, 1) < 64
    zero = jnp.zeros_like(x)
    return jnp.concatenate([jnp.where(first, x, zero), jnp.where(first, zero, x)], axis=0)


def tiles(ref, rows):
    return jnp.concatenate([ref[p, rows] for p in range(4)], axis=1)


def hidden_masks(segment, kinds, mask):
    s, k = segment, kinds
    position = lax.broadcasted_iota(jnp.int32, s.shape, 1)
    follows = (s == pltpu.roll(s, 1, 1)) & (k == 2) & (pltpu.roll(k, 1, 1) == 2) & (position > 0)
    upper = lax.broadcasted_iota(jnp.int32, (SEQ, SEQ), 0) <= lax.broadcasted_iota(jnp.int32, (SEQ, SEQ), 1)
    run = dot(jnp.where(follows, 0.0, 1.0).astype(bf16), jnp.where(upper, 1.0, 0.0).astype(bf16))
    seg = s.astype(f32)
    for r in range(s.shape[0]):
        seg_j = jnp.broadcast_to(seg[r : r + 1], (SEQ, SEQ))
        run_j = jnp.broadcast_to(run[r : r + 1], (SEQ, SEQ))
        mask[r] = jnp.where((seg_j.T == seg_j) & (run_j.T <= run_j), 0.0, -jnp.inf).astype(bf16)


def layer_kernel(
    tokens_hbm, cot_hbm, qkv_s, out_s, up_s, down_s, gains, biases, up_bias, segment, kinds,
    output_hbm, grad_hbm, sums,
    tok, cot, w_qkv, w_out, w_up, w_down, gb, upb, mask,
    normed, packed, att, mix, hid, gpre, gbr, gmix, acc, acc_up, acc_q,
    grad_stage,
    p_down0, p_down1, p_up0, p_up1, p_out, p_qkv, p_small,
    core0, core1, core2, core3, core4, core5, cross0, cross1, cross2, cross3, cross4, cross5,
    sets0, sets1, sets2, sets3, sets4, sets5, line0, line1, line2, line3, line4, line5,
    small_tiles, small_lines, small_line, small_sets,
    g_send, g_recv, g_local, s_send, s_recv, io_sem, out_sem,
):
    T = tok.shape[0]
    ROWS = T // SEQ
    BM = 256
    count = T // BM
    BACK = grad_stage.shape[1]
    back_count = T // BACK
    me = Place()
    load_tok = pltpu.make_async_copy(tokens_hbm, tok, io_sem.at[0])
    load_cot = pltpu.make_async_copy(cot_hbm, cot, io_sem.at[1])
    load_tok.start()
    load_cot.start()

    def columns(h, width=256):
        return pl.ds(pl.multiple_of(h * width, width), width)

    def qkv_view(c):
        return lambda z, p, h: w_qkv.at[c, :, z, p, :, columns(h, LANES)]

    def up_view(half):
        return lambda z, p, h: w_up.at[z, p, h, :, pl.ds(1024 * half, 1024)]

    def down_view(half):
        return lambda z, p, h: w_down.at[z, p, h, pl.ds(32 * half, 32)]

    views = [
        (qkv_s.at[:, :, pl.ds(0, LANES)], qkv_view(0)),
        (qkv_s.at[:, :, pl.ds(LANES, LANES)], qkv_view(1)),
        (out_s, lambda z, p, h: w_out.at[z, p, :, columns(h)]),
        (up_s.at[:, pl.ds(0, 1024)], up_view(0)),
        (up_s.at[:, pl.ds(1024, 1024)], up_view(1)),
        (down_s.at[pl.ds(0, 32)], down_view(0)),
        (down_s.at[pl.ds(32, 32)], down_view(1)),
    ]
    gathers = [
        (DirectGather if i < 2 else PlaneGather if i == 6 else Gather)(me, shard, view, g_send.at[i], g_recv.at[i], g_local.at[i])
        for i, (shard, view) in enumerate(views)
    ]
    qkv_a, qkv_b, out_g, up_a, up_b, down_a, down_b = gathers
    small = SmallGather(me, small_tiles, small_lines, g_send.at[7], g_recv.at[7])
    small.first(gains, biases, up_bias)
    barrier(me)
    small.second()
    qkv_a.first()
    own_rows = pl.ds(pl.multiple_of(me.h * ROWS, ROWS), ROWS)
    hidden_masks(segment[own_rows, :], kinds[own_rows, :], mask)
    qkv_a.relay(1)
    small.third()
    qkv_a.relay(2)
    qkv_a.relay(3)
    qkv_b.first()
    down_b.first()
    out_g.first()
    up_a.first()
    qkv_a.own_across()
    small.fourth(gb, upb)
    load_tok.wait()

    def norm_one(i, carry):
        r = block(i, 256)
        xhat, _ = normalized(tok[r, :].astype(f32))
        normed[r, :] = (xhat * gb[0:1, :] + gb[2:3, :]).astype(bf16)
        return carry

    lax.fori_loop(0, T // 256, norm_one, 0)
    for n in range(2):
        qkv_a.other_across(n)
    for k in (1, 2, 3):
        qkv_b.relay(k)
    qkv_a.other_across(2)
    qkv_b.own_across()
    up_b.first()
    down_a.first()
    qkv_a.fifth()

    def at_step(i, steps):
        for n, actions in steps.items():

            @pl.when(i == n)
            def _():
                for action in actions:
                    action()

    blocks = T // 512

    def project(i):
        c, r = i // blocks, block(lax.rem(i, blocks), 512)
        x = normed[r, :]
        values = []
        for s in range(3):
            value = dot(x, w_qkv[c, s].reshape(D, 256))
            if s != 1:
                row = 3 + s // 2
                value = value + jnp.concatenate(
                    [gb[row : row + 1, columns(c, LANES)], gb[row : row + 1, columns(2 + c, LANES)]], axis=1
                )
            value = value.astype(bf16)
            values.append(value * jnp.asarray(0.125, bf16) if s == 0 else value)
        return values

    def keep(i, projected):
        c, r = i // blocks, block(lax.rem(i, blocks), 512)
        for n in range(2):
            for s, value in enumerate(projected):
                packed[s, 2 * n + c, r, :] = value[:, LANES * n : LANES * n + LANES]

    start = me.z * 0
    keep(start, project(start))

    def attend(i, carry):
        c, b = i // blocks, lax.rem(i, blocks)
        items = [(4 * b + u, 2 * n + c) for u in range(4) for n in range(2)]
        scores = [
            dot(two_heads(packed[1, p, block(r, SEQ), :]), packed[0, p, block(r, SEQ), :], NT) for r, p in items
        ]
        values = [two_heads(packed[2, p, block(r, SEQ), :]) for r, p in items]
        following = jnp.minimum(i + 1, 2 * blocks - 1)
        projected = project(following)
        weights = []
        for (r, p), pair in zip(items, scores):
            heads = []
            for h in range(2):
                t = pair[SEQ * h : SEQ * h + SEQ] + mask[r].astype(f32)
                e = jnp.exp(t - jnp.max(t, axis=0, keepdims=True))
                a = (e * (1.0 / jnp.sum(e, axis=0, keepdims=True))).astype(bf16)
                att[r, 2 * p + h] = a
                heads.append(a)
            weights.append(jnp.concatenate(heads, axis=0))
        for (r, p), pair, value in zip(items, weights, values):
            mix[p, block(r, SEQ), :] = dot(pair, value, TN).astype(bf16)
        keep(following, projected)
        at_step(
            i,
            {
                0: [lambda: qkv_b.other_across(0), lambda: qkv_b.other_across(1), out_g.second, up_a.second],
                1: [lambda: qkv_b.other_across(2)],
                2: [qkv_b.fifth, up_b.second, down_b.second],
                3: [out_g.third],
                5: [up_a.third],
                6: [out_g.fourth],
                7: [up_b.third, down_a.second],
            },
        )
        return carry

    lax.fori_loop(0, 2 * blocks, attend, 0)
    out_g.fifth()

    def middle_of(r):
        return tok[r, :].astype(f32) + dot(tiles(mix, r), w_out[...].reshape(D, D), NT) + gb[5:6, :]

    def norm_two(i, carry):
        r = block(i, 512)
        middle = middle_of(r)
        xhat, _ = normalized(middle)
        tok[r, :] = (xhat * gb[1:2, :] + gb[6:7, :]).astype(bf16)
        middle = middle.astype(bf16)
        for p in range(4):
            gmix[p, r, :] = middle[:, LANES * p : LANES * p + LANES]
        at_step(i, {1: [up_a.fourth]})
        return carry

    lax.fori_loop(0, T // 512, norm_two, 0)
    up_b.fourth()
    up_a.fifth()

    half_count = count // 2

    def up_columns(j):
        return w_up[:, :, :, :, 512 * j : 512 * j + 512].reshape(D, 512)

    def hidden_block(columns_in, steps):
        def body(i, carry):
            r = block(i, BM)
            two = tok[r, :]
            for j in columns_in:
                cols = slice(512 * j, 512 * j + 512)
                hidden, slope = gelu_and_slope(dot(two, up_columns(j)) + upb[:, cols])
                hid[r, cols] = hidden.astype(bf16)
                gpre[r, cols] = slope.astype(bf16)
            at_step(i, steps)
            return carry

        return body

    lax.fori_loop(0, half_count, hidden_block((0, 1), {3: [down_a.third]}), 0)
    up_b.fifth()
    lax.fori_loop(0, half_count, hidden_block((2, 3), {3: [down_a.fourth]}), 0)
    down_b.third()
    load_cot.wait()
    down_a.fifth()
    down_b.fifth()
    acc[...] = jnp.zeros_like(acc)
    acc_up[...] = jnp.zeros_like(acc_up)
    acc_q[...] = jnp.zeros_like(acc_q)

    def branch_back(r, e, c):
        xhat, rstd = normalized(tiles(gmix, r).astype(f32))
        cot_f32 = c.astype(f32)
        branch = (cot_f32 + norm_back(e, xhat, rstd, gb[1:2, :])).astype(bf16)
        gbr[r, :] = branch
        grad_mix = dot(branch, w_out[...].reshape(D, D)).astype(bf16)
        for p in range(4):
            gmix[p, r, :] = grad_mix[:, LANES * p : LANES * p + LANES]
        acc[1] += column_sums(e * xhat)
        acc[6] += column_sums(e)
        acc[5] += column_sums(branch.astype(f32))
        acc[7] += column_sums(cot_f32)

    def hidden_back(i, carry):
        ra, rb = block(i, BM), block(i + half_count, BM)
        ca, cb, two = cot[ra, :], cot[rb, :], tok[rb, :]
        ea = eb = 0.0
        for j in range(4):
            cols = slice(512 * j, 512 * j + 512)
            w_up_j, w_down_j = up_columns(j), w_down[j].reshape(512, D)
            hidden, slope = gelu_and_slope(dot(two, w_up_j) + upb[:, cols])
            hid[rb, cols] = hidden.astype(bf16)
            pre_a = dot(ca, w_down_j, NT) * gpre[ra, cols].astype(f32)
            pre_b = dot(cb, w_down_j, NT) * slope
            acc_up[:, cols] += column_sums(pre_a) + column_sums(pre_b)
            pre_a, pre_b = pre_a.astype(bf16), pre_b.astype(bf16)
            gpre[ra, cols] = pre_a
            gpre[rb, cols] = pre_b
            ea = ea + dot(pre_a, w_up_j, NT)
            eb = eb + dot(pre_b, w_up_j, NT)
        branch_back(ra, ea, ca)
        branch_back(rb, eb, cb)
        return carry

    lax.fori_loop(0, half_count, hidden_back, 0)

    units = [
        Scatter(me, *refs, s_send.at[i], s_recv.at[i])
        for i, refs in enumerate(
            (
                (p_down0, core0, cross0, sets0, line0),
                (p_down1, core1, cross1, sets1, line1),
                (p_up0, core2, cross2, sets2, line2),
                (p_up1, core3, cross3, sets3, line3),
                (p_out, core4, cross4, sets4, line4),
                *((p_qkv.at[n], core5.at[n], cross5.at[n], sets5.at[n], line5.at[n]) for n in range(3)),
            )
        )
    ]
    d0, d1, u0, u1, out_u, *qkv_u = units

    def grad_down_chunk(z, carry):
        o = dot(cot[...], hid[:, block(z, 512)], TN).astype(bf16).T
        for half, part in enumerate((p_down0, p_down1)):
            for p in range(GRID_P):
                for h in range(2):
                    for j in range(2):
                        part[h, z, p, 64 * j : 64 * j + 64] = o[
                            64 * (2 * p + h) : 64 * (2 * p + h) + 64,
                            256 * half + LANES * j : 256 * half + LANES * j + LANES,
                        ]
        return carry

    def grad_up_chunk(half, part):
        def body(c, carry):
            o = dot(tok[...], gpre[:, block(2 * half + c, 512)], TN).astype(bf16)
            for z in range(GRID_Z):
                for p in range(GRID_P):
                    for h in range(2):
                        d = (z * 4 + p) * 2 + h
                        for j in range(4):
                            part[h, z, p, pl.ds(pl.multiple_of(64 * c + 16 * j, 16), 16)] = o[
                                16 * d : 16 * d + 16, LANES * j : LANES * j + LANES
                            ]
            return carry

        return body

    o = dot(gbr[...], jnp.concatenate([mix[p] for p in range(4)], axis=1), TN).astype(bf16)
    for z in range(GRID_Z):
        for p in range(GRID_P):
            d = z * 4 + p
            for h in range(2):
                for j in range(2):
                    p_out[h, z, p, 32 * j : 32 * j + 32] = o[
                        32 * d : 32 * d + 32, 256 * h + LANES * j : 256 * h + LANES * j + LANES
                    ]
    out_u.first()
    lax.fori_loop(0, 4, grad_down_chunk, 0)
    out_u.second()
    d0.first()
    d1.first()
    lax.fori_loop(0, 2, grad_up_chunk(0, p_up0), 0)
    d0.second()
    u0.first()
    d1.second()
    lax.fori_loop(0, 2, grad_up_chunk(1, p_up1), 0)
    u1.first()
    out_u.third()
    load_tok = pltpu.make_async_copy(tokens_hbm, tok, io_sem.at[0])
    load_tok.start()
    u0.second()
    d0.third()

    u1.second()
    d1.third()

    def attend_back(half, steps):
        def body(i, carry):
            row = lax.broadcasted_iota(jnp.int32, (2 * SEQ, LANES), 0) // SEQ
            lane = lax.broadcasted_iota(jnp.int32, (2 * SEQ, LANES), 1) // 64
            minus = jnp.where(row == lane, -1.0, 0.0).astype(bf16)
            items = [(4 * i + u, 2 * half + pp) for u in range(4) for pp in range(2)]
            grads, slopes = [], []
            for r, p in items:
                rows = block(r, SEQ)
                grad = gmix[p, rows, :]
                product = (grad.astype(f32) * mix[p, rows, :].astype(f32)).astype(bf16)
                values = jnp.concatenate([two_heads(packed[2, p, rows, :]), minus], axis=1)
                grads.append(dot(values, jnp.concatenate([grad, product], axis=1), NT))
            for (r, p), pair in zip(items, grads):
                slopes.append(
                    [
                        (att[r, 2 * p + h].astype(f32) * pair[SEQ * h : SEQ * h + SEQ]).astype(bf16)
                        for h in range(2)
                    ]
                )
            results, sums = [], [0.0] * 4
            for n, ((r, p), pair) in enumerate(zip(items, slopes)):
                rows = block(r, SEQ)
                queries, keys = two_heads(packed[0, p, rows, :]), two_heads(packed[1, p, rows, :])
                g_q = dot(jnp.concatenate(pair, axis=0), keys, TN) * 0.125
                g_k = dot(jnp.concatenate(pair, axis=1), queries)
                weights = jnp.concatenate([att[r, 2 * p], att[r, 2 * p + 1]], axis=1)
                g_v = dot(weights, two_heads(gmix[p, rows, :]))
                sums[n % 2] = sums[n % 2] + column_sums(g_q)
                sums[2 + n % 2] = sums[2 + n % 2] + column_sums(g_v)
                results.append((g_q.astype(bf16), g_k.astype(bf16), g_v.astype(bf16)))
            for (r, p), result in zip(items, results):
                for n in range(3):
                    packed[n, p, block(r, SEQ), :] = result[n]
            for pp in range(2):
                acc_q[0, 2 * half + pp] += sums[pp]
                acc_q[1, 2 * half + pp] += sums[2 + pp]
            at_step(i, steps)
            return carry

        return body

    def grad_qkv_half(half, steps):
        def body(s, carry):
            wide = jnp.concatenate([packed[s, 2 * half], packed[s, 2 * half + 1]], axis=1)
            o = dot(normed[...], wide, TN).astype(bf16)
            for z in range(GRID_Z):
                for p in range(GRID_P):
                    d = z * 4 + p
                    for j in range(2):
                        p_qkv[s, half, z, p, 32 * j : 32 * j + 32] = o[
                            32 * d : 32 * d + 32, LANES * j : LANES * j + LANES
                        ]
            at_step(s, steps)
            return carry

        return body

    lax.fori_loop(0, ROWS // 4, attend_back(me.sib, {1: [out_u.fourth], 2: [u0.third]}), 0)
    lax.fori_loop(0, 3, grad_qkv_half(me.sib, {n: [qkv_u[n].first] for n in range(3)}), 0)
    d0.fourth()
    u1.third()
    lax.fori_loop(0, ROWS // 4, attend_back(me.h, {3: [d1.fourth]}), 0)
    lax.fori_loop(0, 3, grad_qkv_half(me.h, {n: [qkv_u[n].second] for n in range(3)}), 0)
    u0.fourth()
    load_tok.wait()

    def grad_copy(i):
        return pltpu.make_async_copy(
            grad_stage.at[parity(i)], grad_hbm.at[block(i, BACK), :], out_sem.at[parity(i)]
        )

    def norm_one_back(i, carry):
        r = block(i, BACK)

        @pl.when(i >= 2)
        def _():
            grad_copy(i - 2).wait()

        e = 0.0
        for c in range(2):
            for s in range(3):
                pair = jnp.concatenate([packed[s, c, r, :], packed[s, 2 + c, r, :]], axis=1)
                e = e + dot(pair, w_qkv[c, s].reshape(D, 256), NT)
        xhat, rstd = normalized(tok[r, :].astype(f32))
        grad = gbr[r, :].astype(f32) + norm_back(e, xhat, rstd, gb[0:1, :])
        grad_stage[parity(i)] = grad.astype(bf16)
        grad_copy(i).start()
        acc[0] += column_sums(e * xhat)
        acc[2] += column_sums(e)
        at_step(i, {0: [qkv_u[0].third], 1: [u1.fourth], 2: [qkv_u[1].third, qkv_u[2].third]})
        return carry

    lax.fori_loop(0, back_count, norm_one_back, 0)
    for p in range(4):
        acc[3, :, LANES * p : LANES * p + LANES] = acc_q[0, p]
        acc[4, :, LANES * p : LANES * p + LANES] = acc_q[1, p]
    for z in range(GRID_Z):
        rows = [jnp.sum(acc[n, :, LANES * z : LANES * z + LANES], axis=0, keepdims=True) for n in range(8)]
        rows += [
            jnp.sum(acc_up[:, 512 * z + LANES * p : 512 * z + LANES * p + LANES], axis=0, keepdims=True)
            for p in range(GRID_P)
        ]
        rows += [jnp.zeros((4, LANES), f32)]
        p_small[z] = jnp.concatenate(rows, axis=0)
    small_sum = SmallScatter(me, p_small, small_line, small_sets, s_send.at[8], s_recv.at[8])
    small_sum.first()

    def out_copies(i):
        r = block(i, 512)
        return [
            pltpu.make_async_copy(
                gmix.at[p, r], output_hbm.at[r, pl.ds(LANES * p, LANES)], out_sem.at[2]
            )
            for p in range(4)
        ]

    def output_block(i, carry):
        r = block(i, 512)
        total = middle_of(r) + dot(hid[r, :], w_down[...].reshape(2048, D)) + gb[7:8, :]
        total = total.astype(bf16)
        for p in range(4):
            gmix[p, r, :] = total[:, LANES * p : LANES * p + LANES]
        for copy in out_copies(i):
            copy.start()
        at_step(i, {0: [qkv_u[0].fourth], 1: [small_sum.second, qkv_u[1].fourth], 2: [qkv_u[2].fourth]})
        return carry

    lax.fori_loop(0, T // 512, output_block, 0)
    for unit, rows in ((out_u, OUT_ROWS), (d0, DOWN_ROWS), (d1, DOWN_ROWS + 128), (u0, UP_ROWS), (u1, UP_ROWS + 128)):
        total = unit.fifth()
        sums[rows : rows + total.shape[0]] = total
    small_sum.third(sums)
    for n in range(3):
        sums[QKV_ROWS + 64 * n : QKV_ROWS + 64 * n + 64] = qkv_u[n].fifth()
    for i in range(T // 512):
        for copy in out_copies(i):
            copy.wait()
    for i in (back_count - 2, back_count - 1):
        grad_copy(i).wait()
    for item in gathers + units + [small, small_sum]:
        item.close()


def finish_kernel(output, grad, sums_hbm, *refs):
    targets, stages, sums, grad_in, sems = refs[:9], refs[9:18], refs[18], refs[19], refs[20]
    staged = (stages[0], grad_in)
    loads, stores = [], []
    load_sums = pltpu.make_async_copy(sums_hbm, sums, sems.at[0, 0, 4])
    load_sums.start()
    for n in range(4):
        for a, source in ((1, grad), (0, output)):
            size = source.shape[0] // 4
            rows = pl.ds(n * size, size)
            loads.append(pltpu.make_async_copy(source.at[rows], staged[a].at[rows], sems.at[0, a, n]))
            stores.append(pltpu.make_async_copy(stages[a].at[rows], targets[a].at[rows], sems.at[1, a, n]))
    for load in loads:
        load.start()
    g_qkv, g_out, g_up, g_down, g_gains, g_biases, g_up_bias = stages[2:]
    load_sums.wait()

    def tile(start, rows, j):
        return sums[start + rows * j : start + rows * (j + 1)]

    for j in range(4):
        g_down[:, LANES * j : LANES * j + LANES] = tile(DOWN_ROWS, 64, j)
    for j in range(16):
        g_up[:, LANES * j : LANES * j + LANES] = tile(UP_ROWS, 16, j)
    for j in range(2):
        g_out[:, LANES * j : LANES * j + LANES] = tile(OUT_ROWS, 32, j)
        for s in range(3):
            g_qkv[s, :, LANES * j : LANES * j + LANES] = tile(QKV_ROWS + 64 * s, 32, j)
    g_gains[...] = sums[SMALL_ROWS : SMALL_ROWS + 2, 0:16]
    g_biases[...] = sums[SMALL_ROWS + 2 : SMALL_ROWS + 8, 0:16]
    g_up_bias[...] = sums[SMALL_ROWS + 8 : SMALL_ROWS + 9, 0:64]
    for n in range(2, 9):
        stores.append(pltpu.make_async_copy(stages[n], targets[n], sems.at[2, n // 5, n % 5]))
        stores[-1].start()
    for i, (load, store) in enumerate(zip(loads, stores)):
        load.wait()
        if i % 2 == 0:
            rows = slice(i // 2 * size, (i // 2 + 1) * size)
            stages[1][rows] = grad_in[rows].astype(f32)
        store.start()
    for store in stores:
        store.wait()


def finish(output, grad, sums):
    shape = jax.ShapeDtypeStruct
    outs = (
        shape(output.shape, bf16),
        shape(grad.shape, f32),
        shape((3, 32, 256), f32),
        shape((32, 256), f32),
        shape((16, 2048), f32),
        shape((64, 512), f32),
        shape((2, 16), f32),
        shape((6, 16), f32),
        shape((1, 64), f32),
    )
    return pl.pallas_call(
        finish_kernel,
        out_shape=outs,
        in_specs=[ANY] * 3,
        out_specs=[ANY] * 9,
        scratch_shapes=[pltpu.VMEM(o.shape, o.dtype) for o in outs]
        + [pltpu.VMEM(sums.shape, f32), pltpu.VMEM(grad.shape, bf16), pltpu.SemaphoreType.DMA((3, 2, 5))],
        compiler_params=pltpu.CompilerParams(vmem_limit_bytes=VMEM_LIMIT),
        name="finish",
    )(output, grad, sums)


def layer(tokens, cotangent, qkv, out, up, down, gains, biases, up_bias, segment, kinds):
    shape = jax.ShapeDtypeStruct
    T = tokens.shape[0]
    rows = T // SEQ
    outs = (shape((T, D), bf16), shape((T, D), bf16), shape((ALL_ROWS, LANES), f32))
    sizes = [128, 128, 128, 128, 64]
    V, S = pltpu.VMEM, pltpu.SemaphoreType.DMA
    scratch = [
        V((T, D), bf16), V((T, D), bf16),
        V((2, 3, 4, 4, 32, 256), bf16), V((4, 4, 32, 512), bf16),
        V((4, 4, 2, 16, 2048), bf16), V((4, 4, 2, 64, 512), bf16),
        V((8, 512), f32), V((1, 2048), f32), V((rows, SEQ, SEQ), bf16),
        V((T, D), bf16), V((3, 4, T, LANES), bf16), V((rows, 8, SEQ, SEQ), bf16),
        V((4, T, LANES), bf16), V((T, 2048), bf16), V((T, 2048), bf16),
        V((T, D), bf16), V((4, T, LANES), bf16), V((8, 8, 512), f32), V((8, 2048), f32),
        V((2, 4, 8, LANES), f32),
        V((2, 512, D), bf16),
    ]
    scratch += [V((2, 4, 4, r, LANES), bf16) for r in sizes] + [V((3, 2, 4, 4, 64, LANES), bf16)] + [V((4, 16, LANES), f32)]
    scratch += [V((4, 4, r, LANES), bf16) for r in sizes] + [V((3, 4, 4, 64, LANES), bf16)]
    scratch += [V((2, 2, r, LANES), bf16) for r in sizes] + [V((3, 2, 2, 64, LANES), bf16)]
    scratch += [V((2, 4, r, LANES), bf16) for r in sizes] + [V((3, 2, 4, 64, LANES), bf16)]
    scratch += [V((3, r, LANES), bf16) for r in sizes] + [V((3, 3, 64, LANES), bf16)]
    scratch += [V((4, 2, 16, LANES), bf16), V((4, 16, LANES), bf16), V((3, 16, LANES), f32), V((8, 16, LANES), f32)]
    scratch += [S((8, 19)), S((8, 19)), S((7,)), S((9, 10)), S((9, 10)), S((2,)), S((3,))]
    return pl.pallas_call(
        layer_kernel,
        out_shape=outs,
        in_specs=[ANY] * 6 + [VM] * 5,
        out_specs=[ANY] * 2 + [VM],
        scratch_shapes=scratch,
        compiler_params=pltpu.CompilerParams(
            collective_id=0, has_side_effects=True, vmem_limit_bytes=VMEM_LIMIT
        ),
        name="layer",
    )(tokens, cotangent, qkv, out, up, down, gains, biases, up_bias, segment, kinds)


def widened(x, axes, dim):
    return lax.all_gather(x, axes, axis=dim, tiled=True)


def on_device(rep):
    def run(
        tokens, qkv, out, up, down, gains, biases, up_bias, segment, kinds, cotangent
    ):
        up_bias = up_bias.reshape(1, -1)
        head = lax.axis_index("head")
        if rep > 1:
            both = ("rep", "head")
            qkv, out = widened(qkv, "rep", 1), widened(out, "rep", 0)
            up = lax.dynamic_slice_in_dim(widened(up, both, 0), head * 16, 16, 0)
            down = lax.dynamic_slice_in_dim(widened(down, both, 0), head * 64, 64, 0)
            gains = lax.dynamic_slice_in_dim(widened(gains, both, 1), head * 16, 16, 1)
            biases = lax.dynamic_slice_in_dim(widened(biases, both, 1), head * 16, 16, 1)
            up_bias = lax.dynamic_slice_in_dim(widened(up_bias, both, 1), head * 64, 64, 1)
        output, grad, *grads = finish(
            *layer(tokens, cotangent, qkv, out, up, down, gains, biases, up_bias, segment, kinds)
        )
        if rep > 1:
            place = lax.axis_index("rep") * 2 + head

            def own(x, dim):
                x = lax.all_gather(lax.psum(x, "rep"), "head", axis=dim, tiled=True)
                size = x.shape[dim] // (2 * rep)
                return lax.dynamic_slice_in_dim(x, place * size, size, dim)

            for i, dim in ((0, 1), (1, 0)):
                grads[i] = lax.psum_scatter(grads[i], "rep", scatter_dimension=dim, tiled=True)
            for i, dim in ((2, 0), (3, 0), (4, 1), (5, 1), (6, 1)):
                grads[i] = own(grads[i], dim)
        grads[6] = grads[6].reshape(-1)
        return (output, grad, *grads)

    return run


def solution(mesh):
    rep = mesh.shape["dp"] // (GRID_Z * GRID_P)
    wide = Mesh(mesh.devices.reshape(GRID_Z * GRID_P, rep, 2), ("dp", "rep", "head"))
    dp, every = ("dp", "rep"), ("dp", "rep", "head")
    in_specs = (
        P(every, None),
        P(None, dp, "head"),
        P(dp, "head"),
        P(every, None),
        P(every, None),
        P(None, every),
        P(None, every),
        P(every),
        P(dp, None),
        P(dp, None),
        P(every, None),
    )
    out_specs = (
        P(every, None),
        P(every, None),
        P(None, dp, "head"),
        P(dp, "head"),
        P(every, None),
        P(every, None),
        P(None, every),
        P(None, every),
        P(every),
    )
    return jax.shard_map(
        on_device(rep), mesh=wide, in_specs=in_specs, out_specs=out_specs, check_vma=False
    )
```

```python
import math

import jax
import jax.numpy as jnp
from jax import lax
from jax.experimental import pallas as pl
from jax.experimental.pallas import tpu as pltpu
from jax.sharding import Mesh
from jax.sharding import PartitionSpec as P

bf16, f32 = jnp.bfloat16, jnp.float32
D = 512
SEQ = 128
LANES = 128
GRID_Z, GRID_P = 4, 4
EPS = 1e-5
MESH = pl.DeviceIdType.MESH
NN = (((1,), (0,)), ((), ()))
NT = (((1,), (1,)), ((), ()))
TN = (((0,), (0,)), ((), ()))
DOWN_ROWS, UP_ROWS, OUT_ROWS, QKV_ROWS, SMALL_ROWS, ALL_ROWS = 0, 256, 512, 576, 768, 784
VMEM_LIMIT = (63 << 20) + (512 << 10)


def dot(a, b, dims=NN):
    return lax.dot_general(a, b, dims, preferred_element_type=f32)


def block(index, size):
    if isinstance(index, int):
        return pl.ds(index * size, size)
    return pl.ds(pl.multiple_of(index * size, size), size)


def parity(index):
    return index % 2 if isinstance(index, int) else lax.rem(index, 2)


class Place:
    def __init__(self):
        dp, self.h = lax.axis_index("dp"), lax.axis_index("head")
        self.z, self.p = dp // GRID_P, lax.rem(dp, GRID_P)
        x, y = lax.rem(self.p, 2), self.p // 2
        self.px = y * 2 + (1 - x)
        self.py = (1 - y) * 2 + x
        self.pd = (1 - y) * 2 + (1 - x)
        self.sib = 1 - self.h

    def at(self, z, p, h):
        return {"dp": z * GRID_P + p, "head": h}

    def line(self, k):
        return lax.rem(self.z + k, GRID_Z)

    def line_back(self, k):
        if k == 0:
            return self.z
        return lax.rem(self.z + (GRID_Z - k), GRID_Z)

    def plane(self):
        places = [(self.px, self.h), (self.py, self.h), (self.pd, self.h)]
        places += [(p, self.sib) for p in (self.p, self.px, self.py, self.pd)]
        return places


def barrier(me):
    sem = pltpu.get_barrier_semaphore()
    for p, h in me.plane():
        pl.semaphore_signal(sem, 1, device_id=me.at(me.z, p, h), device_id_type=MESH)
    for k in (1, 2, 3):
        pl.semaphore_signal(sem, 1, device_id=me.at(me.line(k), me.p, me.h), device_id_type=MESH)
    pl.semaphore_wait(sem, 10)


def remote(src, dst, send, recv, device):
    return pltpu.make_async_remote_copy(
        src_ref=src, dst_ref=dst, send_sem=send, recv_sem=recv, device_id=device, device_id_type=MESH
    )


class Gather:
    SENDS, RECVS = 11, 11

    def __init__(self, me, shard, view, send, recv, local):
        self.me, self.shard, self.view = me, shard, view
        self.send, self.recv, self.local = send, recv, local
        self.started = []

    def go(self, index, parts):
        def make():
            src, dst, device = parts()
            return remote(src, dst, self.send.at[index], self.recv.at[index], device)

        make().start()
        self.started.append(make)

    def landed(self, index, region):
        me = self.me
        remote(region, region, self.send.at[index], self.recv.at[index], me.at(me.z, me.p, me.sib)).wait_recv()

    def set_of(self, z, p):
        return self.view(z, p, self.me.h)

    def first(self):
        me = self.me
        self.mine = pltpu.make_async_copy(self.shard, self.set_of(me.z, me.p), self.local)
        self.mine.start()
        for k in (1, 2, 3):
            self.go(k - 1, lambda k=k: (self.shard, self.set_of(me.z, me.p), me.at(me.line(k), me.p, me.h)))

    def second(self):
        me = self.me
        self.mine.wait()
        for k in (1, 2, 3):
            self.landed(k - 1, self.view(me.line_back(k), me.p, me.h))
        line = lambda: self.set_of(pl.ds(0, 4), me.p)
        self.go(3, lambda: (line(), line(), me.at(me.z, me.px, me.h)))
        self.go(4, lambda: (line(), line(), me.at(me.z, me.py, me.h)))
        self.go(7, lambda: (line(), line(), me.at(me.z, me.p, me.sib)))

    def third(self):
        me = self.me
        from_x, from_y = lambda: self.set_of(pl.ds(0, 4), me.px), lambda: self.set_of(pl.ds(0, 4), me.py)
        half_x, half_y = lambda: self.set_of(pl.ds(0, 2), me.px), lambda: self.set_of(pl.ds(2, 2), me.py)
        self.landed(3, from_x())
        self.go(6, lambda: (half_x(), half_x(), me.at(me.z, me.py, me.h)))
        self.landed(4, from_y())
        self.go(5, lambda: (half_y(), half_y(), me.at(me.z, me.px, me.h)))
        self.go(8, lambda: (from_x(), from_x(), me.at(me.z, me.p, me.sib)))
        self.go(9, lambda: (from_y(), from_y(), me.at(me.z, me.p, me.sib)))

    def fourth(self):
        me = self.me
        self.landed(6, self.view(pl.ds(0, 2), me.pd, me.h))
        self.landed(5, self.view(pl.ds(2, 2), me.pd, me.h))
        diagonal = lambda: self.set_of(pl.ds(0, 4), me.pd)
        self.go(10, lambda: (diagonal(), diagonal(), me.at(me.z, me.p, me.sib)))

    def fifth(self):
        me = self.me
        for index, p in ((7, me.p), (8, me.px), (9, me.py), (10, me.pd)):
            self.landed(index, self.view(pl.ds(0, 4), p, me.sib))

    def close(self):
        for make in self.started:
            make().wait_send()


class DirectGather(Gather):
    def others(self):
        return self.me.px, self.me.py, self.me.pd

    def first(self):
        me = self.me
        own = lambda: self.set_of(me.z, me.p)
        self.mine = pltpu.make_async_copy(self.shard, own(), self.local)
        self.mine.start()
        for k in (1, 2, 3):
            self.go(k - 1, lambda k=k: (self.shard, own(), me.at(me.line(k), me.p, me.h)))
        for n, p in enumerate(self.others()):
            self.go(3 + 4 * n, lambda p=p: (self.shard, own(), me.at(me.z, p, me.h)))

    def relay(self, k):
        me = self.me
        piece = lambda: self.set_of(me.line_back(k), me.p)
        self.landed(k - 1, piece())
        for n, p in enumerate(self.others()):
            self.go(3 + 4 * n + k, lambda p=p: (piece(), piece(), me.at(me.z, p, me.h)))

    def across(self, index, p):
        me = self.me
        group = lambda: self.set_of(pl.ds(0, 4), p)
        self.go(index, lambda: (group(), group(), me.at(me.z, me.p, me.sib)))

    def own_across(self):
        self.mine.wait()
        self.across(15, self.me.p)

    def other_across(self, n):
        me = self.me
        p = self.others()[n]
        for k in range(4):
            self.landed(3 + 4 * n + k, self.set_of(me.line_back(k), p))
        self.across(16 + n, p)

    def fifth(self):
        me = self.me
        for index, p in ((15, me.p), (16, me.px), (17, me.py), (18, me.pd)):
            self.landed(index, self.view(pl.ds(0, 4), p, me.sib))


class PlaneGather(Gather):
    def group(self, z):
        return self.view(z, pl.ds(0, 4), self.me.h)

    def first(self):
        me = self.me
        own = lambda: self.set_of(me.z, me.p)
        self.mine = pltpu.make_async_copy(self.shard, own(), self.local)
        self.mine.start()
        for n, p in enumerate((me.px, me.py, me.pd)):
            self.go(n, lambda p=p: (self.shard, own(), me.at(me.z, p, me.h)))

    def second(self):
        me = self.me
        self.mine.wait()
        for n, p in enumerate((me.px, me.py, me.pd)):
            self.landed(n, self.set_of(me.z, p))
        for k in (1, 2, 3):
            self.go(2 + k, lambda k=k: (self.group(me.z), self.group(me.z), me.at(me.line(k), me.p, me.h)))
        self.go(6, lambda: (self.group(me.z), self.group(me.z), me.at(me.z, me.p, me.sib)))

    def third(self):
        me = self.me
        for k in (1, 2, 3):
            z = me.line_back(k)
            self.landed(2 + k, self.group(z))
            self.go(6 + k, lambda z=z: (self.group(z), self.group(z), me.at(me.z, me.p, me.sib)))

    def fourth(self):
        pass

    def fifth(self):
        me = self.me
        for k in range(4):
            self.landed(6 + k, self.view(me.line_back(k), pl.ds(0, 4), me.sib))


class SmallGather:
    def __init__(self, me, tiles, lines, send, recv):
        self.me, self.tiles, self.lines, self.send, self.recv = me, tiles, lines, send, recv
        self.started = []

    def go(self, index, parts):
        def make():
            region, device = parts()
            return remote(region, region, self.send.at[index], self.recv.at[index], device)

        make().start()
        self.started.append(make)

    def landed(self, index, region):
        me = self.me
        remote(region, region, self.send.at[index], self.recv.at[index], me.at(me.z, me.p, me.sib)).wait_recv()

    def first(self, gains, biases, up_bias):
        me = self.me
        place = lambda rows, width, start: dot(
            rows,
            jnp.where(
                lax.broadcasted_iota(jnp.int32, (width, LANES), 1)
                == lax.broadcasted_iota(jnp.int32, (width, LANES), 0) + start,
                1.0,
                0.0,
            ).astype(bf16),
        )
        start = (me.p * 2 + me.h) * 16
        row = lax.broadcasted_iota(jnp.int32, (8, LANES), 0)
        hidden = jnp.broadcast_to(place(up_bias[...], 64, me.h * 64), (8, LANES))
        rows = jnp.concatenate(
            [
                place(gains[...], 16, start),
                place(biases[...], 16, start),
                jnp.where(row == me.p, hidden, 0.0),
            ],
            axis=0,
        )
        self.tiles[me.p, me.h] = rows.astype(bf16)

    def second(self):
        me = self.me
        for index, (p, h) in enumerate(me.plane()):
            self.go(index, lambda p=p, h=h: (self.tiles.at[me.p, me.h], me.at(me.z, p, h)))

    def third(self):
        me = self.me
        for index, (p, h) in enumerate(me.plane()):
            self.landed(index, self.tiles.at[p, h])
        total = jnp.zeros((16, LANES), f32)
        for p in range(GRID_P):
            for h in range(2):
                total = total + self.tiles[p, h].astype(f32)
        self.lines[me.z] = total.astype(bf16)
        for k in (1, 2, 3):
            self.go(6 + k, lambda k=k: (self.lines.at[me.z], me.at(me.line(k), me.p, me.h)))

    def fourth(self, gain_bias, up_bias):
        me = self.me
        for k in (1, 2, 3):
            self.landed(6 + k, self.lines.at[me.line_back(k)])
        for z in range(GRID_Z):
            line = self.lines[z].astype(f32)
            gain_bias[:, z * LANES : (z + 1) * LANES] = line[:8]
            for p in range(GRID_P):
                up_bias[:, (z * GRID_P + p) * LANES : (z * GRID_P + p + 1) * LANES] = line[8 + p : 9 + p]

    def close(self):
        for make in self.started:
            make().wait_send()


class Scatter:
    SENDS, RECVS = 8, 8

    def __init__(self, me, part, core, cross, sets, line, send, recv):
        self.me, self.part, self.core, self.cross, self.sets, self.line = me, part, core, cross, sets, line
        self.send, self.recv = send, recv
        self.started = []

    def go(self, index, parts):
        def make():
            src, dst, device = parts()
            return remote(src, dst, self.send.at[index], self.recv.at[index], device)

        make().start()
        self.started.append(make)

    def landed(self, index, region):
        me = self.me
        remote(region, region, self.send.at[index], self.recv.at[index], me.at(me.z, me.p, me.sib)).wait_recv()

    def first(self):
        me = self.me
        self.go(0, lambda: (self.part.at[me.sib], self.core, me.at(me.z, me.p, me.sib)))

    def second(self):
        me, part = self.me, self.part
        self.landed(0, self.core)
        part[me.h] = part[me.h] + self.core[...]
        self.go(1, lambda: (part.at[me.h, pl.ds(0, 2), me.pd], self.cross.at[0], me.at(me.z, me.py, me.h)))
        self.go(2, lambda: (part.at[me.h, pl.ds(2, 2), me.pd], self.cross.at[1], me.at(me.z, me.px, me.h)))

    def third(self):
        me, part = self.me, self.part
        self.landed(1, self.cross.at[0])
        self.landed(2, self.cross.at[1])

        for i in range(2):
            part[me.h, i, me.px] = part[me.h, i, me.px] + self.cross[0, i]
            part[me.h, 2 + i, me.py] = part[me.h, 2 + i, me.py] + self.cross[1, i]
        self.go(3, lambda: (part.at[me.h, :, me.px], self.sets.at[0], me.at(me.z, me.px, me.h)))
        self.go(4, lambda: (part.at[me.h, :, me.py], self.sets.at[1], me.at(me.z, me.py, me.h)))

    def fourth(self):
        me, part = self.me, self.part
        self.landed(3, self.sets.at[0])
        self.landed(4, self.sets.at[1])
        for i in range(GRID_Z):
            part[me.h, i, me.p] = (
                part[me.h, i, me.p].astype(f32) + self.sets[0, i].astype(f32) + self.sets[1, i].astype(f32)
            ).astype(bf16)
        for k in (1, 2, 3):
            self.go(
                4 + k,
                lambda k=k: (
                    part.at[me.h, me.line(k), me.p], self.line.at[k - 1], me.at(me.line(k), me.p, me.h)
                ),
            )

    def fifth(self):
        me = self.me
        total = self.part[me.h, me.z, me.p].astype(f32)
        for k in (1, 2, 3):
            self.landed(4 + k, self.line.at[k - 1])
            total = total + self.line[k - 1].astype(f32)
        return total

    def close(self):
        for make in self.started:
            make().wait_send()


class SmallScatter:
    SENDS, RECVS = 10, 10

    def __init__(self, me, part, line, sets, send, recv):
        self.me, self.part, self.line, self.sets = me, part, line, sets
        self.send, self.recv = send, recv
        self.started = []

    def go(self, index, parts):
        def make():
            src, dst, device = parts()
            return remote(src, dst, self.send.at[index], self.recv.at[index], device)

        make().start()
        self.started.append(make)

    def landed(self, index, region):
        me = self.me
        remote(region, region, self.send.at[index], self.recv.at[index], me.at(me.z, me.p, me.sib)).wait_recv()

    def first(self):
        me = self.me
        for k in (1, 2, 3):
            self.go(
                k - 1,
                lambda k=k: (self.part.at[me.line(k)], self.line.at[k - 1], me.at(me.line(k), me.p, me.h)),
            )

    def second(self):
        me = self.me
        total = self.part[me.z]
        for k in (1, 2, 3):
            self.landed(k - 1, self.line.at[k - 1])
            total = total + self.line[k - 1]
        self.sets[7] = total
        for index, (p, h) in enumerate(me.plane()):
            self.go(
                3 + index, lambda i=index, p=p, h=h: (self.sets.at[7], self.sets.at[i], me.at(me.z, p, h))
            )

    def third(self, sums):
        me = self.me
        total = self.sets[7]
        for index in range(7):
            self.landed(3 + index, self.sets.at[index])
            total = total + self.sets[index]
        sums[SMALL_ROWS : SMALL_ROWS + 8] = pltpu.roll(total[:8], LANES - 16 * (me.p * 2 + me.h), 1)
        row = lax.broadcasted_iota(jnp.int32, (8, LANES), 0)
        hidden = jnp.sum(jnp.where(row == me.p, total[8:], 0.0), axis=0, keepdims=True)
        hidden = jnp.broadcast_to(hidden, (8, LANES))
        sums[SMALL_ROWS + 8 : SMALL_ROWS + 16] = jnp.where(me.h == 0, hidden, pltpu.roll(hidden, 64, 1))

    def close(self):
        for make in self.started:
            make().wait_send()


ANY = pl.BlockSpec(memory_space=pl.ANY)
VM = pl.BlockSpec(memory_space=pltpu.VMEM)


def normalized(x):
    center = x - jnp.mean(x, axis=-1, keepdims=True)
    rstd = lax.rsqrt(jnp.mean(center * center, axis=-1, keepdims=True) + EPS)
    return center * rstd, rstd


def norm_back(e, xhat, rstd, gain):
    u = e * gain
    return rstd * (
        u - jnp.mean(u, axis=-1, keepdims=True) - xhat * jnp.mean(u * xhat, axis=-1, keepdims=True)
    )


def column_sums(x):
    return jnp.sum(x.reshape(x.shape[0] // 8, 8, x.shape[1]), axis=0)


def gelu_and_slope(u):
    phi = 0.5 + 0.5 * lax.erf(u * math.sqrt(0.5))
    return u * phi, phi + u * (jnp.exp(u * u * -0.5) * (1 / math.sqrt(2 * math.pi)))


def two_heads(x):
    first = lax.broadcasted_iota(jnp.int32, x.shape, 1) < 64
    zero = jnp.zeros_like(x)
    return jnp.concatenate([jnp.where(first, x, zero), jnp.where(first, zero, x)], axis=0)


def tiles(ref, rows):
    return jnp.concatenate([ref[p, rows] for p in range(4)], axis=1)


def hidden_masks(segment, kinds, mask):
    s, k = segment, kinds
    position = lax.broadcasted_iota(jnp.int32, s.shape, 1)
    follows = (s == pltpu.roll(s, 1, 1)) & (k == 2) & (pltpu.roll(k, 1, 1) == 2) & (position > 0)
    upper = lax.broadcasted_iota(jnp.int32, (SEQ, SEQ), 0) <= lax.broadcasted_iota(jnp.int32, (SEQ, SEQ), 1)
    run = dot(jnp.where(follows, 0.0, 1.0).astype(bf16), jnp.where(upper, 1.0, 0.0).astype(bf16))
    seg = s.astype(f32)
    for r in range(s.shape[0]):
        seg_j = jnp.broadcast_to(seg[r : r + 1], (SEQ, SEQ))
        run_j = jnp.broadcast_to(run[r : r + 1], (SEQ, SEQ))
        mask[r] = jnp.where((seg_j.T == seg_j) & (run_j.T <= run_j), 0.0, -jnp.inf).astype(bf16)


def layer_kernel(
    tokens_hbm, cot_hbm, qkv_s, out_s, up_s, down_s, gains, biases, up_bias, segment, kinds,
    output_hbm, grad_hbm, sums,
    tok, cot, w_qkv, w_out, w_up, w_down, gb, upb, mask,
    normed, packed, att, mix, hid, gpre, gbr, gmix, acc, acc_up, acc_q,
    grad_stage,
    p_down0, p_down1, p_up0, p_up1, p_out, p_qkv, p_small,
    core0, core1, core2, core3, core4, core5, cross0, cross1, cross2, cross3, cross4, cross5,
    sets0, sets1, sets2, sets3, sets4, sets5, line0, line1, line2, line3, line4, line5,
    small_tiles, small_lines, small_line, small_sets,
    g_send, g_recv, g_local, s_send, s_recv, io_sem, out_sem,
):
    T = tok.shape[0]
    ROWS = T // SEQ
    BM = 256
    count = T // BM
    BACK = grad_stage.shape[1]
    back_count = T // BACK
    me = Place()
    load_tok = pltpu.make_async_copy(tokens_hbm, tok, io_sem.at[0])
    load_cot = pltpu.make_async_copy(cot_hbm, cot, io_sem.at[1])
    load_tok.start()
    load_cot.start()

    def columns(h, width=256):
        return pl.ds(pl.multiple_of(h * width, width), width)

    def qkv_view(c):
        return lambda z, p, h: w_qkv.at[c, :, z, p, :, columns(h, LANES)]

    def up_view(half):
        return lambda z, p, h: w_up.at[z, p, h, :, pl.ds(1024 * half, 1024)]

    def down_view(half):
        return lambda z, p, h: w_down.at[z, p, h, pl.ds(32 * half, 32)]

    views = [
        (qkv_s.at[:, :, pl.ds(0, LANES)], qkv_view(0)),
        (qkv_s.at[:, :, pl.ds(LANES, LANES)], qkv_view(1)),
        (out_s, lambda z, p, h: w_out.at[z, p, :, columns(h)]),
        (up_s.at[:, pl.ds(0, 1024)], up_view(0)),
        (up_s.at[:, pl.ds(1024, 1024)], up_view(1)),
        (down_s.at[pl.ds(0, 32)], down_view(0)),
        (down_s.at[pl.ds(32, 32)], down_view(1)),
    ]
    gathers = [
        (DirectGather if i < 2 else PlaneGather if i == 6 else Gather)(me, shard, view, g_send.at[i], g_recv.at[i], g_local.at[i])
        for i, (shard, view) in enumerate(views)
    ]
    qkv_a, qkv_b, out_g, up_a, up_b, down_a, down_b = gathers
    small = SmallGather(me, small_tiles, small_lines, g_send.at[7], g_recv.at[7])
    small.first(gains, biases, up_bias)
    barrier(me)
    small.second()
    qkv_a.first()
    own_rows = pl.ds(pl.multiple_of(me.h * ROWS, ROWS), ROWS)
    hidden_masks(segment[own_rows, :], kinds[own_rows, :], mask)
    qkv_a.relay(1)
    small.third()
    qkv_a.relay(2)
    qkv_a.relay(3)
    qkv_b.first()
    down_b.first()
    out_g.first()
    up_a.first()
    qkv_a.own_across()
    small.fourth(gb, upb)
    load_tok.wait()

    def norm_one(i, carry):
        r = block(i, 256)
        xhat, _ = normalized(tok[r, :].astype(f32))
        normed[r, :] = (xhat * gb[0:1, :] + gb[2:3, :]).astype(bf16)
        return carry

    lax.fori_loop(0, T // 256, norm_one, 0)
    for n in range(2):
        qkv_a.other_across(n)
    for k in (1, 2, 3):
        qkv_b.relay(k)
    qkv_a.other_across(2)
    qkv_b.own_across()
    up_b.first()
    down_a.first()
    qkv_a.fifth()

    def at_step(i, steps):
        for n, actions in steps.items():

            @pl.when(i == n)
            def _():
                for action in actions:
                    action()

    blocks = T // 512

    def project(i):
        c, r = i // blocks, block(lax.rem(i, blocks), 512)
        x = normed[r, :]
        values = []
        for s in range(3):
            value = dot(x, w_qkv[c, s].reshape(D, 256))
            if s != 1:
                row = 3 + s // 2
                value = value + jnp.concatenate(
                    [gb[row : row + 1, columns(c, LANES)], gb[row : row + 1, columns(2 + c, LANES)]], axis=1
                )
            value = value.astype(bf16)
            values.append(value * jnp.asarray(0.125, bf16) if s == 0 else value)
        return values

    def keep(i, projected):
        c, r = i // blocks, block(lax.rem(i, blocks), 512)
        for n in range(2):
            for s, value in enumerate(projected):
                packed[s, 2 * n + c, r, :] = value[:, LANES * n : LANES * n + LANES]

    start = me.z * 0
    keep(start, project(start))

    def attend(i, carry):
        c, b = i // blocks, lax.rem(i, blocks)
        items = [(4 * b + u, 2 * n + c) for u in range(4) for n in range(2)]
        scores = [
            dot(two_heads(packed[1, p, block(r, SEQ), :]), packed[0, p, block(r, SEQ), :], NT) for r, p in items
        ]
        values = [two_heads(packed[2, p, block(r, SEQ), :]) for r, p in items]
        following = jnp.minimum(i + 1, 2 * blocks - 1)
        projected = project(following)
        weights = []
        for (r, p), pair in zip(items, scores):
            heads = []
            for h in range(2):
                t = pair[SEQ * h : SEQ * h + SEQ] + mask[r].astype(f32)
                e = jnp.exp(t - jnp.max(t, axis=0, keepdims=True))
                a = (e * (1.0 / jnp.sum(e, axis=0, keepdims=True))).astype(bf16)
                att[r, 2 * p + h] = a
                heads.append(a)
            weights.append(jnp.concatenate(heads, axis=0))
        for (r, p), pair, value in zip(items, weights, values):
            mix[p, block(r, SEQ), :] = dot(pair, value, TN).astype(bf16)
        keep(following, projected)
        at_step(
            i,
            {
                0: [lambda: qkv_b.other_across(0), lambda: qkv_b.other_across(1), out_g.second, up_a.second],
                1: [lambda: qkv_b.other_across(2)],
                2: [qkv_b.fifth, up_b.second, down_b.second],
                3: [out_g.third],
                5: [up_a.third],
                6: [out_g.fourth],
                7: [up_b.third, down_a.second],
            },
        )
        return carry

    lax.fori_loop(0, 2 * blocks, attend, 0)
    out_g.fifth()

    def middle_of(r):
        return tok[r, :].astype(f32) + dot(tiles(mix, r), w_out[...].reshape(D, D), NT) + gb[5:6, :]

    def norm_two(i, carry):
        r = block(i, 512)
        middle = middle_of(r)
        xhat, _ = normalized(middle)
        tok[r, :] = (xhat * gb[1:2, :] + gb[6:7, :]).astype(bf16)
        middle = middle.astype(bf16)
        for p in range(4):
            gmix[p, r, :] = middle[:, LANES * p : LANES * p + LANES]
        at_step(i, {1: [up_a.fourth]})
        return carry

    lax.fori_loop(0, T // 512, norm_two, 0)
    up_b.fourth()
    up_a.fifth()

    half_count = count // 2

    def up_columns(j):
        return w_up[:, :, :, :, 512 * j : 512 * j + 512].reshape(D, 512)

    def hidden_block(columns_in, steps):
        def body(i, carry):
            r = block(i, BM)
            two = tok[r, :]
            for j in columns_in:
                cols = slice(512 * j, 512 * j + 512)
                hidden, slope = gelu_and_slope(dot(two, up_columns(j)) + upb[:, cols])
                hid[r, cols] = hidden.astype(bf16)
                gpre[r, cols] = slope.astype(bf16)
            at_step(i, steps)
            return carry

        return body

    lax.fori_loop(0, half_count, hidden_block((0, 1), {3: [down_a.third]}), 0)
    up_b.fifth()
    lax.fori_loop(0, half_count, hidden_block((2, 3), {3: [down_a.fourth]}), 0)
    down_b.third()
    load_cot.wait()
    down_a.fifth()
    down_b.fifth()
    acc[...] = jnp.zeros_like(acc)
    acc_up[...] = jnp.zeros_like(acc_up)
    acc_q[...] = jnp.zeros_like(acc_q)

    def branch_back(r, e, c):
        xhat, rstd = normalized(tiles(gmix, r).astype(f32))
        cot_f32 = c.astype(f32)
        branch = (cot_f32 + norm_back(e, xhat, rstd, gb[1:2, :])).astype(bf16)
        gbr[r, :] = branch
        grad_mix = dot(branch, w_out[...].reshape(D, D)).astype(bf16)
        for p in range(4):
            gmix[p, r, :] = grad_mix[:, LANES * p : LANES * p + LANES]
        acc[1] += column_sums(e * xhat)
        acc[6] += column_sums(e)
        acc[5] += column_sums(branch.astype(f32))
        acc[7] += column_sums(cot_f32)

    def hidden_back(i, carry):
        ra, rb = block(i, BM), block(i + half_count, BM)
        ca, cb, two = cot[ra, :], cot[rb, :], tok[rb, :]
        ea = eb = 0.0
        for j in range(4):
            cols = slice(512 * j, 512 * j + 512)
            w_up_j, w_down_j = up_columns(j), w_down[j].reshape(512, D)
            hidden, slope = gelu_and_slope(dot(two, w_up_j) + upb[:, cols])
            hid[rb, cols] = hidden.astype(bf16)
            pre_a = dot(ca, w_down_j, NT) * gpre[ra, cols].astype(f32)
            pre_b = dot(cb, w_down_j, NT) * slope
            acc_up[:, cols] += column_sums(pre_a) + column_sums(pre_b)
            pre_a, pre_b = pre_a.astype(bf16), pre_b.astype(bf16)
            gpre[ra, cols] = pre_a
            gpre[rb, cols] = pre_b
            ea = ea + dot(pre_a, w_up_j, NT)
            eb = eb + dot(pre_b, w_up_j, NT)
        branch_back(ra, ea, ca)
        branch_back(rb, eb, cb)
        return carry

    lax.fori_loop(0, half_count, hidden_back, 0)

    units = [
        Scatter(me, *refs, s_send.at[i], s_recv.at[i])
        for i, refs in enumerate(
            (
                (p_down0, core0, cross0, sets0, line0),
                (p_down1, core1, cross1, sets1, line1),
                (p_up0, core2, cross2, sets2, line2),
                (p_up1, core3, cross3, sets3, line3),
                (p_out, core4, cross4, sets4, line4),
                *((p_qkv.at[n], core5.at[n], cross5.at[n], sets5.at[n], line5.at[n]) for n in range(3)),
            )
        )
    ]
    d0, d1, u0, u1, out_u, *qkv_u = units

    def grad_down_chunk(z, carry):
        o = dot(cot[...], hid[:, block(z, 512)], TN).astype(bf16).T
        for half, part in enumerate((p_down0, p_down1)):
            for p in range(GRID_P):
                for h in range(2):
                    for j in range(2):
                        part[h, z, p, 64 * j : 64 * j + 64] = o[
                            64 * (2 * p + h) : 64 * (2 * p + h) + 64,
                            256 * half + LANES * j : 256 * half + LANES * j + LANES,
                        ]
        return carry

    def grad_up_chunk(half, part):
        def body(c, carry):
            o = dot(tok[...], gpre[:, block(2 * half + c, 512)], TN).astype(bf16)
            for z in range(GRID_Z):
                for p in range(GRID_P):
                    for h in range(2):
                        d = (z * 4 + p) * 2 + h
                        for j in range(4):
                            part[h, z, p, pl.ds(pl.multiple_of(64 * c + 16 * j, 16), 16)] = o[
                                16 * d : 16 * d + 16, LANES * j : LANES * j + LANES
                            ]
            return carry

        return body

    o = dot(gbr[...], jnp.concatenate([mix[p] for p in range(4)], axis=1), TN).astype(bf16)
    for z in range(GRID_Z):
        for p in range(GRID_P):
            d = z * 4 + p
            for h in range(2):
                for j in range(2):
                    p_out[h, z, p, 32 * j : 32 * j + 32] = o[
                        32 * d : 32 * d + 32, 256 * h + LANES * j : 256 * h + LANES * j + LANES
                    ]
    out_u.first()
    lax.fori_loop(0, 4, grad_down_chunk, 0)
    out_u.second()
    d0.first()
    d1.first()
    lax.fori_loop(0, 2, grad_up_chunk(0, p_up0), 0)
    d0.second()
    u0.first()
    d1.second()
    lax.fori_loop(0, 2, grad_up_chunk(1, p_up1), 0)
    u1.first()
    out_u.third()
    load_tok = pltpu.make_async_copy(tokens_hbm, tok, io_sem.at[0])
    load_tok.start()
    u0.second()
    d0.third()

    u1.second()
    d1.third()

    def attend_back(half, steps):
        def body(i, carry):
            row = lax.broadcasted_iota(jnp.int32, (2 * SEQ, LANES), 0) // SEQ
            lane = lax.broadcasted_iota(jnp.int32, (2 * SEQ, LANES), 1) // 64
            minus = jnp.where(row == lane, -1.0, 0.0).astype(bf16)
            items = [(4 * i + u, 2 * half + pp) for u in range(4) for pp in range(2)]
            grads, slopes = [], []
            for r, p in items:
                rows = block(r, SEQ)
                grad = gmix[p, rows, :]
                product = (grad.astype(f32) * mix[p, rows, :].astype(f32)).astype(bf16)
                values = jnp.concatenate([two_heads(packed[2, p, rows, :]), minus], axis=1)
                grads.append(dot(values, jnp.concatenate([grad, product], axis=1), NT))
            for (r, p), pair in zip(items, grads):
                slopes.append(
                    [
                        (att[r, 2 * p + h].astype(f32) * pair[SEQ * h : SEQ * h + SEQ]).astype(bf16)
                        for h in range(2)
                    ]
                )
            results, sums = [], [0.0] * 4
            for n, ((r, p), pair) in enumerate(zip(items, slopes)):
                rows = block(r, SEQ)
                queries, keys = two_heads(packed[0, p, rows, :]), two_heads(packed[1, p, rows, :])
                g_q = dot(jnp.concatenate(pair, axis=0), keys, TN) * 0.125
                g_k = dot(jnp.concatenate(pair, axis=1), queries)
                weights = jnp.concatenate([att[r, 2 * p], att[r, 2 * p + 1]], axis=1)
                g_v = dot(weights, two_heads(gmix[p, rows, :]))
                sums[n % 2] = sums[n % 2] + column_sums(g_q)
                sums[2 + n % 2] = sums[2 + n % 2] + column_sums(g_v)
                results.append((g_q.astype(bf16), g_k.astype(bf16), g_v.astype(bf16)))
            for (r, p), result in zip(items, results):
                for n in range(3):
                    packed[n, p, block(r, SEQ), :] = result[n]
            for pp in range(2):
                acc_q[0, 2 * half + pp] += sums[pp]
                acc_q[1, 2 * half + pp] += sums[2 + pp]
            at_step(i, steps)
            return carry

        return body

    def grad_qkv_half(half, steps):
        def body(s, carry):
            wide = jnp.concatenate([packed[s, 2 * half], packed[s, 2 * half + 1]], axis=1)
            o = dot(normed[...], wide, TN).astype(bf16)
            for z in range(GRID_Z):
                for p in range(GRID_P):
                    d = z * 4 + p
                    for j in range(2):
                        p_qkv[s, half, z, p, 32 * j : 32 * j + 32] = o[
                            32 * d : 32 * d + 32, LANES * j : LANES * j + LANES
                        ]
            at_step(s, steps)
            return carry

        return body

    lax.fori_loop(0, ROWS // 4, attend_back(me.sib, {1: [out_u.fourth], 2: [u0.third]}), 0)
    lax.fori_loop(0, 3, grad_qkv_half(me.sib, {n: [qkv_u[n].first] for n in range(3)}), 0)
    d0.fourth()
    u1.third()
    lax.fori_loop(0, ROWS // 4, attend_back(me.h, {3: [d1.fourth]}), 0)
    lax.fori_loop(0, 3, grad_qkv_half(me.h, {n: [qkv_u[n].second] for n in range(3)}), 0)
    u0.fourth()
    load_tok.wait()

    def grad_copy(i):
        return pltpu.make_async_copy(
            grad_stage.at[parity(i)], grad_hbm.at[block(i, BACK), :], out_sem.at[parity(i)]
        )

    def norm_one_back(i, carry):
        r = block(i, BACK)

        @pl.when(i >= 2)
        def _():
            grad_copy(i - 2).wait()

        e = 0.0
        for c in range(2):
            for s in range(3):
                pair = jnp.concatenate([packed[s, c, r, :], packed[s, 2 + c, r, :]], axis=1)
                e = e + dot(pair, w_qkv[c, s].reshape(D, 256), NT)
        xhat, rstd = normalized(tok[r, :].astype(f32))
        grad = gbr[r, :].astype(f32) + norm_back(e, xhat, rstd, gb[0:1, :])
        grad_stage[parity(i)] = grad.astype(bf16)
        grad_copy(i).start()
        acc[0] += column_sums(e * xhat)
        acc[2] += column_sums(e)
        at_step(i, {0: [qkv_u[0].third], 1: [u1.fourth, qkv_u[1].third], 2: [qkv_u[2].third], 3: [qkv_u[0].fourth]})
        return carry

    lax.fori_loop(0, back_count, norm_one_back, 0)
    for p in range(4):
        acc[3, :, LANES * p : LANES * p + LANES] = acc_q[0, p]
        acc[4, :, LANES * p : LANES * p + LANES] = acc_q[1, p]
    for z in range(GRID_Z):
        rows = [jnp.sum(acc[n, :, LANES * z : LANES * z + LANES], axis=0, keepdims=True) for n in range(8)]
        rows += [
            jnp.sum(acc_up[:, 512 * z + LANES * p : 512 * z + LANES * p + LANES], axis=0, keepdims=True)
            for p in range(GRID_P)
        ]
        rows += [jnp.zeros((4, LANES), f32)]
        p_small[z] = jnp.concatenate(rows, axis=0)
    small_sum = SmallScatter(me, p_small, small_line, small_sets, s_send.at[8], s_recv.at[8])
    small_sum.first()

    def out_copies(i):
        r = block(i, 512)
        return [
            pltpu.make_async_copy(
                gmix.at[p, r], output_hbm.at[r, pl.ds(LANES * p, LANES)], out_sem.at[2]
            )
            for p in range(4)
        ]

    def output_block(i, carry):
        r = block(i, 512)
        total = middle_of(r) + dot(hid[r, :], w_down[...].reshape(2048, D)) + gb[7:8, :]
        total = total.astype(bf16)
        for p in range(4):
            gmix[p, r, :] = total[:, LANES * p : LANES * p + LANES]
        for copy in out_copies(i):
            copy.start()
        at_step(i, {0: [qkv_u[1].fourth], 1: [small_sum.second, qkv_u[2].fourth]})
        return carry

    lax.fori_loop(0, T // 512, output_block, 0)
    for unit, rows in ((out_u, OUT_ROWS), (d0, DOWN_ROWS), (d1, DOWN_ROWS + 128), (u0, UP_ROWS), (u1, UP_ROWS + 128)):
        total = unit.fifth()
        sums[rows : rows + total.shape[0]] = total
    small_sum.third(sums)
    for n in range(3):
        sums[QKV_ROWS + 64 * n : QKV_ROWS + 64 * n + 64] = qkv_u[n].fifth()
    for i in range(T // 512):
        for copy in out_copies(i):
            copy.wait()
    for i in (back_count - 2, back_count - 1):
        grad_copy(i).wait()
    for item in gathers + units + [small, small_sum]:
        item.close()


def finish_kernel(output, grad, sums_hbm, *refs):
    targets, stages, sums, grad_in, sems = refs[:9], refs[9:18], refs[18], refs[19], refs[20]
    staged = (stages[0], grad_in)
    loads, stores = [], []
    load_sums = pltpu.make_async_copy(sums_hbm, sums, sems.at[0, 0, 4])
    load_sums.start()
    for n in range(4):
        for a, source in ((1, grad), (0, output)):
            size = source.shape[0] // 4
            rows = pl.ds(n * size, size)
            loads.append(pltpu.make_async_copy(source.at[rows], staged[a].at[rows], sems.at[0, a, n]))
            stores.append(pltpu.make_async_copy(stages[a].at[rows], targets[a].at[rows], sems.at[1, a, n]))
    for load in loads:
        load.start()
    g_qkv, g_out, g_up, g_down, g_gains, g_biases, g_up_bias = stages[2:]
    load_sums.wait()

    def tile(start, rows, j):
        return sums[start + rows * j : start + rows * (j + 1)]

    for j in range(4):
        g_down[:, LANES * j : LANES * j + LANES] = tile(DOWN_ROWS, 64, j)
    for j in range(16):
        g_up[:, LANES * j : LANES * j + LANES] = tile(UP_ROWS, 16, j)
    for j in range(2):
        g_out[:, LANES * j : LANES * j + LANES] = tile(OUT_ROWS, 32, j)
        for s in range(3):
            g_qkv[s, :, LANES * j : LANES * j + LANES] = tile(QKV_ROWS + 64 * s, 32, j)
    g_gains[...] = sums[SMALL_ROWS : SMALL_ROWS + 2, 0:16]
    g_biases[...] = sums[SMALL_ROWS + 2 : SMALL_ROWS + 8, 0:16]
    g_up_bias[...] = sums[SMALL_ROWS + 8 : SMALL_ROWS + 9, 0:64]
    for n in range(2, 9):
        stores.append(pltpu.make_async_copy(stages[n], targets[n], sems.at[2, n // 5, n % 5]))
        stores[-1].start()
    for i, (load, store) in enumerate(zip(loads, stores)):
        load.wait()
        if i % 2 == 0:
            rows = slice(i // 2 * size, (i // 2 + 1) * size)
            stages[1][rows] = grad_in[rows].astype(f32)
        store.start()
    for store in stores:
        store.wait()


def finish(output, grad, sums):
    shape = jax.ShapeDtypeStruct
    outs = (
        shape(output.shape, bf16),
        shape(grad.shape, f32),
        shape((3, 32, 256), f32),
        shape((32, 256), f32),
        shape((16, 2048), f32),
        shape((64, 512), f32),
        shape((2, 16), f32),
        shape((6, 16), f32),
        shape((1, 64), f32),
    )
    return pl.pallas_call(
        finish_kernel,
        out_shape=outs,
        in_specs=[ANY] * 3,
        out_specs=[ANY] * 9,
        scratch_shapes=[pltpu.VMEM(o.shape, o.dtype) for o in outs]
        + [pltpu.VMEM(sums.shape, f32), pltpu.VMEM(grad.shape, bf16), pltpu.SemaphoreType.DMA((3, 2, 5))],
        compiler_params=pltpu.CompilerParams(vmem_limit_bytes=VMEM_LIMIT),
        name="finish",
    )(output, grad, sums)


def layer(tokens, cotangent, qkv, out, up, down, gains, biases, up_bias, segment, kinds):
    shape = jax.ShapeDtypeStruct
    T = tokens.shape[0]
    rows = T // SEQ
    outs = (shape((T, D), bf16), shape((T, D), bf16), shape((ALL_ROWS, LANES), f32))
    sizes = [128, 128, 128, 128, 64]
    V, S = pltpu.VMEM, pltpu.SemaphoreType.DMA
    scratch = [
        V((T, D), bf16), V((T, D), bf16),
        V((2, 3, 4, 4, 32, 256), bf16), V((4, 4, 32, 512), bf16),
        V((4, 4, 2, 16, 2048), bf16), V((4, 4, 2, 64, 512), bf16),
        V((8, 512), f32), V((1, 2048), f32), V((rows, SEQ, SEQ), bf16),
        V((T, D), bf16), V((3, 4, T, LANES), bf16), V((rows, 8, SEQ, SEQ), bf16),
        V((4, T, LANES), bf16), V((T, 2048), bf16), V((T, 2048), bf16),
        V((T, D), bf16), V((4, T, LANES), bf16), V((8, 8, 512), f32), V((8, 2048), f32),
        V((2, 4, 8, LANES), f32),
        V((2, 512, D), bf16),
    ]
    scratch += [V((2, 4, 4, r, LANES), bf16) for r in sizes] + [V((3, 2, 4, 4, 64, LANES), bf16)] + [V((4, 16, LANES), f32)]
    scratch += [V((4, 4, r, LANES), bf16) for r in sizes] + [V((3, 4, 4, 64, LANES), bf16)]
    scratch += [V((2, 2, r, LANES), bf16) for r in sizes] + [V((3, 2, 2, 64, LANES), bf16)]
    scratch += [V((2, 4, r, LANES), bf16) for r in sizes] + [V((3, 2, 4, 64, LANES), bf16)]
    scratch += [V((3, r, LANES), bf16) for r in sizes] + [V((3, 3, 64, LANES), bf16)]
    scratch += [V((4, 2, 16, LANES), bf16), V((4, 16, LANES), bf16), V((3, 16, LANES), f32), V((8, 16, LANES), f32)]
    scratch += [S((8, 19)), S((8, 19)), S((7,)), S((9, 10)), S((9, 10)), S((2,)), S((3,))]
    return pl.pallas_call(
        layer_kernel,
        out_shape=outs,
        in_specs=[ANY] * 6 + [VM] * 5,
        out_specs=[ANY] * 2 + [VM],
        scratch_shapes=scratch,
        compiler_params=pltpu.CompilerParams(
            collective_id=0, has_side_effects=True, vmem_limit_bytes=VMEM_LIMIT
        ),
        name="layer",
    )(tokens, cotangent, qkv, out, up, down, gains, biases, up_bias, segment, kinds)


def widened(x, axes, dim):
    return lax.all_gather(x, axes, axis=dim, tiled=True)


def on_device(rep):
    def run(
        tokens, qkv, out, up, down, gains, biases, up_bias, segment, kinds, cotangent
    ):
        up_bias = up_bias.reshape(1, -1)
        head = lax.axis_index("head")
        if rep > 1:
            both = ("rep", "head")
            qkv, out = widened(qkv, "rep", 1), widened(out, "rep", 0)
            up = lax.dynamic_slice_in_dim(widened(up, both, 0), head * 16, 16, 0)
            down = lax.dynamic_slice_in_dim(widened(down, both, 0), head * 64, 64, 0)
            gains = lax.dynamic_slice_in_dim(widened(gains, both, 1), head * 16, 16, 1)
            biases = lax.dynamic_slice_in_dim(widened(biases, both, 1), head * 16, 16, 1)
            up_bias = lax.dynamic_slice_in_dim(widened(up_bias, both, 1), head * 64, 64, 1)
        output, grad, *grads = finish(
            *layer(tokens, cotangent, qkv, out, up, down, gains, biases, up_bias, segment, kinds)
        )
        if rep > 1:
            place = lax.axis_index("rep") * 2 + head

            def own(x, dim):
                x = lax.all_gather(lax.psum(x, "rep"), "head", axis=dim, tiled=True)
                size = x.shape[dim] // (2 * rep)
                return lax.dynamic_slice_in_dim(x, place * size, size, dim)

            for i, dim in ((0, 1), (1, 0)):
                grads[i] = lax.psum_scatter(grads[i], "rep", scatter_dimension=dim, tiled=True)
            for i, dim in ((2, 0), (3, 0), (4, 1), (5, 1), (6, 1)):
                grads[i] = own(grads[i], dim)
        grads[6] = grads[6].reshape(-1)
        return (output, grad, *grads)

    return run


def solution(mesh):
    rep = mesh.shape["dp"] // (GRID_Z * GRID_P)
    wide = Mesh(mesh.devices.reshape(GRID_Z * GRID_P, rep, 2), ("dp", "rep", "head"))
    dp, every = ("dp", "rep"), ("dp", "rep", "head")
    in_specs = (
        P(every, None),
        P(None, dp, "head"),
        P(dp, "head"),
        P(every, None),
        P(every, None),
        P(None, every),
        P(None, every),
        P(every),
        P(dp, None),
        P(dp, None),
        P(every, None),
    )
    out_specs = (
        P(every, None),
        P(every, None),
        P(None, dp, "head"),
        P(dp, "head"),
        P(every, None),
        P(every, None),
        P(None, every),
        P(None, every),
        P(every),
    )
    return jax.shard_map(
        on_device(rep), mesh=wide, in_specs=in_specs, out_specs=out_specs, check_vma=False
    )
```
